128 devices in a mesh: section: 2 (over x_lo), shard: 16 (over z, y), replica: 4 (over x_hi, core).
Axes of the slice: x: 4 (x_hi: 2, x_lo: 2; x = x_hi * 2 + x_lo), y: 4, z: 4, core: 2. Of those that a mesh axis runs over, the one named last changes fastest.
Arguments:
- inputs: bfloat16 [2, 4, 2048, 576], P(None, 'replica', 'shard'), may hold values from -6 to 6
- out_grad: bfloat16 [2, 4, 2048, 576], P(None, 'replica', 'shard'), may hold values from -6 to 6
- w_query: bfloat16 [2, 576, 576], P('section', 'shard'), may hold values from -0.25 to 0.25
- w_key: bfloat16 [2, 576, 192], P('section', 'shard'), may hold values from -0.25 to 0.25
- w_value: bfloat16 [2, 576, 192], P('section', 'shard'), may hold values from -0.25 to 0.25
- w_out: bfloat16 [2, 576, 576], P('section', 'shard'), may hold values from -3 to 3
- w_gate: bfloat16 [2, 576, 1536], P('section', 'shard'), may hold values from -0.25 to 0.25
- w_up: bfloat16 [2, 576, 1536], P('section', 'shard'), may hold values from -0.25 to 0.25
- w_down: bfloat16 [2, 1536, 576], P('section', 'shard'), may hold values from -0.15625 to 0.15625
- gain_attn: bfloat16 [2, 576], P('section', 'shard'), may hold values from 0.099609375 to 1.8984375
- gain_ffn: bfloat16 [2, 576], P('section', 'shard'), may hold values from 0.099609375 to 1.8984375
Outputs:
- section_out: bfloat16 [2, 2, 4, 2048, 576], P('section', None, 'replica', 'shard')
- section_in_grad: float32 [2, 2, 4, 2048, 576], P('section', None, 'replica', 'shard')
- grad_query: float32 [2, 576, 576], P('section', 'shard')
- grad_key: float32 [2, 576, 192], P('section', 'shard')
- grad_value: float32 [2, 576, 192], P('section', 'shard')
- grad_out: float32 [2, 576, 576], P('section', 'shard')
- grad_gate: float32 [2, 576, 1536], P('section', 'shard')
- grad_up: float32 [2, 576, 1536], P('section', 'shard')
- grad_down: float32 [2, 1536, 576], P('section', 'shard')
- grad_gain_attn: float32 [2, 576], P('section', 'shard')
- grad_gain_ffn: float32 [2, 576], P('section', 'shard')
The draws below stay inside these ranges and needn't reach their ends.
All inputs are finite; a program needn't handle non-finite values.
Results may differ from the reference program's by a relative error of at most 0.028.
Values may be sent and summed in bfloat16 or wider, within the bound.
A program may use at most 192 MiB of HBM per device.

```python
import jax
import jax.numpy as jnp
from jax import lax

D = 576
FF = 1536
HEADS = 9
KV_HEADS = 3
HEAD_DIM = 64
SEQ_LEN = 2048
MICRO = 2
BATCH = 4
QW = 576
KW = 192
N_SECTION = 2


def block_levels(key, shape, split, low, largest):
    factor_of, own = 1.0, jax.random.fold_in(key, 6)
    for axis_at, parts in split:
        heights = jnp.exp(jax.random.uniform(jax.random.fold_in(own, axis_at), (parts,), jnp.float32, low / len(split), largest / len(split)))
        factor_of = factor_of * jnp.repeat(heights, shape[axis_at] // parts).reshape([-1 if axis == axis_at else 1 for axis in range(len(shape))])
    return factor_of


def scatter_about(stream_key, dims, spread, reach, shards=(), kind=jnp.bfloat16):
    values = jax.random.normal(stream_key, dims, jnp.float32) * spread
    if len(shards) > 0:
        values = block_levels(stream_key, dims, shards, -0.22, 0.18) * values
    return jnp.clip(values, min=-reach, max=reach).astype(kind)


def setup_inputs(seed: int = 0) -> dict:
    key_list = jax.random.split(jax.random.key(seed), 12)
    inputs = scatter_about(key_list[0], (MICRO, BATCH, SEQ_LEN, D), 1.0, 6.0, ((1, 4), (2, 16)))
    out_grad = scatter_about(key_list[1], (MICRO, BATCH, SEQ_LEN, D), 1.0, 6.0, ((1, 4), (2, 16)))
    w_query = scatter_about(key_list[2], (N_SECTION, D, QW), D ** -0.5, 0.25, ((0, 2), (1, 16)))
    w_key = scatter_about(key_list[3], (N_SECTION, D, KW), D ** -0.5, 0.25, ((0, 2), (1, 16)))
    w_value = scatter_about(key_list[4], (N_SECTION, D, KW), D ** -0.5, 0.25, ((0, 2), (1, 16)))
    w_out = scatter_about(key_list[5], (N_SECTION, QW, D), 4 ** -0.5, 3.0, ((0, 2), (1, 16)))
    w_gate = scatter_about(key_list[6], (N_SECTION, D, FF), D ** -0.5, 0.25, ((0, 2), (1, 16)))
    w_up = scatter_about(key_list[7], (N_SECTION, D, FF), D ** -0.5, 0.25, ((0, 2), (1, 16)))
    w_down = scatter_about(key_list[8], (N_SECTION, FF, D), FF ** -0.5, 0.15625, ((0, 2), (1, 16)))
    gain_attn = jnp.clip(1.0 + 0.18 * jax.random.normal(key_list[9], (N_SECTION, D), jnp.float32), 0.099609375, 1.8984375).astype(jnp.bfloat16)
    gain_ffn = jnp.clip(1.0 + 0.18 * jax.random.normal(key_list[10], (N_SECTION, D), jnp.float32), 0.099609375, 1.8984375).astype(jnp.bfloat16)
    return {"inputs": inputs, "out_grad": out_grad, "w_query": w_query, "w_key": w_key, "w_value": w_value, "w_out": w_out, "w_gate": w_gate, "w_up": w_up, "w_down": w_down, "gain_attn": gain_attn, "gain_ffn": gain_ffn}


@jax.custom_vjp
def low(v):
    return lax.optimization_barrier(v.astype(jnp.bfloat16)).astype(jnp.float32)

@jax.custom_vjp
def low_back(v):
    return v

def low_keep(v):
    return (low(v), None)

def low_pass(kept, grad):
    return (grad,)

def back_keep(v):
    return (v, None)

def back_low(kept, grad):
    return (low(grad),)
low.defvjp(low_keep, low_pass)
low_back.defvjp(back_keep, back_low)
epsilon = 1e-05
rope_base = 100000.0
score_scale = 0.125
highest = lax.Precision.HIGHEST

def rope_tables(positions, head_size):
    half_size = head_size // 2
    inverse = rope_base ** (-(jnp.arange(half_size, dtype=jnp.float32) * 2.0 / head_size))
    angles = positions.astype(jnp.float32)[:, None] * inverse[None, :]
    angles = jnp.concatenate([angles, angles], axis=1)
    return (jnp.cos(angles), jnp.sin(angles))

def rotate(values, cosine, sine):
    half_size = values.shape[-1] // 2
    turned = jnp.concatenate([-values[..., half_size:], values[..., :half_size]], axis=-1)
    return values * cosine[:, None, :] + turned * sine[:, None, :]

def matmul(left, right):
    return jnp.dot(left, right, precision=highest, preferred_element_type=jnp.float32)

def rms_norm(values, gain):
    factor = lax.rsqrt(lax.optimization_barrier(jnp.mean(values * values, axis=-1, keepdims=True)) + epsilon)
    return values * factor * gain

def layer(hidden_in, weights):
    w_query, w_key, w_value, w_out, w_gate, w_up, w_down, gain_attn, gain_ffn = weights
    length = hidden_in.shape[0]
    group_size = HEADS // KV_HEADS
    cosine, sine = rope_tables(jnp.arange(length, dtype=jnp.int32), HEAD_DIM)
    normed = low(rms_norm(hidden_in, gain_attn))
    query_pre = low_back(matmul(normed, w_query)).reshape(length, HEADS, HEAD_DIM)
    key_pre = low_back(matmul(normed, w_key)).reshape(length, KV_HEADS, HEAD_DIM)
    value_heads = low_back(low(matmul(normed, w_value))).reshape(length, KV_HEADS, HEAD_DIM)
    queries = low(rotate(query_pre, cosine, sine)).reshape(length, KV_HEADS, group_size, HEAD_DIM)
    key_heads = low(rotate(key_pre, cosine, sine))
    scores = jnp.einsum('qhgd,khd->hgqk', queries, key_heads, precision=highest) * score_scale
    scores = low_back(scores)
    positions = jnp.arange(length, dtype=jnp.int32)
    causal = positions[None, :] <= positions[:, None]
    scores = jnp.where(causal, scores, -1e+30)
    probs = jax.nn.softmax(scores, axis=-1)
    mixed = jnp.einsum('hgqk,khd->qhgd', low(probs), value_heads, precision=highest)
    mixed = low_back(low(mixed.reshape(length, HEADS * HEAD_DIM)))
    middle = hidden_in + low_back(matmul(mixed, w_out))
    ffn_in = low(rms_norm(middle, gain_ffn))
    gate_val = low_back(matmul(ffn_in, w_gate))
    up_val = low_back(matmul(ffn_in, w_up))
    inner = low_back(low(jax.nn.silu(gate_val) * up_val))
    return middle + low_back(matmul(inner, w_down))

def two_layers(seq_in, bump_zero, first_layer, second_layer):
    between = layer(seq_in, first_layer)
    passed = low_back(low(between)) + bump_zero
    return (layer(passed, second_layer), between)

def reference(inputs, out_grad, w_query, w_key, w_value, w_out, w_gate, w_up, w_down, gain_attn, gain_ffn):
    stacked = tuple((weight_arr.astype(jnp.float32) for weight_arr in (w_query, w_key, w_value, w_out, w_gate, w_up, w_down, gain_attn, gain_ffn)))
    first_layer = tuple((weight_arr[0] for weight_arr in stacked))
    second_layer = tuple((weight_arr[1] for weight_arr in stacked))
    count_seqs = MICRO * BATCH
    flat_in = inputs.reshape(count_seqs, SEQ_LEN, D).astype(jnp.float32)
    flat_grad = out_grad.reshape(count_seqs, SEQ_LEN, D).astype(jnp.float32)

    def one_sequence(totals, seq_pair):
        seq_in, seq_grad = seq_pair
        bump_zero = jnp.zeros_like(seq_in)
        final_out, pullback, between = jax.vjp(two_layers, seq_in, bump_zero, first_layer, second_layer, has_aux=True)
        grad_in, grad_mid, grad_first, grad_second = pullback(seq_grad)
        totals = jax.tree.map(lambda running, addend: running + addend, totals, (grad_first, grad_second))
        outs_pair = jnp.stack([between.astype(jnp.bfloat16), final_out.astype(jnp.bfloat16)])
        grads_pair = jnp.stack([grad_in, grad_mid])
        return (totals, (outs_pair, grads_pair))
    initial = jax.tree.map(jnp.zeros_like, (first_layer, second_layer))
    totals, (outs_all, grads_all) = lax.scan(one_sequence, initial, (flat_in, flat_grad))
    section_out = jnp.moveaxis(outs_all, 1, 0).reshape(N_SECTION, MICRO, BATCH, SEQ_LEN, D)
    section_in_grad = jnp.moveaxis(grads_all, 1, 0).reshape(N_SECTION, MICRO, BATCH, SEQ_LEN, D)
    grads_first, grads_second = totals
    merged = tuple((jnp.stack([grad_one, grad_two]) for grad_one, grad_two in zip(grads_first, grads_second)))
    g_query, g_key, g_value, g_out, g_gate, g_up, g_down, g_attn, g_ffn = merged
    return (section_out, section_in_grad, g_query, g_key, g_value, g_out, g_gate, g_up, g_down, g_attn, g_ffn)
```

```python
import functools

import jax
import jax.numpy as jnp
from jax import lax
from jax.experimental import pallas as pl
from jax.experimental.pallas import tpu as pltpu
from jax.sharding import PartitionSpec as P

HEADS = 9
KV_HEADS = 3
HEAD_DIM = 64
D = 576
FF = 1536
TOK = 128
SHARDS = 16
SIDE = 4
ROWS = 36
PAD = 48
BAND = SIDE * ROWS
FROWS = 96
FBAND = SIDE * FROWS
GU = 2 * FF
QO = 1664
QKV = 1024
OAT = 1024
CHUNK = 512
GROUP = 3 * TOK

bf16 = jnp.bfloat16
f32 = jnp.float32
MESH = pl.DeviceIdType.MESH
epsilon = 1e-05
rope_base = 100000.0
score_scale = 0.125


def dot(a, b):
    return lax.dot_general(a, b, (((1,), (0,)), ((), ())), preferred_element_type=f32)


def dot_nt(a, b):
    return lax.dot_general(a, b, (((1,), (1,)), ((), ())), preferred_element_type=f32)


def dot_tn(a, b):
    return lax.dot_general(a, b, (((0,), (0,)), ((), ())), preferred_element_type=f32)


def factor_of(v):
    return lax.rsqrt(jnp.mean(v * v, axis=-1, keepdims=True) + epsilon)


def norm_back(v, r, gain, up):
    scaled = gain * up
    return r * scaled - v * (r * r * r) * jnp.mean(scaled * v, axis=-1, keepdims=True)


def half_swap(u):
    width = u.shape[1]
    lane = lax.broadcasted_iota(jnp.int32, u.shape, 1)
    first = lax.rem(lane, HEAD_DIM) < HEAD_DIM // 2
    return jnp.where(first, pltpu.roll(u, width - 32, 1), pltpu.roll(u, 32, 1))


def body(
    x_ref, dy_ref, p0_ref, p1_ref, pd_ref, cos_ref, sin_ref,
    out_ref, dx_ref, gq_ref, gk_ref, gv_ref, go_ref, gg_ref, gu_ref, gd_ref, gain_ref,
    stage, w_gu, w_qo, w_d, kv, dkv_s, dkv_r, scr, mx, acc,
    xs_, a_, q8_, o_, lse_, mid_, bn_, gu_, hid_,
    dyb_, dob_, delta_, dq_, dkv_acc, acc2, gain_term,
    g_gu, g_qo, g_d, zr, zr_d, ys, ys_d, yr, yr_d, xs, xs_d, xr, xr_d, fs, fs_d, fr, fr_d,
    osend, orecv, dsend, drecv,
    ssem, rsem, credit,
):
    sec = lax.axis_index("section")
    sh = lax.axis_index("shard")
    rep = lax.axis_index("replica")
    z, y = lax.div(sh, SIDE), lax.rem(sh, SIDE)
    core = lax.rem(rep, 2)
    sib = rep + 1 - 2 * core
    far = lax.rem(rep + 2, 4)
    used = [0]

    def take(n):
        at = used[0]
        used[0] += n
        return at

    def copy(src, dst, at, **dev):
        return pltpu.make_async_remote_copy(
            src_ref=src, dst_ref=dst, send_sem=ssem.at[at], recv_sem=rsem.at[at],
            device_id=dev, device_id_type=MESH,
        )

    def arrived(dst, at):
        copy(dst, dst, at, shard=sh).wait_recv()

    def sent(src, at):
        copy(src, src, at, shard=sh).wait_send()

    def y_peer(d):
        return z * SIDE + lax.rem(y + d, SIDE)

    def z_peer(d):
        return lax.rem(z + d, SIDE) * SIDE + y

    def z_from(d):
        return lax.rem(z + SIDE - d, SIDE)

    def y_from(d):
        return lax.rem(y + SIDE - d, SIDE)

    kv[...] = jnp.zeros_like(kv)
    ys[...] = jnp.zeros_like(ys)
    barrier = pltpu.get_barrier_semaphore()

    def greet(d, c):
        pl.semaphore_signal(barrier, inc=1, device_id={"shard": lax.rem(sh + d, SHARDS)}, device_id_type=MESH)
        return c

    lax.fori_loop(1, SHARDS, greet, 0)
    pl.semaphore_signal(barrier, inc=1, device_id={"replica": sib}, device_id_type=MESH)
    pl.semaphore_signal(barrier, inc=1, device_id={"replica": far}, device_id_type=MESH)
    pl.semaphore_signal(barrier, inc=1, device_id={"section": 1 - sec}, device_id_type=MESH)
    pl.semaphore_signal(barrier, inc=1, device_id={"section": 1 - sec, "replica": far}, device_id_type=MESH)
    pl.semaphore_wait(barrier, SHARDS - 1 + 4)

    packs = ((0, p0_ref, w_gu, GU), (1, p1_ref, w_qo, QO))
    at_x, at_xd = take(1), take(1)
    at_y = [take(3) for _ in range(2)]
    at_z = [take(3) for _ in range(2)]
    at_f = [take(4) for _ in range(2)]
    at_dz = [take(3) for _ in range(2)]
    at_dy = [take(3) for _ in range(2)]
    at_df = [take(1) for _ in range(2)]

    def x_start():
        for c, p, w, width in packs:
            @pl.when(core == c)
            def _():
                copy(p, stage.at[sec, y, :, pl.ds(0, width)], at_x, section=1 - sec).start()
                stage[sec, y, :, 0:width] = p[...]

        @pl.when(core == 1)
        def _():
            copy(pd_ref, w_d.at[sec, z, y], at_xd, section=1 - sec).start()
            w_d[sec, z, y] = pd_ref[...]

    def y_start(l):
        for c, p, w, width in packs:
            @pl.when(core == c)
            def _():
                own = stage.at[l, y, :, pl.ds(0, width)]

                @pl.when(sec != l)
                def _():
                    arrived(own, at_x)

                for d in range(1, SIDE):
                    copy(own, own, at_y[l] + d - 1, shard=y_peer(d)).start()

    def dz_start(l):
        @pl.when(core == 1)
        def _():
            own = w_d.at[l, z, y]

            @pl.when(sec != l)
            def _():
                arrived(own, at_xd)

            for d in range(1, SIDE):
                copy(own, own, at_dz[l] + d - 1, shard=z_peer(d)).start()

    def z_start(l):
        for c, p, w, width in packs:
            @pl.when(core == c)
            def _():
                for d in range(1, SIDE):
                    arrived(stage.at[l, y_from(d), :, pl.ds(0, width)], at_y[l] + d - 1)
                for at in range(0, width, 128):
                    cols = pl.ds(at, 128)
                    parts = [stage[l, j, :, cols][0:ROWS].astype(f32) for j in range(SIDE)]
                    w[l, z, :, cols] = jnp.concatenate(parts, axis=0).astype(bf16)
                own = w.at[l, z]
                for d in range(1, SIDE):
                    copy(own, own, at_z[l] + d - 1, shard=z_peer(d)).start()
                copy(own, own, at_f[l], replica=sib).start()

    def dy_start(l):
        @pl.when(core == 1)
        def _():
            for d in range(1, SIDE):
                arrived(w_d.at[l, z_from(d), y], at_dz[l] + d - 1)
            own = w_d.at[l, :, y]
            for d in range(1, SIDE):
                copy(own, own, at_dy[l] + d - 1, shard=y_peer(d)).start()

    def forward_on(l):
        for c, p, w, width in packs:
            @pl.when(core == c)
            def _():
                for d in range(1, SIDE):
                    got = w.at[l, z_from(d)]
                    arrived(got, at_z[l] + d - 1)
                    copy(got, got, at_f[l] + d, replica=sib).start()

    def d_forward_on(l):
        @pl.when(core == 1)
        def _():
            for d in range(1, SIDE):
                arrived(w_d.at[l, :, y_from(d)], at_dy[l] + d - 1)
            copy(w_d.at[l], w_d.at[l], at_df[l], replica=sib).start()

    def gather_end(l):
        for c, p, w, width in packs:
            @pl.when(core != c)
            def _():
                arrived(w.at[l, z], at_f[l])
                for d in range(1, SIDE):
                    arrived(w.at[l, z_from(d)], at_f[l] + d)

        @pl.when(core == 0)
        def _():
            arrived(w_d.at[l], at_df[l])

    def gather_sent(l):
        for c, p, w, width in packs:
            @pl.when(core == c)
            def _():
                own = stage.at[l, y, :, pl.ds(0, width)]

                @pl.when(sec == l)
                def _():
                    sent(p, at_x)

                for d in range(1, SIDE):
                    sent(own, at_y[l] + d - 1)
                    sent(w.at[l, z], at_z[l] + d - 1)
                    sent(w.at[l, z], at_f[l] + d)
                sent(w.at[l, z], at_f[l])

        @pl.when(core == 1)
        def _():
            @pl.when(sec == l)
            def _():
                sent(pd_ref, at_xd)

            for d in range(1, SIDE):
                sent(w_d.at[l, z, y], at_dz[l] + d - 1)
                sent(w_d.at[l, :, y], at_dy[l] + d - 1)
            sent(w_d.at[l], at_df[l])

    at_kv = [take(SHARDS) for _ in range(2)]
    at_dkv = [take(SHARDS) for _ in range(2)]
    tokens = pl.ds(pl.multiple_of(sh * TOK, TOK), TOK)

    def kv_start(l):
        own = kv.at[l, tokens]

        def go(d, c):
            copy(own, own, at_kv[l] + d, shard=sh + d).start()
            return c

        lax.fori_loop(1, SHARDS - sh, go, 0)

    def kv_wait(l):
        def go(d, c):
            arrived(kv.at[l, pl.ds(pl.multiple_of((sh - d) * TOK, TOK), TOK)], at_kv[l] + d)
            return c

        lax.fori_loop(1, sh + 1, go, 0)

    def kv_sent(l):
        def go(d, c):
            sent(kv.at[l, tokens], at_kv[l] + d)
            return c

        lax.fori_loop(1, SHARDS - sh, go, 0)

    def dkv_start(l, j):
        src = dkv_s.at[pl.ds(pl.multiple_of(j * TOK, TOK), TOK)]
        copy(src, dkv_r.at[l, sh - j], at_dkv[l] + sh - j, shard=j).start()

    def dkv_sent(l):
        def go(d, c):
            sent(dkv_s.at[pl.ds(0, TOK)], at_dkv[l] + d)
            return c

        lax.fori_loop(1, sh + 1, go, 0)

    def gains(l):
        tile = w_qo[l, :, :, 896:1024].reshape(D, 128)
        row = lax.broadcasted_iota(jnp.int32, (8, 128), 0)
        lane = lax.broadcasted_iota(jnp.int32, (8, 128), 1)
        pick = jnp.where(lane == row + 64, 1.0, 0.0).astype(bf16)
        both = dot_nt(pick, tile)
        return both[0:1], both[1:2]

    nfull = lax.div(sh, SIDE)

    def causal():
        row = lax.broadcasted_iota(jnp.int32, (GROUP, CHUNK), 0)
        col = lax.broadcasted_iota(jnp.int32, (GROUP, CHUNK), 1)
        return col <= lax.rem(sh, SIDE) * TOK + lax.rem(row, TOK)

    def keys_at(c):
        return pl.ds(pl.multiple_of(c * CHUNK, CHUNK), CHUNK)

    def tables():
        cos = jnp.concatenate([cos_ref[...]] * 6, axis=1)
        sin = jnp.concatenate([sin_ref[...]] * 6, axis=1)
        return cos, sin

    def project_in(l):
        x = xs_[l]
        gain, _ = gains(l)
        a = (x * factor_of(x) * gain).astype(bf16)
        a_[l] = a
        qkv = dot(a, w_qo[l, :, :, 0:QKV].reshape(D, QKV))
        cos, sin = tables()
        u = qkv[:, 0:768]
        turned = u * cos + half_swap(u) * sin
        for h in range(HEADS):
            head = turned[:, h * 64 : h * 64 + 64].astype(bf16)
            q8_[l, h] = (head.astype(f32) * score_scale).astype(bf16)
        block = jnp.concatenate([turned[:, 576:768], qkv[:, 768:960]], axis=1).astype(bf16)
        kv[l, tokens] = block

    def attend(l):
        for g in range(KV_HEADS):
            q = q8_[l, 3 * g : 3 * g + 3].reshape(GROUP, 64)

            def keep(c, s):
                scr[:, keys_at(c)] = s
                top = jnp.maximum(
                    jnp.maximum(s[:, 0:128], s[:, 128:256]), jnp.maximum(s[:, 256:384], s[:, 384:512])
                )
                mx[...] = jnp.maximum(mx[...], top)

            def scores(c):
                k = kv[l, keys_at(c), :][:, g * 64 : g * 64 + 64]
                return dot_nt(q, k)

            mx[...] = jnp.full_like(mx, -1e30)

            def first(c, carry):
                keep(c, scores(c))
                return carry

            lax.fori_loop(0, nfull, first, 0)
            keep(nfull, jnp.where(causal(), scores(nfull), -1e30))
            peak = jnp.max(mx[...], axis=1, keepdims=True)
            acc[...] = jnp.zeros_like(acc)

            def second(c, carry):
                p = jnp.exp(scr[:, keys_at(c)] - peak).astype(bf16)
                v = kv[l, keys_at(c), :][:, 192 + g * 64 : 256 + g * 64]
                v = jnp.concatenate([v, jnp.ones_like(v)], axis=1)
                acc[...] += dot(p, v)
                return carry

            lax.fori_loop(0, nfull + 1, second, 0)
            total = acc[:, 64:65]
            mixed = (acc[:, 0:64] / total).astype(bf16)
            lse_[l, g] = peak + jnp.log(total)
            o_[l, 3 * g : 3 * g + 3] = mixed.reshape(3, TOK, 64)

    def heads_in(ref):
        return jnp.concatenate([ref[h] for h in range(HEADS)], axis=1)

    def after_attention(l):
        o = heads_in(o_.at[l])
        mid = xs_[l] + dot(o, w_qo[l, :, :, OAT : OAT + D].reshape(D, D))
        mid_[l] = mid
        _, gain = gains(l)
        bn_[l] = (mid * factor_of(mid) * gain).astype(bf16)
        acc2[...] = mid

        def tile(t, c):
            gcols = pl.ds(pl.multiple_of(t * FBAND, 128), FBAND)
            ucols = pl.ds(pl.multiple_of(FF + t * FBAND, 128), FBAND)
            bn = bn_[l]
            gt = dot(bn, w_gu[l, :, :, gcols].reshape(D, FBAND))
            up = dot(bn, w_gu[l, :, :, ucols].reshape(D, FBAND))
            gu_[l, :, gcols] = gt
            gu_[l, :, ucols] = up
            hid = (gt * jax.nn.sigmoid(gt) * up).astype(bf16)
            hid_[l, :, gcols] = hid
            acc2[...] += dot(hid, w_d[l, t].reshape(FBAND, D))
            return c

        lax.fori_loop(0, SIDE, tile, 0)
        return acc2[...]

    def ffn_back(l, dy):
        dyb_[...] = dy.astype(bf16)
        acc2[...] = jnp.zeros_like(acc2)

        def tile(t, c):
            gcols = pl.ds(pl.multiple_of(t * FBAND, 128), FBAND)
            ucols = pl.ds(pl.multiple_of(FF + t * FBAND, 128), FBAND)
            dyb = dyb_[...]
            bn = bn_[l]
            wd = w_d[l, t].reshape(FBAND, D)
            dhid = dot_nt(dyb, wd).astype(bf16).astype(f32)
            g_d[t] = dot_tn(hid_[l, :, gcols], dyb).astype(bf16).reshape(SIDE, FROWS, D)
            gt, up = gu_[l, :, gcols], gu_[l, :, ucols]
            s = jax.nn.sigmoid(gt)
            dgt = (dhid * up * s * (1.0 + gt * (1.0 - s))).astype(bf16)
            dup = (dhid * gt * s).astype(bf16)
            g_gu[:, :, gcols] = dot_tn(bn, dgt).astype(bf16).reshape(SIDE, BAND, FBAND)
            g_gu[:, :, ucols] = dot_tn(bn, dup).astype(bf16).reshape(SIDE, BAND, FBAND)
            acc2[...] += dot_nt(dgt, w_gu[l, :, :, gcols].reshape(D, FBAND))
            acc2[...] += dot_nt(dup, w_gu[l, :, :, ucols].reshape(D, FBAND))
            return c

        lax.fori_loop(0, SIDE, tile, 0)
        dbn = acc2[...]
        mid = mid_[l]
        r = factor_of(mid)
        _, gain = gains(l)
        gain_term[...] = (dbn * mid * r).astype(bf16)
        return dy + norm_back(mid, r, gain, dbn)

    def attention_back(l, dmid):
        dmb = dmid.astype(bf16)
        o = heads_in(o_.at[l])
        g_qo[:, :, OAT : OAT + 640] = jnp.concatenate(
            [dot_tn(o, dmb), jnp.zeros((D, 64), f32)], axis=1
        ).astype(bf16).reshape(SIDE, BAND, 640)
        dob = dot_nt(dmb, w_qo[l, :, :, OAT : OAT + D].reshape(D, D)).astype(bf16)
        for h in range(HEADS):
            do_h = dob[:, h * 64 : h * 64 + 64]
            dq_[h] = jnp.zeros((TOK, 64), f32)
            dob_[h] = do_h
        for g in range(KV_HEADS):
            do = dob_[3 * g : 3 * g + 3].reshape(GROUP, 64).astype(f32)
            og = o_[l, 3 * g : 3 * g + 3].reshape(GROUP, 64).astype(f32)
            delta_[g] = jnp.sum(do * og, axis=1, keepdims=True)

        def chunk(c, masked):
            kvb = kv[l, keys_at(c), :]
            dks, dvs = [], []
            for g in range(KV_HEADS):
                q = q8_[l, 3 * g : 3 * g + 3].reshape(GROUP, 64)
                do = dob_[3 * g : 3 * g + 3].reshape(GROUP, 64)
                k = kvb[:, g * 64 : g * 64 + 64]
                v = kvb[:, 192 + g * 64 : 256 + g * 64]
                s = dot_nt(q, k)
                if masked:
                    s = jnp.where(causal(), s, -1e30)
                p = jnp.exp(s - lse_[l, g])
                ds = (p * (dot_nt(do, v) - delta_[g])).astype(bf16)
                dq_[3 * g : 3 * g + 3] += dot(ds, k).reshape(3, TOK, 64)
                dks.append(dot_tn(ds, q))
                dvs.append(dot_tn(p.astype(bf16), do))
            dkv_s[keys_at(c), :] = jnp.concatenate(dks + dvs, axis=1).astype(bf16)

        def full(c, carry):
            chunk(c, False)
            for i in range(SIDE):
                dkv_start(l, c * SIDE + i)
            return carry

        lax.fori_loop(0, nfull, full, 0)
        chunk(nfull, True)

        def rest(j, carry):
            dkv_start(l, j)
            return carry

        lax.fori_loop(nfull * SIDE, sh, rest, 0)

    def finish_back(l, dmid_at):
        dkv_acc[...] = dkv_s[tokens, :].astype(f32)

        def add(d, c):
            arrived(dkv_r.at[l, d], at_dkv[l] + d)
            dkv_acc[...] += dkv_r[l, d].astype(f32)
            return c

        lax.fori_loop(1, SHARDS - sh, add, 0)
        dkv = dkv_acc[...]
        cos, sin = tables()
        dq = jnp.concatenate([dq_[h] for h in range(HEADS)], axis=1) * score_scale
        u = jnp.concatenate([dq, dkv[:, 0:192]], axis=1)
        back = u * cos - half_swap(u) * sin
        dqkv = jnp.concatenate([back, dkv[:, 192:384], jnp.zeros((TOK, 64), f32)], axis=1).astype(bf16)
        a = a_[l]
        gq = dot_tn(a, dqkv)
        da = dot_nt(dqkv, w_qo[l, :, :, 0:QKV].reshape(D, QKV))
        x = xs_[l]
        r = factor_of(x)
        gain, _ = gains(l)
        lane = lax.broadcasted_iota(jnp.int32, (TOK, 128), 1)
        e0 = jnp.where(lane == 64, 1.0, 0.0).astype(bf16)
        e1 = jnp.where(lane == 65, 1.0, 0.0).astype(bf16)
        cols = dot_tn((da * x * r).astype(bf16), e0) + dot_tn(gain_term[...], e1)
        g_qo[:, :, 0:896] = gq[:, 0:896].astype(bf16).reshape(SIDE, BAND, 896)
        g_qo[:, :, 896:1024] = (gq[:, 896:1024] + cols).astype(bf16).reshape(SIDE, BAND, 128)
        return dmid_at + norm_back(x, r, gain, da)

    kinds = (
        ("gu", 0, w_gu, g_gu, zr, ys, yr, xs, xr, fs, fr, GU),
        ("qo", 1, w_qo, g_qo, zr, ys, yr, xs, xr, fs, fr, QO),
        ("d", 1, w_d, g_d, zr_d, ys_d, yr_d, xs_d, xr_d, fs_d, fr_d, D),
    )
    at_rs = {k[0]: [take(1 + 3 + 3 + 3 + 1) for _ in range(2)] for k in kinds}

    def cut(ref, width):
        lead = (slice(None),) * (len(ref.shape) - 1)
        return ref.at[(*lead, pl.ds(0, width))]

    def of_core(kind):
        name, owner, w, g, zr, ys, yr, xs, xr, fs, fr, width = kind
        return owner, w, g, *[cut(r, width) for r in (zr, ys, yr, xs, xr, fs, fr)], width

    def free_weights(l):
        pl.semaphore_signal(credit.at[l], inc=1, device_id={"replica": sib}, device_id_type=MESH)

    def pair_start(l):
        pl.semaphore_wait(credit.at[l], 1)
        for kind in kinds:
            owner, w, g, *_ = of_core(kind)
            at = at_rs[kind[0]][l]

            @pl.when(core != owner)
            def _():
                copy(g, w.at[l], at, replica=sib).start()

    def tiles(width):
        step = 512 if width == GU else 128
        return step, width // step

    def rs_z_start(l):
        for kind in kinds:
            owner, w, g, zr, ys, yr, xs, xr, fs, fr, width = of_core(kind)
            at = at_rs[kind[0]][l]

            @pl.when(core == owner)
            def _():
                arrived(w.at[l], at)
                for d in (1, 2, 3, 0):
                    zt = lax.rem(z + d, SIDE)
                    if kind[0] == "d":
                        g[zt] = (g[zt].astype(f32) + w[l, zt].astype(f32)).astype(bf16)
                    else:
                        step, count = tiles(width)

                        def add(t, c):
                            cols = pl.ds(pl.multiple_of(t * step, 128), step)
                            g[zt, :, cols] = (
                                g[zt, :, cols].astype(f32) + w[l, zt, :, cols].astype(f32)
                            ).astype(bf16)
                            return c

                        lax.fori_loop(0, count, add, 0)
                    if d:
                        copy(g.at[zt], zr.at[d - 1], at + d, shard=z_peer(d)).start()

    def rs_y_start(l):
        for kind in kinds:
            owner, w, g, zr, ys, yr, xs, xr, fs, fr, width = of_core(kind)
            at = at_rs[kind[0]][l]

            @pl.when(core == owner)
            def _():
                for d in range(1, SIDE):
                    arrived(zr.at[d - 1], at + d)
                if kind[0] == "d":
                    tot = g[z].astype(f32)
                    for d in range(3):
                        tot += zr[d].astype(f32)
                    ys[...] = tot.astype(bf16)
                else:
                    step, count = tiles(width)

                    def add(t, c):
                        cols = pl.ds(pl.multiple_of(t * step, 128), step)
                        tot = g[z, :, cols].astype(f32)
                        for d in range(3):
                            tot += zr[d, :, cols].astype(f32)
                        for j in range(SIDE):
                            rows = tot[j * ROWS : j * ROWS + ROWS]
                            rows = jnp.concatenate([rows, jnp.zeros((PAD - ROWS, step), f32)], axis=0)
                            ys[j, :, cols] = rows.astype(bf16)
                        return c

                    lax.fori_loop(0, count, add, 0)
                for d in range(1, SIDE):
                    yt = lax.rem(y + d, SIDE)
                    copy(ys.at[yt], yr.at[d - 1], at + 3 + d, shard=y_peer(d)).start()

    def x_targets(l):
        for k in (1, 2, 3):
            other = 1 - sec if k >= 2 else sec
            where = {}
            if k >= 2:
                where["section"] = 1 - sec
            if k % 2:
                where["replica"] = far
            yield k, other == l, where

    def rs_x_start(l):
        for kind in kinds:
            owner, w, g, zr, ys, yr, xs, xr, fs, fr, width = of_core(kind)
            at = at_rs[kind[0]][l]

            @pl.when(core == owner)
            def _():
                for d in range(1, SIDE):
                    arrived(yr.at[d - 1], at + 3 + d)
                tot = ys[y].astype(f32)
                for d in range(3):
                    tot += yr[d].astype(f32)
                xs[...] = tot.astype(bf16)
                for k, hit, where in x_targets(l):
                    @pl.when(hit)
                    def _():
                        copy(xs, xr.at[k - 1], at + 6 + k, **where).start()

    def write_out(kind, tot):
        if kind[0] == "d":
            gd_ref[0] = tot
        elif kind[0] == "gu":
            gg_ref[0] = tot[0:ROWS, 0:FF]
            gu_ref[0] = tot[0:ROWS, FF:GU]
        else:
            gq_ref[0] = tot[0:ROWS, 0:576]
            gk_ref[0] = tot[0:ROWS, 576:768]
            gv_ref[0] = tot[0:ROWS, 768:960]
            go_ref[0] = tot[0:ROWS, OAT : OAT + D]
            gain_ref[...] = tot[0:ROWS, 896:1024]

    def rs_end_start(l):
        for kind in kinds:
            owner, w, g, zr, ys, yr, xs, xr, fs, fr, width = of_core(kind)
            at = at_rs[kind[0]][l]

            @pl.when((core == owner) & (sec == l))
            def _():
                for k in (1, 2, 3):
                    arrived(xr.at[k - 1], at + 6 + k)
                tot = xs[...].astype(f32)
                for k in range(3):
                    tot += xr[k].astype(f32)
                fs[...] = tot.astype(bf16)
                copy(fs, fr, at + 10, replica=sib).start()
                write_out(kind, tot)

    def rs_end(l):
        for kind in kinds:
            owner, w, g, zr, ys, yr, xs, xr, fs, fr, width = of_core(kind)
            at = at_rs[kind[0]][l]

            @pl.when((core != owner) & (sec == l))
            def _():
                arrived(fr, at + 10)
                write_out(kind, fr[...].astype(f32))

    def rs_sent(l):
        for kind in kinds:
            owner, w, g, zr, ys, yr, xs, xr, fs, fr, width = of_core(kind)
            at = at_rs[kind[0]][l]

            @pl.when(core != owner)
            def _():
                sent(g, at)

            @pl.when(core == owner)
            def _():
                for d in range(1, SIDE):
                    sent(zr.at[0], at + d)
                    sent(yr.at[0], at + 3 + d)
                for k, hit, where in x_targets(l):
                    @pl.when(hit)
                    def _():
                        sent(xs, at + 6 + k)

                @pl.when(sec == l)
                def _():
                    sent(fs, at + 10)

    def again():
        for d in range(1, SIDE):
            pl.semaphore_signal(credit.at[2], inc=1, device_id={"shard": y_peer(d)}, device_id_type=MESH)
            pl.semaphore_signal(credit.at[2], inc=1, device_id={"shard": z_peer(d)}, device_id_type=MESH)
        pl.semaphore_signal(credit.at[2], inc=1, device_id={"replica": sib}, device_id_type=MESH)
        pl.semaphore_signal(credit.at[2], inc=1, device_id={"replica": far}, device_id_type=MESH)
        pl.semaphore_signal(credit.at[2], inc=1, device_id={"section": 1 - sec}, device_id_type=MESH)
        pl.semaphore_signal(
            credit.at[2], inc=1, device_id={"section": 1 - sec, "replica": far}, device_id_type=MESH
        )

    def again_wait():
        pl.semaphore_wait(credit.at[2], 10)

    at_o = [take(1) for _ in range(2)]
    at_d = [take(1) for _ in range(2)]

    def hand_over(l, value, own_ref, send, recv, at):
        @pl.when(sec == l)
        def _():
            own_ref[0, sec, 0] = value

        @pl.when(sec != l)
        def _():
            send[...] = value
            copy(send, recv, at[l], section=1 - sec).start()

    def hand_over_end(own_ref, send, recv, at):
        for l in range(2):
            @pl.when(sec == l)
            def _():
                arrived(recv, at[l])
                own_ref[0, 1 - sec, 0] = recv[...]

            @pl.when(sec != l)
            def _():
                sent(send, at[l])

    x_start()
    for l in range(2):
        y_start(l)
        dz_start(l)
    for l in range(2):
        z_start(l)
        dy_start(l)
    for l in range(2):
        forward_on(l)
        d_forward_on(l)
    for l in range(2):
        gather_end(l)
        gather_sent(l)

    xs_[0] = x_ref[sec, 0].astype(f32)
    for l in range(2):
        project_in(l)
        kv_start(l)
        kv_wait(l)
        attend(l)
        out = after_attention(l).astype(bf16)
        hand_over(l, out, out_ref, osend, orecv, at_o)
        if l == 0:
            xs_[1] = out.astype(f32)
        kv_sent(l)

    dy = dy_ref[sec, 0].astype(f32)
    for l in (1, 0):
        dmid = ffn_back(l, dy)
        mid_[l] = dmid
        attention_back(l, dmid)
        dx = finish_back(l, mid_[l])
        hand_over(l, dx, dx_ref, dsend, drecv, at_d)
        dy = dx.astype(bf16).astype(f32)
        dkv_sent(l)
        free_weights(l)
        pair_start(l)
        if l == 0:
            again_wait()
        rs_z_start(l)
        rs_y_start(l)
        rs_x_start(l)
        rs_end_start(l)
        rs_end(l)
        rs_sent(l)
        if l == 1:
            again()
    hand_over_end(out_ref, osend, orecv, at_o)
    hand_over_end(dx_ref, dsend, drecv, at_d)
    assert used[0] <= SEMS, used[0]


SEMS = 320


def scratch():
    v = lambda *shape: pltpu.VMEM(shape, bf16)
    w = lambda *shape: pltpu.VMEM(shape, f32)
    return dict(
        stage=v(2, SIDE, PAD, GU), w_gu=v(2, SIDE, BAND, GU), w_qo=v(2, SIDE, BAND, QO),
        w_d=v(2, SIDE, SIDE, FROWS, D), kv=v(2, SHARDS * TOK, 384), dkv_s=v(SHARDS * TOK, 384),
        dkv_r=v(2, SHARDS, TOK, 384), scr=w(GROUP, SHARDS * TOK), mx=w(GROUP, 128), acc=w(GROUP, 128),
        xs_=w(2, TOK, D), a_=v(2, TOK, D), q8_=v(2, HEADS, TOK, 64), o_=v(2, HEADS, TOK, 64),
        lse_=w(2, KV_HEADS, GROUP, 1), mid_=w(2, TOK, D), bn_=v(2, TOK, D), gu_=w(2, TOK, GU),
        hid_=v(2, TOK, FF), dyb_=v(TOK, D), dob_=v(HEADS, TOK, 64), delta_=w(KV_HEADS, GROUP, 1),
        dq_=w(HEADS, TOK, 64), dkv_acc=w(TOK, 384), acc2=w(TOK, D), gain_term=v(TOK, D),
        g_gu=v(SIDE, BAND, GU), g_qo=v(SIDE, BAND, QO), g_d=v(SIDE, SIDE, FROWS, D),
        zr=v(3, BAND, GU), zr_d=v(3, SIDE, FROWS, D), ys=v(SIDE, PAD, GU), ys_d=v(SIDE, FROWS, D),
        yr=v(3, PAD, GU), yr_d=v(3, FROWS, D), xs=v(PAD, GU), xs_d=v(FROWS, D),
        xr=v(3, PAD, GU), xr_d=v(3, FROWS, D), fs=v(PAD, GU), fs_d=v(FROWS, D),
        fr=v(PAD, GU), fr_d=v(FROWS, D),
        osend=v(TOK, D), orecv=v(TOK, D), dsend=w(TOK, D), drecv=w(TOK, D),
        ssem=pltpu.SemaphoreType.DMA((SEMS,)), rsem=pltpu.SemaphoreType.DMA((SEMS,)),
        credit=pltpu.SemaphoreType.REGULAR((3,)),
    )


def kernel(*refs):
    body(*refs)


def local(
    inputs, out_grad, w_query, w_key, w_value, w_out, w_gate, w_up, w_down, gain_attn, gain_ffn
):
    shard_index = lax.axis_index("shard")
    positions = shard_index * TOK + jnp.arange(TOK, dtype=jnp.int32)
    half = HEAD_DIM // 2
    inverse = rope_base ** (-(jnp.arange(half, dtype=f32) * 2.0 / HEAD_DIM))
    angles = positions.astype(f32)[:, None] * inverse[None, :]
    cos, sin = jnp.cos(angles), jnp.sin(angles)
    cos = jnp.concatenate([cos] * 4, axis=1)
    sin = jnp.concatenate([-sin, sin, -sin, sin], axis=1)
    more = ((0, PAD - ROWS), (0, 0))
    p0 = jnp.pad(jnp.concatenate([w_gate[0], w_up[0]], axis=1), more)
    gain_cols = jnp.stack([gain_attn[0], gain_ffn[0]], axis=1)
    p1 = jnp.concatenate(
        [w_query[0], w_key[0], w_value[0], gain_cols, jnp.zeros((ROWS, 62), bf16), w_out[0],
         jnp.zeros((ROWS, 64), bf16)], axis=1,
    )
    p1 = jnp.pad(p1, more)
    whole = pl.BlockSpec(memory_space=pltpu.VMEM)
    shapes = (
        ((1, 2, 1, TOK, D), bf16), ((1, 2, 1, TOK, D), f32),
        ((1, ROWS, 576), f32), ((1, ROWS, 192), f32), ((1, ROWS, 192), f32), ((1, ROWS, 576), f32),
        ((1, ROWS, FF), f32), ((1, ROWS, FF), f32), ((1, FROWS, D), f32), ((ROWS, 128), f32),
    )
    res = pl.pallas_call(
        kernel,
        out_shape=[jax.ShapeDtypeStruct(s, t) for s, t in shapes],
        in_specs=[whole] * 7,
        out_specs=[whole] * len(shapes),
        scratch_shapes=list(scratch().values()),
        compiler_params=pltpu.CompilerParams(
            collective_id=0, has_side_effects=True, vmem_limit_bytes=63 * 1024 * 1024
        ),
        name="two_layers",
    )(inputs, out_grad, p0, p1, w_down[0], cos, sin)
    out, dx, gq, gk, gv, go, gg, gu, gd, gain = res
    return (out, dx, gq, gk, gv, go, gg, gu, gd, gain[:, 64][None], gain[:, 65][None])


def solution(mesh):
    return jax.shard_map(
        local,
        mesh=mesh,
        in_specs=(
            P(None, "replica", "shard", None),
            P(None, "replica", "shard", None),
            P("section", "shard", None),
            P("section", "shard", None),
            P("section", "shard", None),
            P("section", "shard", None),
            P("section", "shard", None),
            P("section", "shard", None),
            P("section", "shard", None),
            P("section", "shard"),
            P("section", "shard"),
        ),
        out_specs=(
            P("section", None, "replica", "shard", None),
            P("section", None, "replica", "shard", None),
            P("section", "shard", None),
            P("section", "shard", None),
            P("section", "shard", None),
            P("section", "shard", None),
            P("section", "shard", None),
            P("section", "shard", None),
            P("section", "shard", None),
            P("section", "shard"),
            P("section", "shard"),
        ),
        check_vma=False,
    )
```

```python
import functools

import jax
import jax.numpy as jnp
from jax import lax
from jax.experimental import pallas as pl
from jax.experimental.pallas import tpu as pltpu
from jax.sharding import PartitionSpec as P

HEADS = 9
KV_HEADS = 3
HEAD_DIM = 64
D = 576
FF = 1536
TOK = 128
SHARDS = 16
SIDE = 4
ROWS = 36
PAD = 48
BAND = SIDE * ROWS
FROWS = 96
FBAND = SIDE * FROWS
GU = 2 * FF
QKV = 1024
OUT = 640
CHUNK = 512
GROUP = 3 * TOK

bf16 = jnp.bfloat16
f32 = jnp.float32
MESH = pl.DeviceIdType.MESH
epsilon = 1e-05
rope_base = 100000.0
score_scale = 0.125


def dot(a, b):
    return lax.dot_general(a, b, (((1,), (0,)), ((), ())), preferred_element_type=f32)


def dot_nt(a, b):
    return lax.dot_general(a, b, (((1,), (1,)), ((), ())), preferred_element_type=f32)


def dot_tn(a, b):
    return lax.dot_general(a, b, (((0,), (0,)), ((), ())), preferred_element_type=f32)


def factor_of(v):
    return lax.rsqrt(jnp.mean(v * v, axis=-1, keepdims=True) + epsilon)


def norm_back(v, r, gain, up):
    scaled = gain * up
    return r * scaled - v * (r * r * r) * jnp.mean(scaled * v, axis=-1, keepdims=True)


def half_swap(u):
    width = u.shape[1]
    lane = lax.broadcasted_iota(jnp.int32, u.shape, 1)
    first = lax.rem(lane, HEAD_DIM) < HEAD_DIM // 2
    return jnp.where(first, pltpu.roll(u, width - 32, 1), pltpu.roll(u, 32, 1))


def body(
    x_ref, dy_ref, p0_ref, pq_ref, po_ref, pd_ref, cos_ref, sin_ref,
    out_ref, dx_ref, gq_ref, gk_ref, gv_ref, go_ref, gg_ref, gu_ref, gd_ref, gain_ref,
    stage_gu, stage_q, stage_o, w_gu, w_q, w_o, w_d, kv, dkv_r, scr, mx, acc,
    xs_, a_, q8_, o_, lse_, mid_, bn_, gu_,
    dyb_, dob_, delta_, dq_, dkv_acc, acc2, gain_term,
    g_gu, g_q, g_o, g_d, xg,
    zr_gu, zr_q, zr_o, zr_d, ys_gu, ys_q, ys_o, ys_d, yr_gu, yr_q, yr_o, yr_d,
    xs_gu, xs_q, xs_o, xs_d, xr_gu, xr_q, xr_o, xr_d, fs_gu, fs_q, fs_o, fs_d, fr_gu, fr_q, fr_o, fr_d,
    osend, orecv, dsend, drecv,
    ssem, rsem, credit,
):
    sec = lax.axis_index("section")
    sh = lax.axis_index("shard")
    rep = lax.axis_index("replica")
    z, y = lax.div(sh, SIDE), lax.rem(sh, SIDE)
    core = lax.rem(rep, 2)
    sib = rep + 1 - 2 * core
    far = lax.rem(rep + 2, 4)
    used = [0]

    def take(n):
        at = used[0]
        used[0] += n
        return at

    def copy(src, dst, at, **dev):
        return pltpu.make_async_remote_copy(
            src_ref=src, dst_ref=dst, send_sem=ssem.at[at], recv_sem=rsem.at[at],
            device_id=dev, device_id_type=MESH,
        )

    def arrived(dst, at):
        copy(dst, dst, at, shard=sh).wait_recv()

    def sent(src, at):
        copy(src, src, at, shard=sh).wait_send()

    def y_peer(d):
        return z * SIDE + lax.rem(y + d, SIDE)

    def z_peer(d):
        return lax.rem(z + d, SIDE) * SIDE + y

    def z_from(d):
        return lax.rem(z + SIDE - d, SIDE)

    def y_from(d):
        return lax.rem(y + SIDE - d, SIDE)

    last = pl.ds(pl.multiple_of(lax.div(sh, SIDE) * CHUNK, CHUNK), CHUNK)
    for l in range(2):
        kv[l, last, :] = jnp.zeros((CHUNK, 384), bf16)
    barrier = pltpu.get_barrier_semaphore()

    def greet(d, c):
        pl.semaphore_signal(barrier, inc=1, device_id={"shard": lax.rem(sh + d, SHARDS)}, device_id_type=MESH)
        return c

    lax.fori_loop(1, SHARDS, greet, 0)
    pl.semaphore_signal(barrier, inc=1, device_id={"replica": sib}, device_id_type=MESH)
    pl.semaphore_signal(barrier, inc=1, device_id={"replica": far}, device_id_type=MESH)
    pl.semaphore_signal(barrier, inc=1, device_id={"section": 1 - sec}, device_id_type=MESH)
    pl.semaphore_signal(barrier, inc=1, device_id={"section": 1 - sec, "replica": far}, device_id_type=MESH)
    pl.semaphore_wait(barrier, SHARDS - 1 + 4)

    mine = pl.ds(pl.multiple_of(sec * FF, 128), FF)
    theirs = pl.ds(pl.multiple_of((1 - sec) * FF, 128), FF)

    class Gather:
        def __init__(self, owner, send, keep, stage, w, cols, width):
            self.owner, self.send, self.keep, self.stage, self.w, self.width = owner, send, keep, stage, w, width
            self.cols = cols
            self.at_x = take(1)
            self.at_y = [take(3) for _ in range(2)]
            self.at_z = [take(3) for _ in range(2)]
            self.at_f = [take(4) for _ in range(2)]

        def band(self, l, j):
            return self.w.at[l, j, :, self.cols]

    kgu = Gather(0, p0_ref.at[:, theirs], p0_ref.at[:, mine], stage_gu, w_gu, mine, FF)
    kq = Gather(1, pq_ref, pq_ref, stage_q, w_q, pl.ds(0, QKV), QKV)
    ko = Gather(1, po_ref, po_ref, stage_o, w_o, pl.ds(0, OUT), OUT)
    at_xd = take(1)
    at_dz = [take(3) for _ in range(2)]
    at_dy = [take(3) for _ in range(2)]
    at_df = [take(1) for _ in range(2)]
    at_swap = [take(4) for _ in range(2)]
    at_sf = [take(4) for _ in range(2)]

    def x_start(k):
        @pl.when(core == k.owner)
        def _():
            copy(k.send, k.stage.at[sec, y], k.at_x, section=1 - sec).start()
            k.stage[sec, y] = k.keep[...]

    def dx_start():
        @pl.when(core == 1)
        def _():
            copy(pd_ref, w_d.at[sec, z, y], at_xd, section=1 - sec).start()
            w_d[sec, z, y] = pd_ref[...]

    def y_start(k, l):
        @pl.when(core == k.owner)
        def _():
            own = k.stage.at[l, y]

            @pl.when(sec != l)
            def _():
                arrived(own, k.at_x)

            for d in (2, 1, 3):
                copy(own, own, k.at_y[l] + d - 1, shard=y_peer(d)).start()

    def dz_start(l):
        @pl.when(core == 1)
        def _():
            own = w_d.at[l, z, y]

            @pl.when(sec != l)
            def _():
                arrived(own, at_xd)

            for d in (2, 1, 3):
                copy(own, own, at_dz[l] + d - 1, shard=z_peer(d)).start()

    def z_start(k, l):
        @pl.when(core == k.owner)
        def _():
            for d in range(1, SIDE):
                arrived(k.stage.at[l, y_from(d)], k.at_y[l] + d - 1)
            own = k.band(l, z)
            for at in range(0, k.width, 128):
                parts = [k.stage[l, j, :, at : at + 128][0:ROWS].astype(f32) for j in range(SIDE)]
                own[:, at : at + 128] = jnp.concatenate(parts, axis=0).astype(bf16)
            for d in (2, 1, 3):
                copy(own, own, k.at_z[l] + d - 1, shard=z_peer(d)).start()
            copy(own, own, k.at_f[l], replica=sib).start()

    def dy_start(l):
        @pl.when(core == 1)
        def _():
            for d in range(1, SIDE):
                arrived(w_d.at[l, z_from(d), y], at_dz[l] + d - 1)
            own = w_d.at[l, :, y]
            for d in (2, 1, 3):
                copy(own, own, at_dy[l] + d - 1, shard=y_peer(d)).start()

    def z_end(k, l):
        @pl.when(core == k.owner)
        def _():
            for d in (1, 3, 2):
                got = k.band(l, z_from(d))
                arrived(got, k.at_z[l] + d - 1)
                copy(got, got, k.at_f[l] + d, replica=sib).start()
            if k is kgu:
                for j in range(SIDE):
                    got = k.band(l, j)
                    copy(got, got, at_swap[l] + j, **swap_to(j)).start()

    def swap_to(j):
        return {"section": 1 - sec} if j < 2 else {"section": 1 - sec, "replica": far}

    def swap_end(l):
        @pl.when(core == 0)
        def _():
            for j in range(SIDE):
                got = w_gu.at[l, j, :, theirs]
                arrived(got, at_swap[l] + j)
                copy(got, got, at_sf[l] + j, replica=sib).start()

    def d_forward_on(l):
        @pl.when(core == 1)
        def _():
            for d in range(1, SIDE):
                arrived(w_d.at[l, :, y_from(d)], at_dy[l] + d - 1)
            copy(w_d.at[l], w_d.at[l], at_df[l], replica=sib).start()

    def gather_end(k, l):
        @pl.when(core != k.owner)
        def _():
            arrived(k.band(l, z), k.at_f[l])
            for d in range(1, SIDE):
                arrived(k.band(l, z_from(d)), k.at_f[l] + d)
            if k is kgu:
                for j in range(SIDE):
                    arrived(w_gu.at[l, j, :, theirs], at_sf[l] + j)

    def d_gather_end(l):
        @pl.when(core == 0)
        def _():
            arrived(w_d.at[l], at_df[l])

    def gather_sent():
        for l in range(2):
            for k in (kgu, kq, ko):
                @pl.when(core == k.owner)
                def _():
                    @pl.when(sec == l)
                    def _():
                        sent(k.send, k.at_x)

                    for d in range(1, SIDE):
                        sent(k.stage.at[l, y], k.at_y[l] + d - 1)
                        sent(k.band(l, z), k.at_z[l] + d - 1)
                        sent(k.band(l, z), k.at_f[l] + d)
                    sent(k.band(l, z), k.at_f[l])
                    if k is kgu:
                        for j in range(SIDE):
                            sent(k.band(l, j), at_swap[l] + j)
                            sent(k.band(l, j), at_sf[l] + j)

            @pl.when(core == 1)
            def _():
                @pl.when(sec == l)
                def _():
                    sent(pd_ref, at_xd)

                for d in range(1, SIDE):
                    sent(w_d.at[l, z, y], at_dz[l] + d - 1)
                    sent(w_d.at[l, :, y], at_dy[l] + d - 1)
                sent(w_d.at[l], at_df[l])

    at_kv = [take(SHARDS) for _ in range(2)]
    at_dkv = [take(SHARDS) for _ in range(2)]
    tokens = pl.ds(pl.multiple_of(sh * TOK, TOK), TOK)

    def kv_start(l):
        own = kv.at[l, tokens]

        def go(d, c):
            copy(own, own, at_kv[l] + d, shard=sh + d).start()
            return c

        lax.fori_loop(1, SHARDS - sh, go, 0)

    def kv_wait(l):
        def go(d, c):
            arrived(kv.at[l, pl.ds(pl.multiple_of((sh - d) * TOK, TOK), TOK)], at_kv[l] + d)
            return c

        lax.fori_loop(1, sh + 1, go, 0)

    def kv_sent(l):
        def go(d, c):
            sent(kv.at[l, tokens], at_kv[l] + d)
            return c

        lax.fori_loop(1, SHARDS - sh, go, 0)

    def dkv_start(l, j):
        src = kv.at[l, pl.ds(pl.multiple_of(j * TOK, TOK), TOK)]
        copy(src, dkv_r.at[l, sh - j - 1], at_dkv[l] + sh - j, shard=j).start()

    def dkv_sent(l):
        def go(d, c):
            sent(kv.at[l, pl.ds(0, TOK)], at_dkv[l] + d)
            return c

        lax.fori_loop(1, sh + 1, go, 0)

    def gains(l):
        tile = w_q[l, :, :, 896:1024].reshape(D, 128)
        row = lax.broadcasted_iota(jnp.int32, (8, 128), 0)
        lane = lax.broadcasted_iota(jnp.int32, (8, 128), 1)
        pick = jnp.where(lane == row + 64, 1.0, 0.0).astype(bf16)
        both = dot_nt(pick, tile)
        return both[0:1], both[1:2]

    nfull = lax.div(sh, SIDE)

    def causal():
        row = lax.broadcasted_iota(jnp.int32, (GROUP, CHUNK), 0)
        col = lax.broadcasted_iota(jnp.int32, (GROUP, CHUNK), 1)
        return col <= lax.rem(sh, SIDE) * TOK + lax.rem(row, TOK)

    def keys_at(c):
        return pl.ds(pl.multiple_of(c * CHUNK, CHUNK), CHUNK)

    def tables():
        cos = jnp.concatenate([cos_ref[...]] * 6, axis=1)
        sin = jnp.concatenate([sin_ref[...]] * 6, axis=1)
        return cos, sin

    def project_in(l):
        x = xs_[l]
        gain, _ = gains(l)
        a = (x * factor_of(x) * gain).astype(bf16)
        a_[l] = a
        qkv = dot(a, w_q[l].reshape(D, QKV))
        cos, sin = tables()
        u = qkv[:, 0:768]
        turned = u * cos + half_swap(u) * sin
        for h in range(HEADS):
            head = turned[:, h * 64 : h * 64 + 64].astype(bf16)
            q8_[l, h] = (head.astype(f32) * score_scale).astype(bf16)
        block = jnp.concatenate([turned[:, 576:768], qkv[:, 768:960]], axis=1).astype(bf16)
        kv[l, tokens] = block

    def attend(l, g):
        if True:
            q = q8_[l, 3 * g : 3 * g + 3].reshape(GROUP, 64)

            def keep(c, s):
                scr[:, keys_at(c)] = s
                top = jnp.maximum(
                    jnp.maximum(s[:, 0:128], s[:, 128:256]), jnp.maximum(s[:, 256:384], s[:, 384:512])
                )
                mx[...] = jnp.maximum(mx[...], top)

            def scores(c):
                k = kv[l, keys_at(c), :][:, g * 64 : g * 64 + 64]
                return dot_nt(q, k)

            mx[...] = jnp.full_like(mx, -1e30)

            def first(c, carry):
                keep(c, scores(c))
                return carry

            lax.fori_loop(0, nfull, first, 0)
            keep(nfull, jnp.where(causal(), scores(nfull), -1e30))
            peak = jnp.max(mx[...], axis=1, keepdims=True)
            acc[...] = jnp.zeros_like(acc)

            def second(c, carry):
                p = jnp.exp(scr[:, keys_at(c)] - peak).astype(bf16)
                v = kv[l, keys_at(c), :][:, 192 + g * 64 : 256 + g * 64]
                v = jnp.concatenate([v, jnp.ones_like(v)], axis=1)
                acc[...] += dot(p, v)
                return carry

            lax.fori_loop(0, nfull + 1, second, 0)
            total = acc[:, 64:65]
            mixed = (acc[:, 0:64] / total).astype(bf16)
            lse_[l, g] = peak + jnp.log(total)
            o_[l, 3 * g : 3 * g + 3] = mixed.reshape(3, TOK, 64)

    def heads_in(ref):
        return jnp.concatenate([ref[h] for h in range(HEADS)], axis=1)

    def after_attention(l):
        o = heads_in(o_.at[l])
        mid = xs_[l] + dot(o, w_o[l, :, :, 0:D].reshape(D, D))
        mid_[l] = mid
        _, gain = gains(l)
        bn_[l] = (mid * factor_of(mid) * gain).astype(bf16)
        acc2[...] = mid

        def tile(t, c):
            gcols = pl.ds(pl.multiple_of(t * FBAND, 128), FBAND)
            ucols = pl.ds(pl.multiple_of(FF + t * FBAND, 128), FBAND)
            bn = bn_[l]
            gt = dot(bn, w_gu[l, :, :, gcols].reshape(D, FBAND))
            up = dot(bn, w_gu[l, :, :, ucols].reshape(D, FBAND))
            gu_[l, :, gcols] = gt
            gu_[l, :, ucols] = up
            hid = (gt * jax.nn.sigmoid(gt) * up).astype(bf16)
            acc2[...] += dot(hid, w_d[l, t].reshape(FBAND, D))
            return c

        lax.fori_loop(0, SIDE, tile, 0)
        return acc2[...]

    def ffn_back(l, dy):
        dyb_[...] = dy.astype(bf16)
        acc2[...] = jnp.zeros_like(acc2)

        def tile(t, c):
            gcols = pl.ds(pl.multiple_of(t * FBAND, 128), FBAND)
            ucols = pl.ds(pl.multiple_of(FF + t * FBAND, 128), FBAND)
            dyb = dyb_[...]
            bn = bn_[l]
            wd = w_d[l, t].reshape(FBAND, D)
            dhid = dot_nt(dyb, wd).astype(bf16).astype(f32)
            gt, up = gu_[l, :, gcols], gu_[l, :, ucols]
            s = jax.nn.sigmoid(gt)
            hid = (gt * s * up).astype(bf16)
            g_d[t] = dot_tn(hid, dyb).astype(bf16).reshape(SIDE, FROWS, D)
            dgt = (dhid * up * s * (1.0 + gt * (1.0 - s))).astype(bf16)
            dup = (dhid * gt * s).astype(bf16)
            g_gu[:, :, gcols] = dot_tn(bn, dgt).astype(bf16).reshape(SIDE, BAND, FBAND)
            g_gu[:, :, ucols] = dot_tn(bn, dup).astype(bf16).reshape(SIDE, BAND, FBAND)
            acc2[...] += dot_nt(dgt, w_gu[l, :, :, gcols].reshape(D, FBAND))
            acc2[...] += dot_nt(dup, w_gu[l, :, :, ucols].reshape(D, FBAND))
            return c

        lax.fori_loop(0, SIDE, tile, 0)
        dbn = acc2[...]
        mid = mid_[l]
        r = factor_of(mid)
        _, gain = gains(l)
        gain_term[...] = (dbn * mid * r).astype(bf16)
        return dy + norm_back(mid, r, gain, dbn)

    def out_back(l, dmid):
        dmb = dmid.astype(bf16)
        o = heads_in(o_.at[l])
        g_o[...] = jnp.concatenate(
            [dot_tn(o, dmb), jnp.zeros((D, 64), f32)], axis=1
        ).astype(bf16).reshape(SIDE, BAND, 640)
        dob = dot_nt(dmb, w_o[l, :, :, 0:D].reshape(D, D)).astype(bf16)
        for h in range(HEADS):
            do_h = dob[:, h * 64 : h * 64 + 64]
            dq_[h] = jnp.zeros((TOK, 64), f32)
            dob_[h] = do_h

    def attention_back(l):
        for g in range(KV_HEADS):
            do = dob_[3 * g : 3 * g + 3].reshape(GROUP, 64).astype(f32)
            og = o_[l, 3 * g : 3 * g + 3].reshape(GROUP, 64).astype(f32)
            delta_[g] = jnp.sum(do * og, axis=1, keepdims=True)

        def chunk(c, masked):
            kvb = kv[l, keys_at(c), :]
            dks, dvs = [], []
            for g in range(KV_HEADS):
                q = q8_[l, 3 * g : 3 * g + 3].reshape(GROUP, 64)
                do = dob_[3 * g : 3 * g + 3].reshape(GROUP, 64)
                k = kvb[:, g * 64 : g * 64 + 64]
                v = kvb[:, 192 + g * 64 : 256 + g * 64]
                s = dot_nt(q, k)
                if masked:
                    s = jnp.where(causal(), s, -1e30)
                p = jnp.exp(s - lse_[l, g])
                ds = (p * (dot_nt(do, v) - delta_[g])).astype(bf16)
                dq_[3 * g : 3 * g + 3] += dot(ds, k).reshape(3, TOK, 64)
                dks.append(dot_tn(ds, q))
                dvs.append(dot_tn(p.astype(bf16), do))
            kv[l, keys_at(c), :] = jnp.concatenate(dks + dvs, axis=1).astype(bf16)

        def full(c, carry):
            chunk(c, False)
            for i in range(SIDE):
                dkv_start(l, c * SIDE + i)
            return carry

        lax.fori_loop(0, nfull, full, 0)
        chunk(nfull, True)

        def rest(j, carry):
            dkv_start(l, j)
            return carry

        lax.fori_loop(nfull * SIDE, sh, rest, 0)

    def finish_back(l, dmid_at):
        dkv_acc[...] = kv[l, tokens, :].astype(f32)

        def add(d, c):
            arrived(dkv_r.at[l, d - 1], at_dkv[l] + d)
            dkv_acc[...] += dkv_r[l, d - 1].astype(f32)
            return c

        lax.fori_loop(1, SHARDS - sh, add, 0)
        dkv = dkv_acc[...]
        cos, sin = tables()
        dq = jnp.concatenate([dq_[h] for h in range(HEADS)], axis=1) * score_scale
        u = jnp.concatenate([dq, dkv[:, 0:192]], axis=1)
        back = u * cos - half_swap(u) * sin
        dqkv = jnp.concatenate([back, dkv[:, 192:384], jnp.zeros((TOK, 64), f32)], axis=1).astype(bf16)
        a = a_[l]
        gq = dot_tn(a, dqkv)
        da = dot_nt(dqkv, w_q[l].reshape(D, QKV))
        x = xs_[l]
        r = factor_of(x)
        gain, _ = gains(l)
        lane = lax.broadcasted_iota(jnp.int32, (TOK, 128), 1)
        e0 = jnp.where(lane == 64, 1.0, 0.0).astype(bf16)
        e1 = jnp.where(lane == 65, 1.0, 0.0).astype(bf16)
        cols = dot_tn((da * x * r).astype(bf16), e0) + dot_tn(gain_term[...], e1)
        g_q[:, :, 0:896] = gq[:, 0:896].astype(bf16).reshape(SIDE, BAND, 896)
        g_q[:, :, 896:1024] = (gq[:, 896:1024] + cols).astype(bf16).reshape(SIDE, BAND, 128)
        return dmid_at + norm_back(x, r, gain, da)

    class Sum:
        def __init__(self, name, owner, w, cols, g, zr, ys, yr, xs, xr, fs, fr, width):
            self.name, self.owner, self.w, self.cols, self.g = name, owner, w, cols, g
            self.zr, self.ys, self.yr, self.xs, self.xr, self.fs, self.fr = zr, ys, yr, xs, xr, fs, fr
            self.width = width
            self.at = [take(12) for _ in range(2)]
            self.free = credits(2)
            self.again_z, self.again_y = credits(1), credits(1)

        def band(self, l, j):
            return self.w.at[l, j] if self.name == "d" else self.w.at[l, j, :, self.cols]

    granted = [0]

    def credits(n):
        at = granted[0]
        granted[0] += n
        return at

    sgu = Sum("gu", 0, w_gu, mine, g_gu, zr_gu, ys_gu, yr_gu, xs_gu, xr_gu, fs_gu, fr_gu, FF)
    sq = Sum("q", 1, w_q, pl.ds(0, QKV), g_q, zr_q, ys_q, yr_q, xs_q, xr_q, fs_q, fr_q, QKV)
    so = Sum("o", 1, w_o, pl.ds(0, OUT), g_o, zr_o, ys_o, yr_o, xs_o, xr_o, fs_o, fr_o, OUT)
    sd = Sum("d", 1, w_d, None, g_d, zr_d, ys_d, yr_d, xs_d, xr_d, fs_d, fr_d, D)
    at_rswap = [take(4) for _ in range(2)]
    swap_again = credits(1)

    def pair_start(k, l):
        pl.semaphore_signal(credit.at[k.free + l], inc=1, device_id={"replica": sib}, device_id_type=MESH)
        pl.semaphore_wait(credit.at[k.free + l], 1)

        @pl.when(core != k.owner)
        def _():
            copy(k.g, k.w.at[l], k.at[l], replica=sib).start()

    def pair_sent(k, l):
        @pl.when(core != k.owner)
        def _():
            sent(k.g, k.at[l])

    def add_into(dst, src, width):
        step = 256 if width % 256 == 0 else 128

        def add(t, c):
            cols = pl.ds(pl.multiple_of(t * step, 128), step)
            dst[:, cols] = (dst[:, cols].astype(f32) + src[:, cols].astype(f32)).astype(bf16)
            return c

        lax.fori_loop(0, width // step, add, 0)

    def rs_swap_start(l):
        @pl.when(core == 0)
        def _():
            arrived(w_gu.at[l], sgu.at[l])
            if l == 0:
                pl.semaphore_wait(credit.at[swap_again], 2)
            for j in (0, 2, 1, 3):
                src = w_gu.at[l, j, :, theirs]
                add_into(src, g_gu.at[j, :, theirs], FF)
                copy(src, xg.at[j], at_rswap[l] + j, **swap_to(j)).start()
            for j in range(SIDE):
                add_into(w_gu.at[l, j, :, mine], g_gu.at[j, :, mine], FF)

    def rs_z_start(k, l):
        @pl.when(core == k.owner)
        def _():
            if k is not sgu:
                arrived(k.w.at[l], k.at[l])
            if l == 0:
                pl.semaphore_wait(credit.at[k.again_z], 3)
            for d in (2, 1, 3, 0):
                zt = lax.rem(z + d, SIDE)
                part = k.band(l, zt)
                if k is sd:
                    part[...] = (part[...].astype(f32) + k.g[zt].astype(f32)).astype(bf16)
                elif k is sgu:
                    arrived(xg.at[zt], at_rswap[l] + zt)
                    add_into(part, xg.at[zt], FF)
                else:
                    add_into(part, k.g.at[zt], k.width)
                if d:
                    copy(part, k.zr.at[d - 1], k.at[l] + d, shard=z_peer(d)).start()
            if k is sgu and l == 1:
                for j in (0, 2):
                    pl.semaphore_signal(
                        credit.at[swap_again], inc=1, device_id=swap_to(j), device_id_type=MESH
                    )

    def rs_y_start(k, l):
        @pl.when(core == k.owner)
        def _():
            for d in range(1, SIDE):
                arrived(k.zr.at[d - 1], k.at[l] + d)
            if l == 0:
                for d in range(1, SIDE):
                    sent(k.yr.at[0], k.at[1] + 3 + d)
            own = k.band(l, z)
            if k is sd:
                tot = own[...].astype(f32)
                for d in range(3):
                    tot += k.zr[d].astype(f32)
                k.ys[...] = tot.astype(bf16)
            else:
                step = 256 if k.width % 256 == 0 else 128

                def add(t, c):
                    cols = pl.ds(pl.multiple_of(t * step, 128), step)
                    tot = own[:, cols].astype(f32)
                    for d in range(3):
                        tot += k.zr[d, :, cols].astype(f32)
                    for j in range(SIDE):
                        rows = tot[j * ROWS : j * ROWS + ROWS]
                        rows = jnp.concatenate([rows, jnp.zeros((PAD - ROWS, step), f32)], axis=0)
                        k.ys[j, :, cols] = rows.astype(bf16)
                    return c

                lax.fori_loop(0, k.width // step, add, 0)
            if l == 1:
                for d in range(1, SIDE):
                    pl.semaphore_signal(
                        credit.at[k.again_z], inc=1, device_id={"shard": z_peer(d)}, device_id_type=MESH
                    )
            else:
                pl.semaphore_wait(credit.at[k.again_y], 3)
            for d in (2, 1, 3):
                yt = lax.rem(y + d, SIDE)
                copy(k.ys.at[yt], k.yr.at[d - 1], k.at[l] + 3 + d, shard=y_peer(d)).start()

    def x_targets(l):
        for t in (1, 2, 3):
            other = 1 - sec if t >= 2 else sec
            where = {}
            if t >= 2:
                where["section"] = 1 - sec
            if t % 2:
                where["replica"] = far
            yield t, other == l, where

    def rs_x_start(k, l):
        @pl.when(core == k.owner)
        def _():
            for d in range(1, SIDE):
                arrived(k.yr.at[d - 1], k.at[l] + 3 + d)
            if l == 0:
                xs_sent(k, 1)
            tot = k.ys[y].astype(f32)
            for d in range(3):
                tot += k.yr[d].astype(f32)
            k.xs[...] = tot.astype(bf16)
            if l == 1:
                for d in range(1, SIDE):
                    pl.semaphore_signal(
                        credit.at[k.again_y], inc=1, device_id={"shard": y_peer(d)}, device_id_type=MESH
                    )
            for t, hit, where in x_targets(l):
                @pl.when(hit)
                def _():
                    copy(k.xs, k.xr.at[t - 1], k.at[l] + 6 + t, **where).start()

    def xs_sent(k, l):
        for t, hit, where in x_targets(l):
            @pl.when(hit)
            def _():
                sent(k.xs, k.at[l] + 6 + t)

    def write_out(k, tot):
        if k is sd:
            gd_ref[0] = tot
        elif k is sq:
            gq_ref[0] = tot[0:ROWS, 0:576]
            gk_ref[0] = tot[0:ROWS, 576:768]
            gv_ref[0] = tot[0:ROWS, 768:960]
            gain_ref[...] = tot[0:ROWS, 896:1024]
        else:
            go_ref[0] = tot[0:ROWS, 0:D]

    def rs_end_start(k, l):
        @pl.when((core == k.owner) & (sec == l))
        def _():
            for t in (1, 2, 3):
                arrived(k.xr.at[t - 1], k.at[l] + 6 + t)
            if k is sgu:
                own = k.xs[...].astype(f32) + k.xr[0].astype(f32)
                other = k.xr[1].astype(f32) + k.xr[2].astype(f32)
                own_ref, other_ref = (gg_ref, gu_ref) if l == 0 else (gu_ref, gg_ref)
                k.fs[l] = own.astype(bf16)
                k.fs[1 - l] = other.astype(bf16)
                copy(k.fs, k.fr, k.at[l] + 10, replica=sib).start()
                own_ref[0] = own[0:ROWS]
                other_ref[0] = other[0:ROWS]
            else:
                tot = k.xs[...].astype(f32)
                for t in range(3):
                    tot += k.xr[t].astype(f32)
                k.fs[...] = tot.astype(bf16)
                copy(k.fs, k.fr, k.at[l] + 10, replica=sib).start()
                write_out(k, tot)

    def rs_end(k, l):
        @pl.when((core != k.owner) & (sec == l))
        def _():
            arrived(k.fr, k.at[l] + 10)
            if k is sgu:
                gg_ref[0] = k.fr[0, 0:ROWS].astype(f32)
                gu_ref[0] = k.fr[1, 0:ROWS].astype(f32)
            else:
                write_out(k, k.fr[...].astype(f32))

    def rs_sent():
        for k in (sgu, sd, so, sq):
            @pl.when(core == k.owner)
            def _():
                for l in (1, 0):
                    for d in range(1, SIDE):
                        sent(k.zr.at[0], k.at[l] + d)
                    if k is sgu:
                        for j in range(SIDE):
                            sent(xg.at[j], at_rswap[l] + j)

                    @pl.when(sec == l)
                    def _():
                        sent(k.fs, k.at[l] + 10)

                for d in range(1, SIDE):
                    sent(k.yr.at[0], k.at[0] + 3 + d)
                xs_sent(k, 0)

    at_o = [take(1) for _ in range(2)]
    at_d = [take(1) for _ in range(2)]

    def hand_over(l, value, own_ref, send, recv, at):
        @pl.when(sec == l)
        def _():
            own_ref[0, sec, 0] = value

        @pl.when(sec != l)
        def _():
            send[...] = value
            copy(send, recv, at[l], section=1 - sec).start()

    def hand_over_end(own_ref, send, recv, at):
        for l in range(2):
            @pl.when(sec == l)
            def _():
                arrived(recv, at[l])
                own_ref[0, 1 - sec, 0] = recv[...]

            @pl.when(sec != l)
            def _():
                sent(send, at[l])

    x_start(kq)
    x_start(kgu)
    x_start(ko)
    dx_start()
    xs_[0] = x_ref[sec, 0].astype(f32)
    y_start(kq, 0)
    y_start(kgu, 0)
    dz_start(0)
    y_start(ko, 0)
    z_start(kq, 0)
    z_start(kgu, 0)
    z_start(ko, 0)
    dy_start(0)
    y_start(kq, 1)
    y_start(kgu, 1)
    dz_start(1)
    y_start(ko, 1)
    z_end(kq, 0)
    gather_end(kq, 0)
    project_in(0)
    kv_start(0)
    z_end(kgu, 0)
    z_end(ko, 0)
    d_forward_on(0)
    z_start(kq, 1)
    kv_wait(0)
    attend(0, 0)
    swap_end(0)
    z_start(kgu, 1)
    z_start(ko, 1)
    dy_start(1)
    attend(0, 1)
    z_end(kq, 1)
    attend(0, 2)
    gather_end(ko, 0)
    gather_end(kgu, 0)
    d_gather_end(0)
    out = after_attention(0).astype(bf16)
    xs_[1] = out.astype(f32)
    hand_over(0, out, out_ref, osend, orecv, at_o)
    gather_end(kq, 1)
    project_in(1)
    kv_start(1)
    z_end(kgu, 1)
    z_end(ko, 1)
    d_forward_on(1)
    kv_wait(1)
    attend(1, 0)
    attend(1, 1)
    swap_end(1)
    attend(1, 2)
    gather_end(ko, 1)
    gather_end(kgu, 1)
    d_gather_end(1)
    out = after_attention(1).astype(bf16)
    hand_over(1, out, out_ref, osend, orecv, at_o)
    kv_sent(0)
    kv_sent(1)
    gather_sent()

    dmid = ffn_back(1, dy_ref[sec, 0].astype(f32))
    mid_[1] = dmid
    pair_start(sgu, 1)
    pair_start(sd, 1)
    out_back(1, dmid)
    pair_start(so, 1)
    attention_back(1)
    rs_swap_start(1)
    rs_z_start(sd, 1)
    rs_z_start(so, 1)
    dx = finish_back(1, mid_[1])
    pair_start(sq, 1)
    hand_over(1, dx, dx_ref, dsend, drecv, at_d)
    dkv_sent(1)
    rs_z_start(sgu, 1)
    rs_y_start(sd, 1)
    rs_y_start(so, 1)
    pair_sent(sgu, 1)
    pair_sent(sd, 1)
    dmid = ffn_back(0, dx.astype(bf16).astype(f32))
    mid_[0] = dmid
    pair_start(sgu, 0)
    pair_start(sd, 0)
    rs_z_start(sq, 1)
    rs_y_start(sgu, 1)
    rs_x_start(sd, 1)
    rs_x_start(so, 1)
    pair_sent(so, 1)
    out_back(0, mid_[0])
    pair_start(so, 0)
    attention_back(0)
    rs_swap_start(0)
    rs_z_start(sd, 0)
    rs_z_start(so, 0)
    rs_y_start(sq, 1)
    rs_x_start(sgu, 1)
    pair_sent(sq, 1)
    dx = finish_back(0, mid_[0])
    pair_start(sq, 0)
    hand_over(0, dx, dx_ref, dsend, drecv, at_d)
    rs_x_start(sq, 1)
    rs_end_start(sd, 1)
    rs_end_start(so, 1)
    rs_end_start(sgu, 1)
    rs_z_start(sgu, 0)
    rs_z_start(sq, 0)
    rs_end_start(sq, 1)
    rs_y_start(sd, 0)
    rs_y_start(so, 0)
    rs_y_start(sgu, 0)
    rs_y_start(sq, 0)
    for k in (sd, so, sgu, sq):
        rs_end(k, 1)
    for k in (sd, so, sgu, sq):
        rs_x_start(k, 0)
    for k in (sd, so, sgu, sq):
        rs_end_start(k, 0)
    for k in (sd, so, sgu, sq):
        rs_end(k, 0)
    for k in (sd, so, sgu, sq):
        pair_sent(k, 0)
    dkv_sent(0)
    rs_sent()
    hand_over_end(out_ref, osend, orecv, at_o)
    hand_over_end(dx_ref, dsend, drecv, at_d)
    assert used[0] <= SEMS, used[0]


SEMS = 400


def scratch():
    v = lambda *shape: pltpu.VMEM(shape, bf16)
    w = lambda *shape: pltpu.VMEM(shape, f32)
    widths = (FF, QKV, OUT)
    return [
        *[v(2, SIDE, PAD, n) for n in widths],
        *[v(2, SIDE, BAND, n) for n in (GU, QKV, OUT)], v(2, SIDE, SIDE, FROWS, D),
        v(2, SHARDS * TOK, 384), v(2, SHARDS - 1, TOK, 384),
        w(GROUP, SHARDS * TOK), w(GROUP, 128), w(GROUP, 128),
        w(2, TOK, D), v(2, TOK, D), v(2, HEADS, TOK, 64), v(2, HEADS, TOK, 64),
        w(2, KV_HEADS, GROUP, 1), w(2, TOK, D), v(2, TOK, D), w(2, TOK, GU),
        v(TOK, D), v(HEADS, TOK, 64), w(KV_HEADS, GROUP, 1), w(HEADS, TOK, 64), w(TOK, 384),
        w(TOK, D), v(TOK, D),
        *[v(SIDE, BAND, n) for n in (GU, QKV, OUT)], v(SIDE, SIDE, FROWS, D), v(SIDE, BAND, FF),
        *[v(3, BAND, n) for n in widths], v(3, SIDE, FROWS, D),
        *[v(SIDE, PAD, n) for n in widths], v(SIDE, FROWS, D),
        *[v(3, PAD, n) for n in widths], v(3, FROWS, D),
        *[v(PAD, n) for n in widths], v(FROWS, D),
        *[v(3, PAD, n) for n in widths], v(3, FROWS, D),
        v(2, PAD, FF), v(PAD, QKV), v(PAD, OUT), v(FROWS, D),
        v(2, PAD, FF), v(PAD, QKV), v(PAD, OUT), v(FROWS, D),
        v(TOK, D), v(TOK, D), w(TOK, D), w(TOK, D),
        pltpu.SemaphoreType.DMA((SEMS,)), pltpu.SemaphoreType.DMA((SEMS,)),
        pltpu.SemaphoreType.REGULAR((32,)),
    ]


def kernel(*refs):
    body(*refs)


def local(
    inputs, out_grad, w_query, w_key, w_value, w_out, w_gate, w_up, w_down, gain_attn, gain_ffn
):
    shard_index = lax.axis_index("shard")
    positions = shard_index * TOK + jnp.arange(TOK, dtype=jnp.int32)
    half = HEAD_DIM // 2
    inverse = rope_base ** (-(jnp.arange(half, dtype=f32) * 2.0 / HEAD_DIM))
    angles = positions.astype(f32)[:, None] * inverse[None, :]
    cos, sin = jnp.cos(angles), jnp.sin(angles)
    cos = jnp.concatenate([cos] * 4, axis=1)
    sin = jnp.concatenate([-sin, sin, -sin, sin], axis=1)
    more = ((0, PAD - ROWS), (0, 0))
    p0 = jnp.pad(jnp.concatenate([w_gate[0], w_up[0]], axis=1), more)
    gain_cols = jnp.stack([gain_attn[0], gain_ffn[0]], axis=1)
    pq = jnp.concatenate(
        [w_query[0], w_key[0], w_value[0], gain_cols, jnp.zeros((ROWS, 62), bf16)], axis=1
    )
    pq = jnp.pad(pq, more)
    po = jnp.pad(w_out[0], ((0, PAD - ROWS), (0, OUT - D)))
    whole = pl.BlockSpec(memory_space=pltpu.VMEM)
    shapes = (
        ((1, 2, 1, TOK, D), bf16), ((1, 2, 1, TOK, D), f32),
        ((1, ROWS, 576), f32), ((1, ROWS, 192), f32), ((1, ROWS, 192), f32), ((1, ROWS, 576), f32),
        ((1, ROWS, FF), f32), ((1, ROWS, FF), f32), ((1, FROWS, D), f32), ((ROWS, 128), f32),
    )
    res = pl.pallas_call(
        kernel,
        out_shape=[jax.ShapeDtypeStruct(s, t) for s, t in shapes],
        in_specs=[whole] * 8,
        out_specs=[whole] * len(shapes),
        scratch_shapes=scratch(),
        compiler_params=pltpu.CompilerParams(
            collective_id=0, has_side_effects=True, vmem_limit_bytes=63 * 1024 * 1024
        ),
        name="two_layers",
    )(inputs, out_grad, p0, pq, po, w_down[0], cos, sin)
    out, dx, gq, gk, gv, go, gg, gu, gd, gain = res
    return (out, dx, gq, gk, gv, go, gg, gu, gd, gain[:, 64][None], gain[:, 65][None])


def solution(mesh):
    return jax.shard_map(
        local,
        mesh=mesh,
        in_specs=(
            P(None, "replica", "shard", None),
            P(None, "replica", "shard", None),
            P("section", "shard", None),
            P("section", "shard", None),
            P("section", "shard", None),
            P("section", "shard", None),
            P("section", "shard", None),
            P("section", "shard", None),
            P("section", "shard", None),
            P("section", "shard"),
            P("section", "shard"),
        ),
        out_specs=(
            P("section", None, "replica", "shard", None),
            P("section", None, "replica", "shard", None),
            P("section", "shard", None),
            P("section", "shard", None),
            P("section", "shard", None),
            P("section", "shard", None),
            P("section", "shard", None),
            P("section", "shard", None),
            P("section", "shard", None),
            P("section", "shard"),
            P("section", "shard"),
        ),
        check_vma=False,
    )
```

```python
import functools

import jax
import jax.numpy as jnp
from jax import lax
from jax.experimental import pallas as pl
from jax.experimental.pallas import tpu as pltpu
from jax.sharding import PartitionSpec as P

HEADS = 9
KV_HEADS = 3
HEAD_DIM = 64
D = 576
FF = 1536
TOK = 128
SHARDS = 16
SIDE = 4
ROWS = 36
PAD = 48
BAND = SIDE * ROWS
FROWS = 96
FBAND = SIDE * FROWS
GU = 2 * FF
QKV = 1024
OUT = 640
CHUNK = 512
GROUP = 3 * TOK

bf16 = jnp.bfloat16
f32 = jnp.float32
MESH = pl.DeviceIdType.MESH
epsilon = 1e-05
rope_base = 100000.0
score_scale = 0.125


def dot(a, b):
    return lax.dot_general(a, b, (((1,), (0,)), ((), ())), preferred_element_type=f32)


def dot_nt(a, b):
    return lax.dot_general(a, b, (((1,), (1,)), ((), ())), preferred_element_type=f32)


def dot_tn(a, b):
    return lax.dot_general(a, b, (((0,), (0,)), ((), ())), preferred_element_type=f32)


def factor_of(v):
    return lax.rsqrt(jnp.mean(v * v, axis=-1, keepdims=True) + epsilon)


def norm_back(v, r, gain, up):
    scaled = gain * up
    return r * scaled - v * (r * r * r) * jnp.mean(scaled * v, axis=-1, keepdims=True)


def half_swap(u):
    width = u.shape[1]
    lane = lax.broadcasted_iota(jnp.int32, u.shape, 1)
    first = lax.rem(lane, HEAD_DIM) < HEAD_DIM // 2
    return jnp.where(first, pltpu.roll(u, width - 32, 1), pltpu.roll(u, 32, 1))


def body(
    x_ref, dy_ref, p0_ref, pq_ref, po_ref, pd_ref, cos_ref, sin_ref,
    out_ref, dx_ref, gq_ref, gk_ref, gv_ref, go_ref, gg_ref, gu_ref, gd_ref, gain_ref,
    stage_gu, stage_q, stage_o, w_gu, w_q, w_o, w_d, kv, dkv_r, scr, mx, acc,
    xs_, a_, q8_, o_, lse_, mid_, bn_, gu_,
    dyb_, dob_, delta_, dq_, dkv_acc, acc2, gain_term,
    g_gu, g_q, g_o, g_d, xg,
    zr_gu, zr_q, zr_o, zr_d, ys_gu, ys_q, ys_o, ys_d, yr_gu, yr_q, yr_o, yr_d,
    xs_gu, xs_q, xs_o, xs_d, xr_gu, xr_q, xr_o, xr_d, fs_gu, fs_q, fs_o, fs_d, fr_gu, fr_q, fr_o, fr_d,
    osend, orecv, dsend, drecv,
    ssem, rsem, credit,
):
    sec = lax.axis_index("section")
    sh = lax.axis_index("shard")
    rep = lax.axis_index("replica")
    z, y = lax.div(sh, SIDE), lax.rem(sh, SIDE)
    core = lax.rem(rep, 2)
    sib = rep + 1 - 2 * core
    far = lax.rem(rep + 2, 4)
    used = [0]

    def take(n):
        at = used[0]
        used[0] += n
        return at

    def copy(src, dst, at, to=None, **dev):
        return pltpu.make_async_remote_copy(
            src_ref=src, dst_ref=dst, send_sem=ssem.at[at], recv_sem=rsem.at[at if to is None else to],
            device_id=dev, device_id_type=MESH,
        )

    def arrived(dst, at):
        copy(dst, dst, at, shard=sh).wait_recv()

    def sent(src, at):
        copy(src, src, at, shard=sh).wait_send()

    def y_peer(d):
        return z * SIDE + lax.rem(y + d, SIDE)

    def z_peer(d):
        return lax.rem(z + d, SIDE) * SIDE + y

    def z_from(d):
        return lax.rem(z + SIDE - d, SIDE)

    def y_from(d):
        return lax.rem(y + SIDE - d, SIDE)

    last = pl.ds(pl.multiple_of(lax.div(sh, SIDE) * CHUNK, CHUNK), CHUNK)
    for l in range(2):
        kv[l, last, :] = jnp.zeros((CHUNK, 384), bf16)
    barrier = pltpu.get_barrier_semaphore()

    def greet(d, c):
        pl.semaphore_signal(barrier, inc=1, device_id={"shard": lax.rem(sh + d, SHARDS)}, device_id_type=MESH)
        return c

    lax.fori_loop(1, SHARDS, greet, 0)
    pl.semaphore_signal(barrier, inc=1, device_id={"replica": sib}, device_id_type=MESH)
    pl.semaphore_signal(barrier, inc=1, device_id={"replica": far}, device_id_type=MESH)
    pl.semaphore_signal(barrier, inc=1, device_id={"section": 1 - sec}, device_id_type=MESH)
    pl.semaphore_signal(barrier, inc=1, device_id={"section": 1 - sec, "replica": far}, device_id_type=MESH)
    pl.semaphore_wait(barrier, SHARDS - 1 + 4)

    mine = pl.ds(pl.multiple_of(sec * FF, 128), FF)
    theirs = pl.ds(pl.multiple_of((1 - sec) * FF, 128), FF)

    class Gather:
        def __init__(self, owner, send, keep, stage, w, cols, width):
            self.owner, self.send, self.keep, self.stage, self.w, self.width = owner, send, keep, stage, w, width
            self.cols = cols
            self.at_x = take(1)
            self.at_y = [take(3) for _ in range(2)]
            self.at_z = [take(3) for _ in range(2)]
            self.at_f = [take(4) for _ in range(2)]

        def band(self, l, j):
            return self.w.at[l, j, :, self.cols]

    kgu = Gather(0, p0_ref.at[:, theirs], p0_ref.at[:, mine], stage_gu, w_gu, mine, FF)
    kq = Gather(1, pq_ref, pq_ref, stage_q, w_q, pl.ds(0, QKV), QKV)
    ko = Gather(1, po_ref, po_ref, stage_o, w_o, pl.ds(0, OUT), OUT)
    at_xd = take(1)
    at_dz = [take(3) for _ in range(2)]
    at_dy = [take(3) for _ in range(2)]
    at_df = [take(1) for _ in range(2)]
    at_swap = [take(4) for _ in range(2)]
    at_sf = [take(4) for _ in range(2)]

    def x_start(k):
        @pl.when(core == k.owner)
        def _():
            copy(k.send, k.stage.at[sec, y], k.at_x, section=1 - sec).start()
            k.stage[sec, y] = k.keep[...]

    def dx_start():
        @pl.when(core == 1)
        def _():
            copy(pd_ref, w_d.at[sec, z, y], at_xd, section=1 - sec).start()
            w_d[sec, z, y] = pd_ref[...]

    def y_start(k, l):
        @pl.when(core == k.owner)
        def _():
            own = k.stage.at[l, y]

            @pl.when(sec != l)
            def _():
                arrived(own, k.at_x)

            for d in (2, 1, 3):
                copy(own, own, k.at_y[l] + d - 1, shard=y_peer(d)).start()

    def dz_start(l):
        @pl.when(core == 1)
        def _():
            own = w_d.at[l, z, y]

            @pl.when(sec != l)
            def _():
                arrived(own, at_xd)

            for d in (2, 1, 3):
                copy(own, own, at_dz[l] + d - 1, shard=z_peer(d)).start()

    def z_start(k, l):
        @pl.when(core == k.owner)
        def _():
            for d in range(1, SIDE):
                arrived(k.stage.at[l, y_from(d)], k.at_y[l] + d - 1)
            own = k.band(l, z)
            for at in range(0, k.width, 128):
                parts = [k.stage[l, j, :, at : at + 128][0:ROWS].astype(f32) for j in range(SIDE)]
                own[:, at : at + 128] = jnp.concatenate(parts, axis=0).astype(bf16)
            for d in (2, 1, 3):
                copy(own, own, k.at_z[l] + d - 1, shard=z_peer(d)).start()
            copy(own, own, k.at_f[l], replica=sib).start()

    def dy_start(l):
        @pl.when(core == 1)
        def _():
            for d in range(1, SIDE):
                arrived(w_d.at[l, z_from(d), y], at_dz[l] + d - 1)
            own = w_d.at[l, :, y]
            for d in (2, 1, 3):
                copy(own, own, at_dy[l] + d - 1, shard=y_peer(d)).start()

    def z_end(k, l):
        @pl.when(core == k.owner)
        def _():
            for d in (1, 3, 2):
                got = k.band(l, z_from(d))
                arrived(got, k.at_z[l] + d - 1)
                copy(got, got, k.at_f[l] + d, replica=sib).start()
            if k is kgu:
                for j in range(SIDE):
                    got = k.band(l, j)
                    copy(got, got, at_swap[l] + j, **swap_to(j)).start()

    def swap_to(j):
        return {"section": 1 - sec} if j < 2 else {"section": 1 - sec, "replica": far}

    def swap_end(l):
        @pl.when(core == 0)
        def _():
            for j in range(SIDE):
                got = w_gu.at[l, j, :, theirs]
                arrived(got, at_swap[l] + j)
                copy(got, got, at_sf[l] + j, replica=sib).start()

    def d_forward_on(l):
        @pl.when(core == 1)
        def _():
            for d in range(1, SIDE):
                arrived(w_d.at[l, :, y_from(d)], at_dy[l] + d - 1)
            copy(w_d.at[l], w_d.at[l], at_df[l], replica=sib).start()

    def gather_end(k, l):
        @pl.when(core != k.owner)
        def _():
            arrived(k.band(l, z), k.at_f[l])
            for d in range(1, SIDE):
                arrived(k.band(l, z_from(d)), k.at_f[l] + d)
            if k is kgu:
                for j in range(SIDE):
                    arrived(w_gu.at[l, j, :, theirs], at_sf[l] + j)

    def d_gather_end(l):
        @pl.when(core == 0)
        def _():
            arrived(w_d.at[l], at_df[l])

    def gather_sent():
        for l in range(2):
            for k in (kgu, kq, ko):
                @pl.when(core == k.owner)
                def _():
                    @pl.when(sec == l)
                    def _():
                        sent(k.send, k.at_x)

                    for d in range(1, SIDE):
                        sent(k.stage.at[l, y], k.at_y[l] + d - 1)
                        sent(k.band(l, z), k.at_z[l] + d - 1)
                        sent(k.band(l, z), k.at_f[l] + d)
                    sent(k.band(l, z), k.at_f[l])
                    if k is kgu:
                        for j in range(SIDE):
                            sent(k.band(l, j), at_swap[l] + j)
                            sent(k.band(l, j), at_sf[l] + j)

            @pl.when(core == 1)
            def _():
                @pl.when(sec == l)
                def _():
                    sent(pd_ref, at_xd)

                for d in range(1, SIDE):
                    sent(w_d.at[l, z, y], at_dz[l] + d - 1)
                    sent(w_d.at[l, :, y], at_dy[l] + d - 1)
                sent(w_d.at[l], at_df[l])

    at_kv = [take(SHARDS) for _ in range(2)]
    at_kvr = [take(4) for _ in range(2)]
    at_dkv = [take(SHARDS) for _ in range(2)]
    at_dky = [take(4) for _ in range(2)]
    tokens = pl.ds(pl.multiple_of(sh * TOK, TOK), TOK)
    twice = 2 * SIDE

    def block(l, j):
        return kv.at[l, pl.ds(pl.multiple_of(j * TOK, TOK), TOK)]

    def relayed(j):
        gap = lax.div(j, SIDE) - z
        return ((gap == 2) | (gap == -2)) & (lax.rem(j, SIDE) != y)

    def kv_start(l):
        own = kv.at[l, tokens]

        def go(d, c):
            @pl.when(jnp.logical_not(relayed(sh + d)))
            def _():
                copy(own, own, at_kv[l] + d, shard=sh + d).start()

            return c

        lax.fori_loop(1, SHARDS - sh, go, 0)

    def kv_wait(l):
        @pl.when(z >= 2)
        def _():
            passing = block(l, sh - twice)
            arrived(passing, at_kv[l] + twice)
            for e in range(1, SIDE):
                yt = lax.rem(y + e, SIDE)
                copy(passing, passing, at_kvr[l] + e, to=at_kv[l] + twice + yt - y, shard=y_peer(e)).start()

        def go(d, c):
            @pl.when(d != twice)
            def _():
                arrived(block(l, sh - d), at_kv[l] + d)

            return c

        lax.fori_loop(1, sh + 1, go, 0)

    def kv_sent(l):
        def go(d, c):
            @pl.when(jnp.logical_not(relayed(sh + d)))
            def _():
                sent(kv.at[l, tokens], at_kv[l] + d)

            return c

        lax.fori_loop(1, SHARDS - sh, go, 0)

        @pl.when(z >= 2)
        def _():
            for e in range(1, SIDE):
                sent(kv.at[l, tokens], at_kvr[l] + e)

    def dkv_start(l, j):
        away = relayed(j)

        @pl.when(away)
        def _():
            e = lax.rem(lax.rem(j, SIDE) - y + SIDE, SIDE)
            copy(
                block(l, j), dkv_r.at[l, twice - 1 + e], at_dkv[l] + sh - j,
                to=at_dky[l] + e, shard=z * SIDE + lax.rem(j, SIDE),
            ).start()

        @pl.when(jnp.logical_not(away) & (sh - j != twice))
        def _():
            copy(block(l, j), dkv_r.at[l, sh - j - 1], at_dkv[l] + sh - j, shard=j).start()

    def dkv_relay(l):
        @pl.when(z >= 2)
        def _():
            passing = block(l, sh - twice)
            for e in range(1, SIDE):
                arrived(dkv_r.at[l, twice - 1 + e], at_dky[l] + e)
            tot = passing[...].astype(f32)
            for e in range(1, SIDE):
                tot += dkv_r[l, twice - 1 + e].astype(f32)
            passing[...] = tot.astype(bf16)
            copy(passing, dkv_r.at[l, twice - 1], at_dkv[l] + twice, shard=sh - twice).start()

    def dkv_sent(l):
        def go(d, c):
            sent(kv.at[l, pl.ds(0, TOK)], at_dkv[l] + d)
            return c

        lax.fori_loop(1, sh + 1, go, 0)

    def gains(l):
        tile = w_q[l, :, :, 896:1024].reshape(D, 128)
        row = lax.broadcasted_iota(jnp.int32, (8, 128), 0)
        lane = lax.broadcasted_iota(jnp.int32, (8, 128), 1)
        pick = jnp.where(lane == row + 64, 1.0, 0.0).astype(bf16)
        both = dot_nt(pick, tile)
        return both[0:1], both[1:2]

    nfull = lax.div(sh, SIDE)

    def causal():
        row = lax.broadcasted_iota(jnp.int32, (GROUP, CHUNK), 0)
        col = lax.broadcasted_iota(jnp.int32, (GROUP, CHUNK), 1)
        return col <= lax.rem(sh, SIDE) * TOK + lax.rem(row, TOK)

    def keys_at(c):
        return pl.ds(pl.multiple_of(c * CHUNK, CHUNK), CHUNK)

    def tables():
        cos = jnp.concatenate([cos_ref[...]] * 6, axis=1)
        sin = jnp.concatenate([sin_ref[...]] * 6, axis=1)
        return cos, sin

    def project_in(l):
        x = xs_[l]
        gain, _ = gains(l)
        a = (x * factor_of(x) * gain).astype(bf16)
        a_[l] = a
        qkv = dot(a, w_q[l].reshape(D, QKV))
        cos, sin = tables()
        u = qkv[:, 0:768]
        turned = u * cos + half_swap(u) * sin
        for h in range(HEADS):
            head = turned[:, h * 64 : h * 64 + 64].astype(bf16)
            q8_[l, h] = (head.astype(f32) * score_scale).astype(bf16)
        block = jnp.concatenate([turned[:, 576:768], qkv[:, 768:960]], axis=1).astype(bf16)
        kv[l, tokens] = block

    def attend(l, g):
        if True:
            q = q8_[l, 3 * g : 3 * g + 3].reshape(GROUP, 64)

            def keep(c, s):
                scr[:, keys_at(c)] = s
                top = jnp.maximum(
                    jnp.maximum(s[:, 0:128], s[:, 128:256]), jnp.maximum(s[:, 256:384], s[:, 384:512])
                )
                mx[...] = jnp.maximum(mx[...], top)

            def scores(c):
                k = kv[l, keys_at(c), :][:, g * 64 : g * 64 + 64]
                return dot_nt(q, k)

            mx[...] = jnp.full_like(mx, -1e30)

            def first(c, carry):
                keep(c, scores(c))
                return carry

            lax.fori_loop(0, nfull, first, 0)
            keep(nfull, jnp.where(causal(), scores(nfull), -1e30))
            peak = jnp.max(mx[...], axis=1, keepdims=True)
            acc[...] = jnp.zeros_like(acc)

            def second(c, carry):
                p = jnp.exp(scr[:, keys_at(c)] - peak).astype(bf16)
                v = kv[l, keys_at(c), :][:, 192 + g * 64 : 256 + g * 64]
                v = jnp.concatenate([v, jnp.ones_like(v)], axis=1)
                acc[...] += dot(p, v)
                return carry

            lax.fori_loop(0, nfull + 1, second, 0)
            total = acc[:, 64:65]
            mixed = (acc[:, 0:64] / total).astype(bf16)
            lse_[l, g] = peak + jnp.log(total)
            o_[l, 3 * g : 3 * g + 3] = mixed.reshape(3, TOK, 64)

    def heads_in(ref):
        return jnp.concatenate([ref[h] for h in range(HEADS)], axis=1)

    def after_attention(l):
        o = heads_in(o_.at[l])
        mid = xs_[l] + dot(o, w_o[l, :, :, 0:D].reshape(D, D))
        mid_[l] = mid
        _, gain = gains(l)
        bn_[l] = (mid * factor_of(mid) * gain).astype(bf16)
        acc2[...] = mid

        def tile(t, c):
            gcols = pl.ds(pl.multiple_of(t * FBAND, 128), FBAND)
            ucols = pl.ds(pl.multiple_of(FF + t * FBAND, 128), FBAND)
            bn = bn_[l]
            gt = dot(bn, w_gu[l, :, :, gcols].reshape(D, FBAND))
            up = dot(bn, w_gu[l, :, :, ucols].reshape(D, FBAND))
            gu_[l, :, gcols] = gt
            gu_[l, :, ucols] = up
            hid = (gt * jax.nn.sigmoid(gt) * up).astype(bf16)
            acc2[...] += dot(hid, w_d[l, t].reshape(FBAND, D))
            return c

        lax.fori_loop(0, SIDE, tile, 0)
        return acc2[...]

    def ffn_back(l, dy):
        dyb_[...] = dy.astype(bf16)
        acc2[...] = jnp.zeros_like(acc2)

        def tile(t, c):
            gcols = pl.ds(pl.multiple_of(t * FBAND, 128), FBAND)
            ucols = pl.ds(pl.multiple_of(FF + t * FBAND, 128), FBAND)
            dyb = dyb_[...]
            bn = bn_[l]
            wd = w_d[l, t].reshape(FBAND, D)
            dhid = dot_nt(dyb, wd).astype(bf16).astype(f32)
            gt, up = gu_[l, :, gcols], gu_[l, :, ucols]
            s = jax.nn.sigmoid(gt)
            hid = (gt * s * up).astype(bf16)
            g_d[t] = dot_tn(hid, dyb).astype(bf16).reshape(SIDE, FROWS, D)
            dgt = (dhid * up * s * (1.0 + gt * (1.0 - s))).astype(bf16)
            dup = (dhid * gt * s).astype(bf16)
            g_gu[:, :, gcols] = dot_tn(bn, dgt).astype(bf16).reshape(SIDE, BAND, FBAND)
            g_gu[:, :, ucols] = dot_tn(bn, dup).astype(bf16).reshape(SIDE, BAND, FBAND)
            acc2[...] += dot_nt(dgt, w_gu[l, :, :, gcols].reshape(D, FBAND))
            acc2[...] += dot_nt(dup, w_gu[l, :, :, ucols].reshape(D, FBAND))
            return c

        lax.fori_loop(0, SIDE, tile, 0)
        dbn = acc2[...]
        mid = mid_[l]
        r = factor_of(mid)
        _, gain = gains(l)
        gain_term[...] = (dbn * mid * r).astype(bf16)
        return dy + norm_back(mid, r, gain, dbn)

    def out_back(l, dmid):
        dmb = dmid.astype(bf16)
        o = heads_in(o_.at[l])
        g_o[...] = jnp.concatenate(
            [dot_tn(o, dmb), jnp.zeros((D, 64), f32)], axis=1
        ).astype(bf16).reshape(SIDE, BAND, 640)
        dob = dot_nt(dmb, w_o[l, :, :, 0:D].reshape(D, D)).astype(bf16)
        for h in range(HEADS):
            do_h = dob[:, h * 64 : h * 64 + 64]
            dq_[h] = jnp.zeros((TOK, 64), f32)
            dob_[h] = do_h

    def attention_back(l):
        for g in range(KV_HEADS):
            do = dob_[3 * g : 3 * g + 3].reshape(GROUP, 64).astype(f32)
            og = o_[l, 3 * g : 3 * g + 3].reshape(GROUP, 64).astype(f32)
            delta_[g] = jnp.sum(do * og, axis=1, keepdims=True)

        def chunk(c, masked):
            kvb = kv[l, keys_at(c), :]
            dks, dvs = [], []
            for g in range(KV_HEADS):
                q = q8_[l, 3 * g : 3 * g + 3].reshape(GROUP, 64)
                do = dob_[3 * g : 3 * g + 3].reshape(GROUP, 64)
                k = kvb[:, g * 64 : g * 64 + 64]
                v = kvb[:, 192 + g * 64 : 256 + g * 64]
                s = dot_nt(q, k)
                if masked:
                    s = jnp.where(causal(), s, -1e30)
                p = jnp.exp(s - lse_[l, g])
                ds = (p * (dot_nt(do, v) - delta_[g])).astype(bf16)
                dq_[3 * g : 3 * g + 3] += dot(ds, k).reshape(3, TOK, 64)
                dks.append(dot_tn(ds, q))
                dvs.append(dot_tn(p.astype(bf16), do))
            kv[l, keys_at(c), :] = jnp.concatenate(dks + dvs, axis=1).astype(bf16)

        def full(c, carry):
            chunk(c, False)
            for i in range(SIDE):
                dkv_start(l, c * SIDE + i)
            return carry

        lax.fori_loop(0, nfull, full, 0)
        chunk(nfull, True)

        def rest(j, carry):
            dkv_start(l, j)
            return carry

        lax.fori_loop(nfull * SIDE, sh, rest, 0)

    def finish_back(l, dmid_at):
        dkv_acc[...] = kv[l, tokens, :].astype(f32)

        def add(d, c):
            @pl.when(jnp.logical_not(relayed(sh + d)))
            def _():
                arrived(dkv_r.at[l, d - 1], at_dkv[l] + d)
                dkv_acc[...] += dkv_r[l, d - 1].astype(f32)

            return c

        lax.fori_loop(1, SHARDS - sh, add, 0)
        dkv = dkv_acc[...]
        cos, sin = tables()
        dq = jnp.concatenate([dq_[h] for h in range(HEADS)], axis=1) * score_scale
        u = jnp.concatenate([dq, dkv[:, 0:192]], axis=1)
        back = u * cos - half_swap(u) * sin
        dqkv = jnp.concatenate([back, dkv[:, 192:384], jnp.zeros((TOK, 64), f32)], axis=1).astype(bf16)
        a = a_[l]
        gq = dot_tn(a, dqkv)
        da = dot_nt(dqkv, w_q[l].reshape(D, QKV))
        x = xs_[l]
        r = factor_of(x)
        gain, _ = gains(l)
        lane = lax.broadcasted_iota(jnp.int32, (TOK, 128), 1)
        e0 = jnp.where(lane == 64, 1.0, 0.0).astype(bf16)
        e1 = jnp.where(lane == 65, 1.0, 0.0).astype(bf16)
        cols = dot_tn((da * x * r).astype(bf16), e0) + dot_tn(gain_term[...], e1)
        g_q[:, :, 0:896] = gq[:, 0:896].astype(bf16).reshape(SIDE, BAND, 896)
        g_q[:, :, 896:1024] = (gq[:, 896:1024] + cols).astype(bf16).reshape(SIDE, BAND, 128)
        return dmid_at + norm_back(x, r, gain, da)

    class Sum:
        def __init__(self, name, owner, w, cols, g, zr, ys, yr, xs, xr, fs, fr, width):
            self.name, self.owner, self.w, self.cols, self.g = name, owner, w, cols, g
            self.zr, self.ys, self.yr, self.xs, self.xr, self.fs, self.fr = zr, ys, yr, xs, xr, fs, fr
            self.width = width
            self.at = [take(12) for _ in range(2)]
            self.free = credits(2)
            self.again_z, self.again_y = credits(1), credits(1)

        def band(self, l, j):
            return self.w.at[l, j] if self.name == "d" else self.w.at[l, j, :, self.cols]

    granted = [0]

    def credits(n):
        at = granted[0]
        granted[0] += n
        return at

    sgu = Sum("gu", 0, w_gu, mine, g_gu, zr_gu, ys_gu, yr_gu, xs_gu, xr_gu, fs_gu, fr_gu, FF)
    sq = Sum("q", 1, w_q, pl.ds(0, QKV), g_q, zr_q, ys_q, yr_q, xs_q, xr_q, fs_q, fr_q, QKV)
    so = Sum("o", 1, w_o, pl.ds(0, OUT), g_o, zr_o, ys_o, yr_o, xs_o, xr_o, fs_o, fr_o, OUT)
    sd = Sum("d", 1, w_d, None, g_d, zr_d, ys_d, yr_d, xs_d, xr_d, fs_d, fr_d, D)
    at_rswap = [take(4) for _ in range(2)]
    swap_again = credits(1)

    def pair_start(k, l):
        pl.semaphore_signal(credit.at[k.free + l], inc=1, device_id={"replica": sib}, device_id_type=MESH)
        pl.semaphore_wait(credit.at[k.free + l], 1)

        @pl.when(core != k.owner)
        def _():
            copy(k.g, k.w.at[l], k.at[l], replica=sib).start()

    def pair_sent(k, l):
        @pl.when(core != k.owner)
        def _():
            sent(k.g, k.at[l])

    def add_into(dst, src, width):
        step = 256 if width % 256 == 0 else 128

        def add(t, c):
            cols = pl.ds(pl.multiple_of(t * step, 128), step)
            dst[:, cols] = (dst[:, cols].astype(f32) + src[:, cols].astype(f32)).astype(bf16)
            return c

        lax.fori_loop(0, width // step, add, 0)

    def rs_swap_start(l):
        @pl.when(core == 0)
        def _():
            arrived(w_gu.at[l], sgu.at[l])
            if l == 0:
                pl.semaphore_wait(credit.at[swap_again], 2)
            for j in (0, 2, 1, 3):
                src = w_gu.at[l, j, :, theirs]
                add_into(src, g_gu.at[j, :, theirs], FF)
                copy(src, xg.at[j], at_rswap[l] + j, **swap_to(j)).start()
            for j in range(SIDE):
                add_into(w_gu.at[l, j, :, mine], g_gu.at[j, :, mine], FF)

    def rs_z_start(k, l):
        @pl.when(core == k.owner)
        def _():
            if k is not sgu:
                arrived(k.w.at[l], k.at[l])
            if l == 0:
                pl.semaphore_wait(credit.at[k.again_z], 3)
            for d in (2, 1, 3, 0):
                zt = lax.rem(z + d, SIDE)
                part = k.band(l, zt)
                if k is sd:
                    part[...] = (part[...].astype(f32) + k.g[zt].astype(f32)).astype(bf16)
                elif k is sgu:
                    arrived(xg.at[zt], at_rswap[l] + zt)
                    add_into(part, xg.at[zt], FF)
                else:
                    add_into(part, k.g.at[zt], k.width)
                if d:
                    copy(part, k.zr.at[d - 1], k.at[l] + d, shard=z_peer(d)).start()
            if k is sgu and l == 1:
                for j in (0, 2):
                    pl.semaphore_signal(
                        credit.at[swap_again], inc=1, device_id=swap_to(j), device_id_type=MESH
                    )

    def rs_y_start(k, l):
        @pl.when(core == k.owner)
        def _():
            for d in range(1, SIDE):
                arrived(k.zr.at[d - 1], k.at[l] + d)
            if l == 0:
                for d in range(1, SIDE):
                    sent(k.yr.at[0], k.at[1] + 3 + d)
            own = k.band(l, z)
            if k is sd:
                tot = own[...].astype(f32)
                for d in range(3):
                    tot += k.zr[d].astype(f32)
                k.ys[...] = tot.astype(bf16)
            else:
                step = 256 if k.width % 256 == 0 else 128

                def add(t, c):
                    cols = pl.ds(pl.multiple_of(t * step, 128), step)
                    tot = own[:, cols].astype(f32)
                    for d in range(3):
                        tot += k.zr[d, :, cols].astype(f32)
                    for j in range(SIDE):
                        rows = tot[j * ROWS : j * ROWS + ROWS]
                        rows = jnp.concatenate([rows, jnp.zeros((PAD - ROWS, step), f32)], axis=0)
                        k.ys[j, :, cols] = rows.astype(bf16)
                    return c

                lax.fori_loop(0, k.width // step, add, 0)
            if l == 1:
                for d in range(1, SIDE):
                    pl.semaphore_signal(
                        credit.at[k.again_z], inc=1, device_id={"shard": z_peer(d)}, device_id_type=MESH
                    )
            else:
                pl.semaphore_wait(credit.at[k.again_y], 3)
            for d in (2, 1, 3):
                yt = lax.rem(y + d, SIDE)
                copy(k.ys.at[yt], k.yr.at[d - 1], k.at[l] + 3 + d, shard=y_peer(d)).start()

    def x_targets(l):
        for t in (1, 2, 3):
            other = 1 - sec if t >= 2 else sec
            where = {}
            if t >= 2:
                where["section"] = 1 - sec
            if t % 2:
                where["replica"] = far
            yield t, other == l, where

    def rs_x_start(k, l):
        @pl.when(core == k.owner)
        def _():
            for d in range(1, SIDE):
                arrived(k.yr.at[d - 1], k.at[l] + 3 + d)
            if l == 0:
                xs_sent(k, 1)
            tot = k.ys[y].astype(f32)
            for d in range(3):
                tot += k.yr[d].astype(f32)
            k.xs[...] = tot.astype(bf16)
            if l == 1:
                for d in range(1, SIDE):
                    pl.semaphore_signal(
                        credit.at[k.again_y], inc=1, device_id={"shard": y_peer(d)}, device_id_type=MESH
                    )
            for t, hit, where in x_targets(l):
                @pl.when(hit)
                def _():
                    copy(k.xs, k.xr.at[t - 1], k.at[l] + 6 + t, **where).start()

    def xs_sent(k, l):
        for t, hit, where in x_targets(l):
            @pl.when(hit)
            def _():
                sent(k.xs, k.at[l] + 6 + t)

    def write_out(k, tot):
        if k is sd:
            gd_ref[0] = tot
        elif k is sq:
            gq_ref[0] = tot[0:ROWS, 0:576]
            gk_ref[0] = tot[0:ROWS, 576:768]
            gv_ref[0] = tot[0:ROWS, 768:960]
            gain_ref[...] = tot[0:ROWS, 896:1024]
        else:
            go_ref[0] = tot[0:ROWS, 0:D]

    def rs_end_start(k, l):
        @pl.when((core == k.owner) & (sec == l))
        def _():
            for t in (1, 2, 3):
                arrived(k.xr.at[t - 1], k.at[l] + 6 + t)
            if k is sgu:
                own = k.xs[...].astype(f32) + k.xr[0].astype(f32)
                other = k.xr[1].astype(f32) + k.xr[2].astype(f32)
                own_ref, other_ref = (gg_ref, gu_ref) if l == 0 else (gu_ref, gg_ref)
                k.fs[l] = own.astype(bf16)
                k.fs[1 - l] = other.astype(bf16)
                copy(k.fs, k.fr, k.at[l] + 10, replica=sib).start()
                own_ref[0] = own[0:ROWS]
                other_ref[0] = other[0:ROWS]
            else:
                tot = k.xs[...].astype(f32)
                for t in range(3):
                    tot += k.xr[t].astype(f32)
                k.fs[...] = tot.astype(bf16)
                copy(k.fs, k.fr, k.at[l] + 10, replica=sib).start()
                write_out(k, tot)

    def rs_end(k, l):
        @pl.when((core != k.owner) & (sec == l))
        def _():
            arrived(k.fr, k.at[l] + 10)
            if k is sgu:
                gg_ref[0] = k.fr[0, 0:ROWS].astype(f32)
                gu_ref[0] = k.fr[1, 0:ROWS].astype(f32)
            else:
                write_out(k, k.fr[...].astype(f32))

    def rs_sent():
        for k in (sgu, sd, so, sq):
            @pl.when(core == k.owner)
            def _():
                for l in (1, 0):
                    for d in range(1, SIDE):
                        sent(k.zr.at[0], k.at[l] + d)
                    if k is sgu:
                        for j in range(SIDE):
                            sent(xg.at[j], at_rswap[l] + j)

                    @pl.when(sec == l)
                    def _():
                        sent(k.fs, k.at[l] + 10)

                for d in range(1, SIDE):
                    sent(k.yr.at[0], k.at[0] + 3 + d)
                xs_sent(k, 0)

    at_o = [take(1) for _ in range(2)]
    at_d = [take(1) for _ in range(2)]

    def hand_over(l, value, own_ref, send, recv, at):
        @pl.when(sec == l)
        def _():
            own_ref[0, sec, 0] = value

        @pl.when(sec != l)
        def _():
            send[...] = value
            copy(send, recv, at[l], section=1 - sec).start()

    def hand_over_end(own_ref, send, recv, at):
        for l in range(2):
            @pl.when(sec == l)
            def _():
                arrived(recv, at[l])
                own_ref[0, 1 - sec, 0] = recv[...]

            @pl.when(sec != l)
            def _():
                sent(send, at[l])

    x_start(kq)
    x_start(kgu)
    x_start(ko)
    dx_start()
    xs_[0] = x_ref[sec, 0].astype(f32)
    y_start(kq, 0)
    y_start(kgu, 0)
    dz_start(0)
    y_start(ko, 0)
    z_start(kq, 0)
    z_start(kgu, 0)
    z_start(ko, 0)
    dy_start(0)
    y_start(kq, 1)
    y_start(kgu, 1)
    dz_start(1)
    y_start(ko, 1)
    z_end(kq, 0)
    gather_end(kq, 0)
    project_in(0)
    kv_start(0)
    z_end(kgu, 0)
    z_end(ko, 0)
    d_forward_on(0)
    z_start(kq, 1)
    kv_wait(0)
    attend(0, 0)
    swap_end(0)
    z_start(kgu, 1)
    z_start(ko, 1)
    dy_start(1)
    attend(0, 1)
    z_end(kq, 1)
    attend(0, 2)
    gather_end(ko, 0)
    gather_end(kgu, 0)
    d_gather_end(0)
    out = after_attention(0).astype(bf16)
    xs_[1] = out.astype(f32)
    hand_over(0, out, out_ref, osend, orecv, at_o)
    gather_end(kq, 1)
    project_in(1)
    kv_start(1)
    z_end(kgu, 1)
    z_end(ko, 1)
    d_forward_on(1)
    kv_wait(1)
    attend(1, 0)
    attend(1, 1)
    swap_end(1)
    attend(1, 2)
    gather_end(ko, 1)
    gather_end(kgu, 1)
    d_gather_end(1)
    out = after_attention(1).astype(bf16)
    hand_over(1, out, out_ref, osend, orecv, at_o)
    kv_sent(0)
    kv_sent(1)
    gather_sent()

    dmid = ffn_back(1, dy_ref[sec, 0].astype(f32))
    mid_[1] = dmid
    pair_start(sgu, 1)
    pair_start(sd, 1)
    out_back(1, dmid)
    pair_start(so, 1)
    attention_back(1)
    dkv_relay(1)
    rs_swap_start(1)
    rs_z_start(sd, 1)
    rs_z_start(so, 1)
    dx = finish_back(1, mid_[1])
    pair_start(sq, 1)
    hand_over(1, dx, dx_ref, dsend, drecv, at_d)
    dkv_sent(1)
    rs_z_start(sgu, 1)
    rs_y_start(sd, 1)
    rs_y_start(so, 1)
    pair_sent(sgu, 1)
    pair_sent(sd, 1)
    dmid = ffn_back(0, dx.astype(bf16).astype(f32))
    mid_[0] = dmid
    pair_start(sgu, 0)
    pair_start(sd, 0)
    rs_z_start(sq, 1)
    rs_y_start(sgu, 1)
    rs_x_start(sd, 1)
    rs_x_start(so, 1)
    pair_sent(so, 1)
    out_back(0, mid_[0])
    pair_start(so, 0)
    attention_back(0)
    dkv_relay(0)
    rs_swap_start(0)
    rs_z_start(sd, 0)
    rs_z_start(so, 0)
    rs_y_start(sq, 1)
    rs_x_start(sgu, 1)
    pair_sent(sq, 1)
    dx = finish_back(0, mid_[0])
    pair_start(sq, 0)
    hand_over(0, dx, dx_ref, dsend, drecv, at_d)
    rs_x_start(sq, 1)
    rs_end_start(sd, 1)
    rs_end_start(so, 1)
    rs_end_start(sgu, 1)
    rs_z_start(sgu, 0)
    rs_z_start(sq, 0)
    rs_end_start(sq, 1)
    rs_y_start(sd, 0)
    rs_y_start(so, 0)
    rs_y_start(sgu, 0)
    rs_y_start(sq, 0)
    for k in (sd, so, sgu, sq):
        rs_end(k, 1)
    for k in (sd, so, sgu, sq):
        rs_x_start(k, 0)
    for k in (sd, so, sgu, sq):
        rs_end_start(k, 0)
    for k in (sd, so, sgu, sq):
        rs_end(k, 0)
    for k in (sd, so, sgu, sq):
        pair_sent(k, 0)
    dkv_sent(0)
    rs_sent()
    hand_over_end(out_ref, osend, orecv, at_o)
    hand_over_end(dx_ref, dsend, drecv, at_d)
    assert used[0] <= SEMS, used[0]


SEMS = 400


def scratch():
    v = lambda *shape: pltpu.VMEM(shape, bf16)
    w = lambda *shape: pltpu.VMEM(shape, f32)
    widths = (FF, QKV, OUT)
    return [
        *[v(2, SIDE, PAD, n) for n in widths],
        *[v(2, SIDE, BAND, n) for n in (GU, QKV, OUT)], v(2, SIDE, SIDE, FROWS, D),
        v(2, SHARDS * TOK, 384), v(2, SHARDS - 1, TOK, 384),
        w(GROUP, SHARDS * TOK), w(GROUP, 128), w(GROUP, 128),
        w(2, TOK, D), v(2, TOK, D), v(2, HEADS, TOK, 64), v(2, HEADS, TOK, 64),
        w(2, KV_HEADS, GROUP, 1), w(2, TOK, D), v(2, TOK, D), w(2, TOK, GU),
        v(TOK, D), v(HEADS, TOK, 64), w(KV_HEADS, GROUP, 1), w(HEADS, TOK, 64), w(TOK, 384),
        w(TOK, D), v(TOK, D),
        *[v(SIDE, BAND, n) for n in (GU, QKV, OUT)], v(SIDE, SIDE, FROWS, D), v(SIDE, BAND, FF),
        *[v(3, BAND, n) for n in widths], v(3, SIDE, FROWS, D),
        *[v(SIDE, PAD, n) for n in widths], v(SIDE, FROWS, D),
        *[v(3, PAD, n) for n in widths], v(3, FROWS, D),
        *[v(PAD, n) for n in widths], v(FROWS, D),
        *[v(3, PAD, n) for n in widths], v(3, FROWS, D),
        v(2, PAD, FF), v(PAD, QKV), v(PAD, OUT), v(FROWS, D),
        v(2, PAD, FF), v(PAD, QKV), v(PAD, OUT), v(FROWS, D),
        v(TOK, D), v(TOK, D), w(TOK, D), w(TOK, D),
        pltpu.SemaphoreType.DMA((SEMS,)), pltpu.SemaphoreType.DMA((SEMS,)),
        pltpu.SemaphoreType.REGULAR((32,)),
    ]


def kernel(*refs):
    body(*refs)


def local(
    inputs, out_grad, w_query, w_key, w_value, w_out, w_gate, w_up, w_down, gain_attn, gain_ffn
):
    shard_index = lax.axis_index("shard")
    positions = shard_index * TOK + jnp.arange(TOK, dtype=jnp.int32)
    half = HEAD_DIM // 2
    inverse = rope_base ** (-(jnp.arange(half, dtype=f32) * 2.0 / HEAD_DIM))
    angles = positions.astype(f32)[:, None] * inverse[None, :]
    cos, sin = jnp.cos(angles), jnp.sin(angles)
    cos = jnp.concatenate([cos] * 4, axis=1)
    sin = jnp.concatenate([-sin, sin, -sin, sin], axis=1)
    more = ((0, PAD - ROWS), (0, 0))
    p0 = jnp.pad(jnp.concatenate([w_gate[0], w_up[0]], axis=1), more)
    gain_cols = jnp.stack([gain_attn[0], gain_ffn[0]], axis=1)
    pq = jnp.concatenate(
        [w_query[0], w_key[0], w_value[0], gain_cols, jnp.zeros((ROWS, 62), bf16)], axis=1
    )
    pq = jnp.pad(pq, more)
    po = jnp.pad(w_out[0], ((0, PAD - ROWS), (0, OUT - D)))
    whole = pl.BlockSpec(memory_space=pltpu.VMEM)
    shapes = (
        ((1, 2, 1, TOK, D), bf16), ((1, 2, 1, TOK, D), f32),
        ((1, ROWS, 576), f32), ((1, ROWS, 192), f32), ((1, ROWS, 192), f32), ((1, ROWS, 576), f32),
        ((1, ROWS, FF), f32), ((1, ROWS, FF), f32), ((1, FROWS, D), f32), ((ROWS, 128), f32),
    )
    res = pl.pallas_call(
        kernel,
        out_shape=[jax.ShapeDtypeStruct(s, t) for s, t in shapes],
        in_specs=[whole] * 8,
        out_specs=[whole] * len(shapes),
        scratch_shapes=scratch(),
        compiler_params=pltpu.CompilerParams(
            collective_id=0, has_side_effects=True, vmem_limit_bytes=63 * 1024 * 1024
        ),
        name="two_layers",
    )(inputs, out_grad, p0, pq, po, w_down[0], cos, sin)
    out, dx, gq, gk, gv, go, gg, gu, gd, gain = res
    return (out, dx, gq, gk, gv, go, gg, gu, gd, gain[:, 64][None], gain[:, 65][None])


def solution(mesh):
    return jax.shard_map(
        local,
        mesh=mesh,
        in_specs=(
            P(None, "replica", "shard", None),
            P(None, "replica", "shard", None),
            P("section", "shard", None),
            P("section", "shard", None),
            P("section", "shard", None),
            P("section", "shard", None),
            P("section", "shard", None),
            P("section", "shard", None),
            P("section", "shard", None),
            P("section", "shard"),
            P("section", "shard"),
        ),
        out_specs=(
            P("section", None, "replica", "shard", None),
            P("section", None, "replica", "shard", None),
            P("section", "shard", None),
            P("section", "shard", None),
            P("section", "shard", None),
            P("section", "shard", None),
            P("section", "shard", None),
            P("section", "shard", None),
            P("section", "shard", None),
            P("section", "shard"),
            P("section", "shard"),
        ),
        check_vma=False,
    )
```

```python
import functools

import jax
import jax.numpy as jnp
from jax import lax
from jax.experimental import pallas as pl
from jax.experimental.pallas import tpu as pltpu
from jax.sharding import PartitionSpec as P

HEADS = 9
KV_HEADS = 3
HEAD_DIM = 64
D = 576
FF = 1536
TOK = 128
SHARDS = 16
SIDE = 4
ROWS = 36
PAD = 48
BAND = SIDE * ROWS
FROWS = 96
FBAND = SIDE * FROWS
GU = 2 * FF
QKV = 1024
OUT = 640
CHUNK = 512
GROUP = 3 * TOK

bf16 = jnp.bfloat16
f32 = jnp.float32
MESH = pl.DeviceIdType.MESH
epsilon = 1e-05
rope_base = 100000.0
score_scale = 0.125


def dot(a, b):
    return lax.dot_general(a, b, (((1,), (0,)), ((), ())), preferred_element_type=f32)


def dot_nt(a, b):
    return lax.dot_general(a, b, (((1,), (1,)), ((), ())), preferred_element_type=f32)


def dot_tn(a, b):
    return lax.dot_general(a, b, (((0,), (0,)), ((), ())), preferred_element_type=f32)


def factor_of(v):
    return lax.rsqrt(jnp.mean(v * v, axis=-1, keepdims=True) + epsilon)


def norm_back(v, r, gain, up):
    scaled = gain * up
    return r * scaled - v * (r * r * r) * jnp.mean(scaled * v, axis=-1, keepdims=True)


def half_swap(u):
    width = u.shape[1]
    lane = lax.broadcasted_iota(jnp.int32, u.shape, 1)
    first = lax.rem(lane, HEAD_DIM) < HEAD_DIM // 2
    return jnp.where(first, pltpu.roll(u, width - 32, 1), pltpu.roll(u, 32, 1))


def body(
    x_ref, dy_ref, p0_ref, pq_ref, po_ref, pd_ref, cos_ref, sin_ref,
    out_ref, dx_ref, gq_ref, gk_ref, gv_ref, go_ref, gg_ref, gu_ref, gd_ref, gain_ref,
    stage_gu, stage_q, stage_o, w_gu, w_q, w_o, w_d, kv, dkv_r, scr, mx, acc,
    xs_, a_, q8_, o_, lse_, mid_, bn_, gu_,
    dyb_, dob_, delta_, dq_, dkv_acc, acc2, gain_term,
    g_gu, g_q, g_o, g_d, xg,
    zr_gu, zr_q, zr_o, zr_d, ys_gu, ys_q, ys_o, ys_d, yr_gu, yr_q, yr_o, yr_d,
    xs_gu, xs_q, xs_o, xs_d, xr_gu, xr_q, xr_o, xr_d, fs_gu, fs_q, fs_o, fs_d, fr_gu, fr_q, fr_o, fr_d,
    osend, orecv, dsend, drecv,
    ssem, rsem, credit,
):
    sec = lax.axis_index("section")
    sh = lax.axis_index("shard")
    rep = lax.axis_index("replica")
    z, y = lax.div(sh, SIDE), lax.rem(sh, SIDE)
    core = lax.rem(rep, 2)
    sib = rep + 1 - 2 * core
    far = lax.rem(rep + 2, 4)
    used = [0]

    def take(n):
        at = used[0]
        used[0] += n
        return at

    def copy(src, dst, at, to=None, **dev):
        return pltpu.make_async_remote_copy(
            src_ref=src, dst_ref=dst, send_sem=ssem.at[at], recv_sem=rsem.at[at if to is None else to],
            device_id=dev, device_id_type=MESH,
        )

    def arrived(dst, at):
        copy(dst, dst, at, shard=sh).wait_recv()

    def sent(src, at):
        copy(src, src, at, shard=sh).wait_send()

    def y_peer(d):
        return z * SIDE + lax.rem(y + d, SIDE)

    def z_peer(d):
        return lax.rem(z + d, SIDE) * SIDE + y

    def z_from(d):
        return lax.rem(z + SIDE - d, SIDE)

    def y_from(d):
        return lax.rem(y + SIDE - d, SIDE)

    last = pl.ds(pl.multiple_of(lax.div(sh, SIDE) * CHUNK, CHUNK), CHUNK)
    for l in range(2):
        kv[l, last, :] = jnp.zeros((CHUNK, 384), bf16)
    barrier = pltpu.get_barrier_semaphore()

    def greet(d, c):
        pl.semaphore_signal(barrier, inc=1, device_id={"shard": lax.rem(sh + d, SHARDS)}, device_id_type=MESH)
        return c

    lax.fori_loop(1, SHARDS, greet, 0)
    pl.semaphore_signal(barrier, inc=1, device_id={"replica": sib}, device_id_type=MESH)
    pl.semaphore_signal(barrier, inc=1, device_id={"replica": far}, device_id_type=MESH)
    pl.semaphore_signal(barrier, inc=1, device_id={"section": 1 - sec}, device_id_type=MESH)
    pl.semaphore_signal(barrier, inc=1, device_id={"section": 1 - sec, "replica": far}, device_id_type=MESH)
    pl.semaphore_wait(barrier, SHARDS - 1 + 4)

    mine = pl.ds(pl.multiple_of(sec * FF, 128), FF)
    theirs = pl.ds(pl.multiple_of((1 - sec) * FF, 128), FF)

    class Gather:
        def __init__(self, owner, send, keep, stage, w, cols, width):
            self.owner, self.send, self.keep, self.stage, self.w, self.width = owner, send, keep, stage, w, width
            self.cols = cols
            self.at_x = take(1)
            self.at_y = [take(3) for _ in range(2)]
            self.at_z = [take(3) for _ in range(2)]
            self.at_f = [take(4) for _ in range(2)]

        def band(self, l, j):
            return self.w.at[l, j, :, self.cols]

    kgu = Gather(0, p0_ref.at[:, theirs], p0_ref.at[:, mine], stage_gu, w_gu, mine, FF)
    kq = Gather(1, pq_ref, pq_ref, stage_q, w_q, pl.ds(0, QKV), QKV)
    ko = Gather(1, po_ref, po_ref, stage_o, w_o, pl.ds(0, OUT), OUT)
    at_xd = take(1)
    at_dz = [take(3) for _ in range(2)]
    at_dy = [take(3) for _ in range(2)]
    at_df = [take(1) for _ in range(2)]
    at_swap = [take(4) for _ in range(2)]
    at_sf = [take(4) for _ in range(2)]

    def x_start(k):
        @pl.when(core == k.owner)
        def _():
            copy(k.send, k.stage.at[sec, y], k.at_x, section=1 - sec).start()
            k.stage[sec, y] = k.keep[...]

    def dx_start():
        @pl.when(core == 1)
        def _():
            copy(pd_ref, w_d.at[sec, z, y], at_xd, section=1 - sec).start()
            w_d[sec, z, y] = pd_ref[...]

    def y_start(k, l):
        @pl.when(core == k.owner)
        def _():
            own = k.stage.at[l, y]

            @pl.when(sec != l)
            def _():
                arrived(own, k.at_x)

            for d in (2, 1, 3):
                copy(own, own, k.at_y[l] + d - 1, shard=y_peer(d)).start()

    def dz_start(l):
        @pl.when(core == 1)
        def _():
            own = w_d.at[l, z, y]

            @pl.when(sec != l)
            def _():
                arrived(own, at_xd)

            for d in (2, 1, 3):
                copy(own, own, at_dz[l] + d - 1, shard=z_peer(d)).start()

    def z_start(k, l):
        @pl.when(core == k.owner)
        def _():
            for d in range(1, SIDE):
                arrived(k.stage.at[l, y_from(d)], k.at_y[l] + d - 1)
            own = k.band(l, z)
            for at in range(0, k.width, 128):
                parts = [k.stage[l, j, :, at : at + 128][0:ROWS].astype(f32) for j in range(SIDE)]
                own[:, at : at + 128] = jnp.concatenate(parts, axis=0).astype(bf16)
            for d in (2, 1, 3):
                copy(own, own, k.at_z[l] + d - 1, shard=z_peer(d)).start()
            copy(own, own, k.at_f[l], replica=sib).start()

    def dy_start(l):
        @pl.when(core == 1)
        def _():
            for d in range(1, SIDE):
                arrived(w_d.at[l, z_from(d), y], at_dz[l] + d - 1)
            own = w_d.at[l, :, y]
            for d in (2, 1, 3):
                copy(own, own, at_dy[l] + d - 1, shard=y_peer(d)).start()

    def z_end(k, l):
        @pl.when(core == k.owner)
        def _():
            for d in (1, 3, 2):
                got = k.band(l, z_from(d))
                arrived(got, k.at_z[l] + d - 1)
                copy(got, got, k.at_f[l] + d, replica=sib).start()
            if k is kgu:
                for j in range(SIDE):
                    got = k.band(l, j)
                    copy(got, got, at_swap[l] + j, **swap_to(j)).start()

    def swap_to(j):
        return {"section": 1 - sec} if j < 2 else {"section": 1 - sec, "replica": far}

    def swap_end(l):
        @pl.when(core == 0)
        def _():
            for j in range(SIDE):
                got = w_gu.at[l, j, :, theirs]
                arrived(got, at_swap[l] + j)
                copy(got, got, at_sf[l] + j, replica=sib).start()

    def d_forward_on(l):
        @pl.when(core == 1)
        def _():
            for d in range(1, SIDE):
                arrived(w_d.at[l, :, y_from(d)], at_dy[l] + d - 1)
            copy(w_d.at[l], w_d.at[l], at_df[l], replica=sib).start()

    def gather_end(k, l):
        @pl.when(core != k.owner)
        def _():
            arrived(k.band(l, z), k.at_f[l])
            for d in range(1, SIDE):
                arrived(k.band(l, z_from(d)), k.at_f[l] + d)
            if k is kgu:
                for j in range(SIDE):
                    arrived(w_gu.at[l, j, :, theirs], at_sf[l] + j)

    def d_gather_end(l):
        @pl.when(core == 0)
        def _():
            arrived(w_d.at[l], at_df[l])

    def gather_sent():
        for l in range(2):
            for k in (kgu, kq, ko):
                @pl.when(core == k.owner)
                def _():
                    @pl.when(sec == l)
                    def _():
                        sent(k.send, k.at_x)

                    for d in range(1, SIDE):
                        sent(k.stage.at[l, y], k.at_y[l] + d - 1)
                        sent(k.band(l, z), k.at_z[l] + d - 1)
                        sent(k.band(l, z), k.at_f[l] + d)
                    sent(k.band(l, z), k.at_f[l])
                    if k is kgu:
                        for j in range(SIDE):
                            sent(k.band(l, j), at_swap[l] + j)
                            sent(k.band(l, j), at_sf[l] + j)

            @pl.when(core == 1)
            def _():
                @pl.when(sec == l)
                def _():
                    sent(pd_ref, at_xd)

                for d in range(1, SIDE):
                    sent(w_d.at[l, z, y], at_dz[l] + d - 1)
                    sent(w_d.at[l, :, y], at_dy[l] + d - 1)
                sent(w_d.at[l], at_df[l])

    at_kv = [take(SHARDS) for _ in range(2)]
    at_kvr = [take(4) for _ in range(2)]
    at_dkv = [take(SHARDS) for _ in range(2)]
    at_dky = [take(4) for _ in range(2)]
    tokens = pl.ds(pl.multiple_of(sh * TOK, TOK), TOK)
    twice = 2 * SIDE

    def block(l, j):
        return kv.at[l, pl.ds(pl.multiple_of(j * TOK, TOK), TOK)]

    def relayed(j):
        gap = lax.div(j, SIDE) - z
        return ((gap == 2) | (gap == -2)) & (lax.rem(j, SIDE) != y)

    def kv_start(l):
        own = kv.at[l, tokens]

        def go(d, c):
            @pl.when(jnp.logical_not(relayed(sh + d)))
            def _():
                copy(own, own, at_kv[l] + d, shard=sh + d).start()

            return c

        lax.fori_loop(1, SHARDS - sh, go, 0)

    def kv_wait(l):
        @pl.when(z >= 2)
        def _():
            passing = block(l, sh - twice)
            arrived(passing, at_kv[l] + twice)
            for e in range(1, SIDE):
                yt = lax.rem(y + e, SIDE)
                copy(passing, passing, at_kvr[l] + e, to=at_kv[l] + twice + yt - y, shard=y_peer(e)).start()

        def go(d, c):
            @pl.when(d != twice)
            def _():
                arrived(block(l, sh - d), at_kv[l] + d)

            return c

        lax.fori_loop(1, sh + 1, go, 0)

    def kv_sent(l):
        def go(d, c):
            @pl.when(jnp.logical_not(relayed(sh + d)))
            def _():
                sent(kv.at[l, tokens], at_kv[l] + d)

            return c

        lax.fori_loop(1, SHARDS - sh, go, 0)

        @pl.when(z >= 2)
        def _():
            for e in range(1, SIDE):
                sent(kv.at[l, tokens], at_kvr[l] + e)

    def dkv_start(l, j):
        away = relayed(j)

        @pl.when(away)
        def _():
            e = lax.rem(lax.rem(j, SIDE) - y + SIDE, SIDE)
            copy(
                block(l, j), dkv_r.at[l, twice - 1 + e], at_dkv[l] + sh - j,
                to=at_dky[l] + e, shard=z * SIDE + lax.rem(j, SIDE),
            ).start()

        @pl.when(jnp.logical_not(away) & (sh - j != twice))
        def _():
            copy(block(l, j), dkv_r.at[l, sh - j - 1], at_dkv[l] + sh - j, shard=j).start()

    def dkv_relay(l):
        @pl.when(z >= 2)
        def _():
            passing = block(l, sh - twice)
            for e in range(1, SIDE):
                arrived(dkv_r.at[l, twice - 1 + e], at_dky[l] + e)
            tot = passing[...].astype(f32)
            for e in range(1, SIDE):
                tot += dkv_r[l, twice - 1 + e].astype(f32)
            passing[...] = tot.astype(bf16)
            copy(passing, dkv_r.at[l, twice - 1], at_dkv[l] + twice, shard=sh - twice).start()

    def dkv_sent(l):
        def go(d, c):
            sent(kv.at[l, pl.ds(0, TOK)], at_dkv[l] + d)
            return c

        lax.fori_loop(1, sh + 1, go, 0)

    def gains(l):
        tile = w_q[l, :, :, 896:1024].reshape(D, 128)
        row = lax.broadcasted_iota(jnp.int32, (8, 128), 0)
        lane = lax.broadcasted_iota(jnp.int32, (8, 128), 1)
        pick = jnp.where(lane == row + 64, 1.0, 0.0).astype(bf16)
        both = dot_nt(pick, tile)
        return both[0:1], both[1:2]

    nfull = lax.div(sh, SIDE)

    def causal():
        row = lax.broadcasted_iota(jnp.int32, (GROUP, CHUNK), 0)
        col = lax.broadcasted_iota(jnp.int32, (GROUP, CHUNK), 1)
        return col <= lax.rem(sh, SIDE) * TOK + lax.rem(row, TOK)

    def keys_at(c):
        return pl.ds(pl.multiple_of(c * CHUNK, CHUNK), CHUNK)

    def tables():
        cos = jnp.concatenate([cos_ref[...]] * 6, axis=1)
        sin = jnp.concatenate([sin_ref[...]] * 6, axis=1)
        return cos, sin

    def project_in(l):
        x = xs_[l]
        gain, _ = gains(l)
        a = (x * factor_of(x) * gain).astype(bf16)
        a_[l] = a
        qkv = dot(a, w_q[l].reshape(D, QKV))
        cos, sin = tables()
        u = qkv[:, 0:768]
        turned = u * cos + half_swap(u) * sin
        for h in range(HEADS):
            head = turned[:, h * 64 : h * 64 + 64].astype(bf16)
            q8_[l, h] = (head.astype(f32) * score_scale).astype(bf16)
        block = jnp.concatenate([turned[:, 576:768], qkv[:, 768:960]], axis=1).astype(bf16)
        kv[l, tokens] = block

    def attend(l, g):
        if True:
            q = q8_[l, 3 * g : 3 * g + 3].reshape(GROUP, 64)

            def keep(c, s):
                scr[:, keys_at(c)] = s
                top = jnp.maximum(
                    jnp.maximum(s[:, 0:128], s[:, 128:256]), jnp.maximum(s[:, 256:384], s[:, 384:512])
                )
                mx[...] = jnp.maximum(mx[...], top)

            def scores(c):
                k = kv[l, keys_at(c), :][:, g * 64 : g * 64 + 64]
                return dot_nt(q, k)

            mx[...] = jnp.full_like(mx, -1e30)

            def first(c, carry):
                keep(c, scores(c))
                return carry

            lax.fori_loop(0, nfull, first, 0)
            keep(nfull, jnp.where(causal(), scores(nfull), -1e30))
            peak = jnp.max(mx[...], axis=1, keepdims=True)
            acc[...] = jnp.zeros_like(acc)

            def second(c, carry):
                p = jnp.exp(scr[:, keys_at(c)] - peak).astype(bf16)
                v = kv[l, keys_at(c), :][:, 192 + g * 64 : 256 + g * 64]
                v = jnp.concatenate([v, jnp.ones_like(v)], axis=1)
                acc[...] += dot(p, v)
                return carry

            lax.fori_loop(0, nfull + 1, second, 0)
            total = acc[:, 64:65]
            mixed = (acc[:, 0:64] / total).astype(bf16)
            lse_[l, g] = peak + jnp.log(total)
            o_[l, 3 * g : 3 * g + 3] = mixed.reshape(3, TOK, 64)

    def heads_in(ref):
        return jnp.concatenate([ref[h] for h in range(HEADS)], axis=1)

    def after_attention(l):
        o = heads_in(o_.at[l])
        mid = xs_[l] + dot(o, w_o[l, :, :, 0:D].reshape(D, D))
        mid_[l] = mid
        _, gain = gains(l)
        bn_[l] = (mid * factor_of(mid) * gain).astype(bf16)
        acc2[...] = mid

        def tile(t, c):
            gcols = pl.ds(pl.multiple_of(t * FBAND, 128), FBAND)
            ucols = pl.ds(pl.multiple_of(FF + t * FBAND, 128), FBAND)
            bn = bn_[l]
            gt = dot(bn, w_gu[l, :, :, gcols].reshape(D, FBAND))
            up = dot(bn, w_gu[l, :, :, ucols].reshape(D, FBAND))
            gu_[l, :, gcols] = gt
            gu_[l, :, ucols] = up
            hid = (gt * jax.nn.sigmoid(gt) * up).astype(bf16)
            acc2[...] += dot(hid, w_d[l, t].reshape(FBAND, D))
            return c

        lax.fori_loop(0, SIDE, tile, 0)
        return acc2[...]

    def ffn_back(l, dy):
        dyb_[...] = dy.astype(bf16)
        acc2[...] = jnp.zeros_like(acc2)

        def tile(t, c):
            gcols = pl.ds(pl.multiple_of(t * FBAND, 128), FBAND)
            ucols = pl.ds(pl.multiple_of(FF + t * FBAND, 128), FBAND)
            dyb = dyb_[...]
            bn = bn_[l]
            wd = w_d[l, t].reshape(FBAND, D)
            dhid = dot_nt(dyb, wd).astype(bf16).astype(f32)
            gt, up = gu_[l, :, gcols], gu_[l, :, ucols]
            s = jax.nn.sigmoid(gt)
            hid = (gt * s * up).astype(bf16)
            g_d[t] = dot_tn(hid, dyb).astype(bf16).reshape(SIDE, FROWS, D)
            dgt = (dhid * up * s * (1.0 + gt * (1.0 - s))).astype(bf16)
            dup = (dhid * gt * s).astype(bf16)
            g_gu[:, :, gcols] = dot_tn(bn, dgt).astype(bf16).reshape(SIDE, BAND, FBAND)
            g_gu[:, :, ucols] = dot_tn(bn, dup).astype(bf16).reshape(SIDE, BAND, FBAND)
            acc2[...] += dot_nt(dgt, w_gu[l, :, :, gcols].reshape(D, FBAND))
            acc2[...] += dot_nt(dup, w_gu[l, :, :, ucols].reshape(D, FBAND))
            return c

        lax.fori_loop(0, SIDE, tile, 0)
        dbn = acc2[...]
        mid = mid_[l]
        r = factor_of(mid)
        _, gain = gains(l)
        gain_term[...] = (dbn * mid * r).astype(bf16)
        return dy + norm_back(mid, r, gain, dbn)

    def out_back(l, dmid):
        dmb = dmid.astype(bf16)
        o = heads_in(o_.at[l])
        g_o[...] = jnp.concatenate(
            [dot_tn(o, dmb), jnp.zeros((D, 64), f32)], axis=1
        ).astype(bf16).reshape(SIDE, BAND, 640)
        dob = dot_nt(dmb, w_o[l, :, :, 0:D].reshape(D, D)).astype(bf16)
        for h in range(HEADS):
            do_h = dob[:, h * 64 : h * 64 + 64]
            dq_[h] = jnp.zeros((TOK, 64), f32)
            dob_[h] = do_h

    def attention_back(l, part):
        for g in range(KV_HEADS):
            do = dob_[3 * g : 3 * g + 3].reshape(GROUP, 64).astype(f32)
            og = o_[l, 3 * g : 3 * g + 3].reshape(GROUP, 64).astype(f32)
            delta_[g] = jnp.sum(do * og, axis=1, keepdims=True)

        def chunk(c, masked):
            kvb = kv[l, keys_at(c), :]
            dks, dvs = [], []
            for g in range(KV_HEADS):
                q = q8_[l, 3 * g : 3 * g + 3].reshape(GROUP, 64)
                do = dob_[3 * g : 3 * g + 3].reshape(GROUP, 64)
                k = kvb[:, g * 64 : g * 64 + 64]
                v = kvb[:, 192 + g * 64 : 256 + g * 64]
                s = dot_nt(q, k)
                if masked:
                    s = jnp.where(causal(), s, -1e30)
                p = jnp.exp(s - lse_[l, g])
                ds = (p * (dot_nt(do, v) - delta_[g])).astype(bf16)
                dq_[3 * g : 3 * g + 3] += dot(ds, k).reshape(3, TOK, 64)
                dks.append(dot_tn(ds, q))
                dvs.append(dot_tn(p.astype(bf16), do))
            kv[l, keys_at(c), :] = jnp.concatenate(dks + dvs, axis=1).astype(bf16)

        def full(c, carry):
            chunk(c, False)
            for i in range(SIDE):
                dkv_start(l, c * SIDE + i)
            return carry

        def rest(j, carry):
            dkv_start(l, j)
            return carry

        if part == 0:
            lax.fori_loop(0, nfull, full, 0)
        else:
            chunk(nfull, True)
            lax.fori_loop(nfull * SIDE, sh, rest, 0)

    def finish_back(l, dmid_at):
        dkv_acc[...] = kv[l, tokens, :].astype(f32)

        def add(d, c):
            @pl.when(jnp.logical_not(relayed(sh + d)))
            def _():
                arrived(dkv_r.at[l, d - 1], at_dkv[l] + d)
                dkv_acc[...] += dkv_r[l, d - 1].astype(f32)

            return c

        lax.fori_loop(1, SHARDS - sh, add, 0)
        dkv = dkv_acc[...]
        cos, sin = tables()
        dq = jnp.concatenate([dq_[h] for h in range(HEADS)], axis=1) * score_scale
        u = jnp.concatenate([dq, dkv[:, 0:192]], axis=1)
        back = u * cos - half_swap(u) * sin
        dqkv = jnp.concatenate([back, dkv[:, 192:384], jnp.zeros((TOK, 64), f32)], axis=1).astype(bf16)
        a = a_[l]
        gq = dot_tn(a, dqkv)
        da = dot_nt(dqkv, w_q[l].reshape(D, QKV))
        x = xs_[l]
        r = factor_of(x)
        gain, _ = gains(l)
        lane = lax.broadcasted_iota(jnp.int32, (TOK, 128), 1)
        e0 = jnp.where(lane == 64, 1.0, 0.0).astype(bf16)
        e1 = jnp.where(lane == 65, 1.0, 0.0).astype(bf16)
        cols = dot_tn((da * x * r).astype(bf16), e0) + dot_tn(gain_term[...], e1)
        g_q[:, :, 0:896] = gq[:, 0:896].astype(bf16).reshape(SIDE, BAND, 896)
        g_q[:, :, 896:1024] = (gq[:, 896:1024] + cols).astype(bf16).reshape(SIDE, BAND, 128)
        return dmid_at + norm_back(x, r, gain, da)

    class Sum:
        def __init__(self, name, owner, w, cols, g, zr, ys, yr, xs, xr, fs, fr, width):
            self.name, self.owner, self.w, self.cols, self.g = name, owner, w, cols, g
            self.zr, self.ys, self.yr, self.xs, self.xr, self.fs, self.fr = zr, ys, yr, xs, xr, fs, fr
            self.width = width
            self.at = [take(12) for _ in range(2)]
            self.free = credits(2)
            self.again_z, self.again_y = credits(1), credits(1)

            first_y = name == "d"
            self.i1, self.peer1 = (y, y_peer) if first_y else (z, z_peer)
            self.i2, self.peer2 = (z, z_peer) if first_y else (y, y_peer)

        def band(self, l, j):
            return self.w.at[l, :, j] if self.name == "d" else self.w.at[l, j, :, self.cols]

    granted = [0]

    def credits(n):
        at = granted[0]
        granted[0] += n
        return at

    sgu = Sum("gu", 0, w_gu, mine, g_gu, zr_gu, ys_gu, yr_gu, xs_gu, xr_gu, fs_gu, fr_gu, FF)
    sq = Sum("q", 1, w_q, pl.ds(0, QKV), g_q, zr_q, ys_q, yr_q, xs_q, xr_q, fs_q, fr_q, QKV)
    so = Sum("o", 1, w_o, pl.ds(0, OUT), g_o, zr_o, ys_o, yr_o, xs_o, xr_o, fs_o, fr_o, OUT)
    sd = Sum("d", 1, w_d, None, g_d, zr_d, ys_d, yr_d, xs_d, xr_d, fs_d, fr_d, D)
    at_rswap = [take(4) for _ in range(2)]
    swap_again = credits(1)

    def pair_start(k, l):
        pl.semaphore_signal(credit.at[k.free + l], inc=1, device_id={"replica": sib}, device_id_type=MESH)
        pl.semaphore_wait(credit.at[k.free + l], 1)

        @pl.when(core != k.owner)
        def _():
            copy(k.g, k.w.at[l], k.at[l], replica=sib).start()

    def pair_sent(k, l):
        @pl.when(core != k.owner)
        def _():
            sent(k.g, k.at[l])

    def add_into(dst, src, width):
        step = 256 if width % 256 == 0 else 128

        def add(t, c):
            cols = pl.ds(pl.multiple_of(t * step, 128), step)
            dst[:, cols] = (dst[:, cols].astype(f32) + src[:, cols].astype(f32)).astype(bf16)
            return c

        lax.fori_loop(0, width // step, add, 0)

    def rs_swap_start(l):
        @pl.when(core == 0)
        def _():
            arrived(w_gu.at[l], sgu.at[l])
            if l == 0:
                pl.semaphore_wait(credit.at[swap_again], 2)
            for j in (0, 2, 1, 3):
                src = w_gu.at[l, j, :, theirs]
                add_into(src, g_gu.at[j, :, theirs], FF)
                copy(src, xg.at[j], at_rswap[l] + j, **swap_to(j)).start()
            for j in range(SIDE):
                add_into(w_gu.at[l, j, :, mine], g_gu.at[j, :, mine], FF)

    def rs_z_start(k, l):
        @pl.when(core == k.owner)
        def _():
            if k is not sgu:
                arrived(k.w.at[l], k.at[l])
            if l == 0:
                pl.semaphore_wait(credit.at[k.again_z], 3)
            for d in (2, 1, 3, 0):
                zt = lax.rem(k.i1 + d, SIDE)
                part = k.band(l, zt)
                if k is sd:
                    part[...] = (part[...].astype(f32) + k.g[:, zt].astype(f32)).astype(bf16)
                elif k is sgu:
                    arrived(xg.at[zt], at_rswap[l] + zt)
                    add_into(part, xg.at[zt], FF)
                else:
                    add_into(part, k.g.at[zt], k.width)
                if d:
                    copy(part, k.zr.at[d - 1], k.at[l] + d, shard=k.peer1(d)).start()
            if k is sgu and l == 1:
                for j in (0, 2):
                    pl.semaphore_signal(
                        credit.at[swap_again], inc=1, device_id=swap_to(j), device_id_type=MESH
                    )

    def rs_y_start(k, l):
        @pl.when(core == k.owner)
        def _():
            for d in range(1, SIDE):
                arrived(k.zr.at[d - 1], k.at[l] + d)
            if l == 0:
                for d in range(1, SIDE):
                    sent(k.yr.at[0], k.at[1] + 3 + d)
            own = k.band(l, k.i1)
            if k is sd:
                tot = own[...].astype(f32)
                for d in range(3):
                    tot += k.zr[d].astype(f32)
                k.ys[...] = tot.astype(bf16)
            else:
                step = 256 if k.width % 256 == 0 else 128

                def add(t, c):
                    cols = pl.ds(pl.multiple_of(t * step, 128), step)
                    tot = own[:, cols].astype(f32)
                    for d in range(3):
                        tot += k.zr[d, :, cols].astype(f32)
                    for j in range(SIDE):
                        rows = tot[j * ROWS : j * ROWS + ROWS]
                        rows = jnp.concatenate([rows, jnp.zeros((PAD - ROWS, step), f32)], axis=0)
                        k.ys[j, :, cols] = rows.astype(bf16)
                    return c

                lax.fori_loop(0, k.width // step, add, 0)
            if l == 1:
                for d in range(1, SIDE):
                    pl.semaphore_signal(
                        credit.at[k.again_z], inc=1, device_id={"shard": k.peer1(d)}, device_id_type=MESH
                    )
            else:
                pl.semaphore_wait(credit.at[k.again_y], 3)
            for d in (2, 1, 3):
                yt = lax.rem(k.i2 + d, SIDE)
                copy(k.ys.at[yt], k.yr.at[d - 1], k.at[l] + 3 + d, shard=k.peer2(d)).start()

    def x_targets(l):
        for t in (1, 2, 3):
            other = 1 - sec if t >= 2 else sec
            where = {}
            if t >= 2:
                where["section"] = 1 - sec
            if t % 2:
                where["replica"] = far
            yield t, other == l, where

    def rs_x_start(k, l):
        @pl.when(core == k.owner)
        def _():
            for d in range(1, SIDE):
                arrived(k.yr.at[d - 1], k.at[l] + 3 + d)
            if l == 0:
                xs_sent(k, 1)
            tot = k.ys[k.i2].astype(f32)
            for d in range(3):
                tot += k.yr[d].astype(f32)
            k.xs[...] = tot.astype(bf16)
            if l == 1:
                for d in range(1, SIDE):
                    pl.semaphore_signal(
                        credit.at[k.again_y], inc=1, device_id={"shard": k.peer2(d)}, device_id_type=MESH
                    )
            for t, hit, where in x_targets(l):
                @pl.when(hit)
                def _():
                    copy(k.xs, k.xr.at[t - 1], k.at[l] + 6 + t, **where).start()

    def xs_sent(k, l):
        for t, hit, where in x_targets(l):
            @pl.when(hit)
            def _():
                sent(k.xs, k.at[l] + 6 + t)

    def write_out(k, tot):
        if k is sd:
            gd_ref[0] = tot
        elif k is sq:
            gq_ref[0] = tot[0:ROWS, 0:576]
            gk_ref[0] = tot[0:ROWS, 576:768]
            gv_ref[0] = tot[0:ROWS, 768:960]
            gain_ref[...] = tot[0:ROWS, 896:1024]
        else:
            go_ref[0] = tot[0:ROWS, 0:D]

    def rs_end_start(k, l):
        @pl.when((core == k.owner) & (sec == l))
        def _():
            for t in (1, 2, 3):
                arrived(k.xr.at[t - 1], k.at[l] + 6 + t)
            if k is sgu:
                own = k.xs[...].astype(f32) + k.xr[0].astype(f32)
                other = k.xr[1].astype(f32) + k.xr[2].astype(f32)
                own_ref, other_ref = (gg_ref, gu_ref) if l == 0 else (gu_ref, gg_ref)
                k.fs[l] = own.astype(bf16)
                k.fs[1 - l] = other.astype(bf16)
                copy(k.fs, k.fr, k.at[l] + 10, replica=sib).start()
                own_ref[0] = k.fs[l, 0:ROWS].astype(f32)
                other_ref[0] = k.fs[1 - l, 0:ROWS].astype(f32)
            else:
                tot = k.xs[...].astype(f32)
                for t in range(3):
                    tot += k.xr[t].astype(f32)
                k.fs[...] = tot.astype(bf16)
                copy(k.fs, k.fr, k.at[l] + 10, replica=sib).start()
                write_out(k, k.fs[...].astype(f32))

    def rs_end(k, l):
        @pl.when((core != k.owner) & (sec == l))
        def _():
            arrived(k.fr, k.at[l] + 10)
            if k is sgu:
                gg_ref[0] = k.fr[0, 0:ROWS].astype(f32)
                gu_ref[0] = k.fr[1, 0:ROWS].astype(f32)
            else:
                write_out(k, k.fr[...].astype(f32))

    def rs_sent():
        for k in (sgu, sd, so, sq):
            @pl.when(core == k.owner)
            def _():
                for l in (1, 0):
                    for d in range(1, SIDE):
                        sent(k.zr.at[0], k.at[l] + d)
                    if k is sgu:
                        for j in range(SIDE):
                            sent(xg.at[j], at_rswap[l] + j)

                    @pl.when(sec == l)
                    def _():
                        sent(k.fs, k.at[l] + 10)

                for d in range(1, SIDE):
                    sent(k.yr.at[0], k.at[0] + 3 + d)
                xs_sent(k, 0)

    at_o = [take(1) for _ in range(2)]
    at_d = [take(1) for _ in range(2)]

    def hand_over(l, value, own_ref, send, recv, at):
        @pl.when(sec == l)
        def _():
            own_ref[0, sec, 0] = value

        @pl.when(sec != l)
        def _():
            send[...] = value
            copy(send, recv, at[l], section=1 - sec).start()

    def hand_over_end(own_ref, send, recv, at):
        for l in range(2):
            @pl.when(sec == l)
            def _():
                arrived(recv, at[l])
                own_ref[0, 1 - sec, 0] = recv[...]

            @pl.when(sec != l)
            def _():
                sent(send, at[l])

    x_start(kq)
    x_start(kgu)
    x_start(ko)
    dx_start()
    xs_[0] = x_ref[sec, 0].astype(f32)
    y_start(kq, 0)
    y_start(kgu, 0)
    dz_start(0)
    y_start(ko, 0)
    z_start(kq, 0)
    z_start(kgu, 0)
    z_start(ko, 0)
    dy_start(0)
    y_start(kq, 1)
    y_start(kgu, 1)
    dz_start(1)
    y_start(ko, 1)
    z_end(kq, 0)
    gather_end(kq, 0)
    project_in(0)
    kv_start(0)
    z_end(kgu, 0)
    z_end(ko, 0)
    d_forward_on(0)
    z_start(kq, 1)
    kv_wait(0)
    attend(0, 0)
    swap_end(0)
    z_start(kgu, 1)
    z_start(ko, 1)
    dy_start(1)
    attend(0, 1)
    z_end(kq, 1)
    attend(0, 2)
    gather_end(ko, 0)
    gather_end(kgu, 0)
    d_gather_end(0)
    out = after_attention(0).astype(bf16)
    xs_[1] = out.astype(f32)
    hand_over(0, out, out_ref, osend, orecv, at_o)
    gather_end(kq, 1)
    project_in(1)
    kv_start(1)
    z_end(kgu, 1)
    z_end(ko, 1)
    d_forward_on(1)
    kv_wait(1)
    attend(1, 0)
    attend(1, 1)
    swap_end(1)
    attend(1, 2)
    gather_end(ko, 1)
    gather_end(kgu, 1)
    d_gather_end(1)
    out = after_attention(1).astype(bf16)
    hand_over(1, out, out_ref, osend, orecv, at_o)
    kv_sent(0)
    kv_sent(1)
    gather_sent()

    dmid = ffn_back(1, dy_ref[sec, 0].astype(f32))
    mid_[1] = dmid
    pair_start(sgu, 1)
    pair_start(sd, 1)
    out_back(1, dmid)
    pair_start(so, 1)
    attention_back(1, 0)
    rs_swap_start(1)
    attention_back(1, 1)
    rs_z_start(sd, 1)
    dkv_relay(1)
    rs_z_start(so, 1)
    rs_z_start(sgu, 1)
    dx = finish_back(1, mid_[1])
    pair_start(sq, 1)
    hand_over(1, dx, dx_ref, dsend, drecv, at_d)
    dkv_sent(1)
    rs_y_start(sd, 1)
    pair_sent(sgu, 1)
    pair_sent(sd, 1)
    dmid = ffn_back(0, dx.astype(bf16).astype(f32))
    mid_[0] = dmid
    pair_start(sgu, 0)
    pair_start(sd, 0)
    rs_z_start(sq, 1)
    rs_y_start(so, 1)
    pair_sent(so, 1)
    out_back(0, mid_[0])
    pair_start(so, 0)
    rs_y_start(sgu, 1)
    attention_back(0, 0)
    rs_swap_start(0)
    attention_back(0, 1)
    rs_x_start(sd, 1)
    rs_z_start(sd, 0)
    dkv_relay(0)
    rs_z_start(so, 0)
    rs_z_start(sgu, 0)
    rs_y_start(sq, 1)
    rs_x_start(so, 1)
    rs_x_start(sgu, 1)
    pair_sent(sq, 1)
    dx = finish_back(0, mid_[0])
    pair_start(sq, 0)
    hand_over(0, dx, dx_ref, dsend, drecv, at_d)
    rs_y_start(sd, 0)
    rs_z_start(sq, 0)
    rs_y_start(so, 0)
    rs_x_start(sq, 1)
    rs_y_start(sgu, 0)
    for k in (sd, so, sgu, sq):
        rs_end_start(k, 1)
    rs_x_start(sd, 0)
    rs_x_start(so, 0)
    rs_y_start(sq, 0)
    rs_x_start(sgu, 0)
    for k in (sd, so, sgu, sq):
        rs_end(k, 1)
    rs_x_start(sq, 0)
    for k in (sd, so, sgu, sq):
        rs_end_start(k, 0)
    for k in (sd, so, sgu, sq):
        rs_end(k, 0)
    for k in (sd, so, sgu, sq):
        pair_sent(k, 0)
    dkv_sent(0)
    rs_sent()
    hand_over_end(out_ref, osend, orecv, at_o)
    hand_over_end(dx_ref, dsend, drecv, at_d)
    assert used[0] <= SEMS, used[0]


SEMS = 400


def scratch():
    v = lambda *shape: pltpu.VMEM(shape, bf16)
    w = lambda *shape: pltpu.VMEM(shape, f32)
    widths = (FF, QKV, OUT)
    return [
        *[v(2, SIDE, PAD, n) for n in widths],
        *[v(2, SIDE, BAND, n) for n in (GU, QKV, OUT)], v(2, SIDE, SIDE, FROWS, D),
        v(2, SHARDS * TOK, 384), v(2, SHARDS - 1, TOK, 384),
        w(GROUP, SHARDS * TOK), w(GROUP, 128), w(GROUP, 128),
        w(2, TOK, D), v(2, TOK, D), v(2, HEADS, TOK, 64), v(2, HEADS, TOK, 64),
        w(2, KV_HEADS, GROUP, 1), w(2, TOK, D), v(2, TOK, D), w(2, TOK, GU),
        v(TOK, D), v(HEADS, TOK, 64), w(KV_HEADS, GROUP, 1), w(HEADS, TOK, 64), w(TOK, 384),
        w(TOK, D), v(TOK, D),
        *[v(SIDE, BAND, n) for n in (GU, QKV, OUT)], v(SIDE, SIDE, FROWS, D), v(SIDE, BAND, FF),
        *[v(3, BAND, n) for n in widths], v(3, SIDE, FROWS, D),
        *[v(SIDE, PAD, n) for n in widths], v(SIDE, FROWS, D),
        *[v(3, PAD, n) for n in widths], v(3, FROWS, D),
        *[v(PAD, n) for n in widths], v(FROWS, D),
        *[v(3, PAD, n) for n in widths], v(3, FROWS, D),
        v(2, PAD, FF), v(PAD, QKV), v(PAD, OUT), v(FROWS, D),
        v(2, PAD, FF), v(PAD, QKV), v(PAD, OUT), v(FROWS, D),
        v(TOK, D), v(TOK, D), w(TOK, D), w(TOK, D),
        pltpu.SemaphoreType.DMA((SEMS,)), pltpu.SemaphoreType.DMA((SEMS,)),
        pltpu.SemaphoreType.REGULAR((32,)),
    ]


def kernel(*refs):
    body(*refs)


def local(
    inputs, out_grad, w_query, w_key, w_value, w_out, w_gate, w_up, w_down, gain_attn, gain_ffn
):
    shard_index = lax.axis_index("shard")
    positions = shard_index * TOK + jnp.arange(TOK, dtype=jnp.int32)
    half = HEAD_DIM // 2
    inverse = rope_base ** (-(jnp.arange(half, dtype=f32) * 2.0 / HEAD_DIM))
    angles = positions.astype(f32)[:, None] * inverse[None, :]
    cos, sin = jnp.cos(angles), jnp.sin(angles)
    cos = jnp.concatenate([cos] * 4, axis=1)
    sin = jnp.concatenate([-sin, sin, -sin, sin], axis=1)
    more = ((0, PAD - ROWS), (0, 0))
    p0 = jnp.pad(jnp.concatenate([w_gate[0], w_up[0]], axis=1), more)
    gain_cols = jnp.stack([gain_attn[0], gain_ffn[0]], axis=1)
    pq = jnp.concatenate(
        [w_query[0], w_key[0], w_value[0], gain_cols, jnp.zeros((ROWS, 62), bf16)], axis=1
    )
    pq = jnp.pad(pq, more)
    po = jnp.pad(w_out[0], ((0, PAD - ROWS), (0, OUT - D)))
    whole = pl.BlockSpec(memory_space=pltpu.VMEM)
    shapes = (
        ((1, 2, 1, TOK, D), bf16), ((1, 2, 1, TOK, D), f32),
        ((1, ROWS, 576), f32), ((1, ROWS, 192), f32), ((1, ROWS, 192), f32), ((1, ROWS, 576), f32),
        ((1, ROWS, FF), f32), ((1, ROWS, FF), f32), ((1, FROWS, D), f32), ((ROWS, 128), f32),
    )
    res = pl.pallas_call(
        kernel,
        out_shape=[jax.ShapeDtypeStruct(s, t) for s, t in shapes],
        in_specs=[whole] * 8,
        out_specs=[whole] * len(shapes),
        scratch_shapes=scratch(),
        compiler_params=pltpu.CompilerParams(
            collective_id=0, has_side_effects=True, vmem_limit_bytes=63 * 1024 * 1024
        ),
        name="two_layers",
    )(inputs, out_grad, p0, pq, po, w_down[0], cos, sin)
    out, dx, gq, gk, gv, go, gg, gu, gd, gain = res
    return (out, dx, gq, gk, gv, go, gg, gu, gd, gain[:, 64][None], gain[:, 65][None])


def solution(mesh):
    return jax.shard_map(
        local,
        mesh=mesh,
        in_specs=(
            P(None, "replica", "shard", None),
            P(None, "replica", "shard", None),
            P("section", "shard", None),
            P("section", "shard", None),
            P("section", "shard", None),
            P("section", "shard", None),
            P("section", "shard", None),
            P("section", "shard", None),
            P("section", "shard", None),
            P("section", "shard"),
            P("section", "shard"),
        ),
        out_specs=(
            P("section", None, "replica", "shard", None),
            P("section", None, "replica", "shard", None),
            P("section", "shard", None),
            P("section", "shard", None),
            P("section", "shard", None),
            P("section", "shard", None),
            P("section", "shard", None),
            P("section", "shard", None),
            P("section", "shard", None),
            P("section", "shard"),
            P("section", "shard"),
        ),
        check_vma=False,
    )
```

```python
import functools

import jax
import jax.numpy as jnp
import numpy as np
from jax import lax
from jax.experimental import pallas as pl
from jax.experimental.pallas import tpu as pltpu
from jax.sharding import PartitionSpec as P

HEADS = 9
KV_HEADS = 3
HEAD_DIM = 64
D = 576
FF = 1536
TOK = 128
SHARDS = 16
SIDE = 4
ROWS = 36
PAD = 48
BAND = SIDE * ROWS
FROWS = 96
FBAND = SIDE * FROWS
GU = 2 * FF
QKV = 1024
OUT = 640
CHUNK = 512
GROUP = 3 * TOK

bf16 = jnp.bfloat16
f32 = jnp.float32
MESH = pl.DeviceIdType.MESH
epsilon = 1e-05
rope_base = 100000.0
score_scale = 0.125


def dot(a, b):
    return lax.dot_general(a, b, (((1,), (0,)), ((), ())), preferred_element_type=f32)


def dot_nt(a, b):
    return lax.dot_general(a, b, (((1,), (1,)), ((), ())), preferred_element_type=f32)


def dot_tn(a, b):
    return lax.dot_general(a, b, (((0,), (0,)), ((), ())), preferred_element_type=f32)


def factor_of(v):
    return lax.rsqrt(jnp.mean(v * v, axis=-1, keepdims=True) + epsilon)


def norm_back(v, r, gain, up):
    scaled = gain * up
    return r * scaled - v * (r * r * r) * jnp.mean(scaled * v, axis=-1, keepdims=True)


def half_swap(u):
    width = u.shape[1]
    lane = lax.broadcasted_iota(jnp.int32, u.shape, 1)
    first = lax.rem(lane, HEAD_DIM) < HEAD_DIM // 2
    return jnp.where(first, pltpu.roll(u, width - 32, 1), pltpu.roll(u, 32, 1))


def body(
    x_ref, dy_ref, wq_ref, wk_ref, wv_ref, wo_ref, wg_ref, wu_ref, wd_ref, ga_ref, gf_ref, near_ref, far_ref,
    out_ref, dx_ref, fin_gu, fin_q, fin_o, fin_d,
    stage_gu, stage_q, stage_o, w_gu, w_q, w_o, w_d, kv, dkv_r, scr, mx, acc,
    xs_, a_, q8_, o_, lse_, mid_, bn_, gu_,
    dyb_, dob_, delta_, dq_, dkv_acc, acc2, gain_term,
    g_gu, g_q, g_o, g_d, xg,
    zr_gu, zr_q, zr_o, zr_d, ys_gu, ys_q, ys_o, ys_d, yr_gu, yr_q, yr_o, yr_d,
    xs_gu, xs_q, xs_o, xs_d, xr_gu, xr_q, xr_o, xr_d, fs_gu, fs_q, fs_o, fs_d, fr_gu, fr_q, fr_o, fr_d,
    osend, orecv, dsend, drecv, pack_gu, cos_ref, sin_ref,
    ssem, rsem, credit,
):
    sec = lax.axis_index("section")
    sh = lax.axis_index("shard")
    rep = lax.axis_index("replica")
    z, y = lax.div(sh, SIDE), lax.rem(sh, SIDE)
    core = lax.rem(rep, 2)
    sib = rep + 1 - 2 * core
    far = lax.rem(rep + 2, 4)
    used = [0]

    def take(n):
        at = used[0]
        used[0] += n
        return at

    def copy(src, dst, at, to=None, **dev):
        return pltpu.make_async_remote_copy(
            src_ref=src, dst_ref=dst, send_sem=ssem.at[at], recv_sem=rsem.at[at if to is None else to],
            device_id=dev, device_id_type=MESH,
        )

    def arrived(dst, at):
        copy(dst, dst, at, shard=sh).wait_recv()

    def sent(src, at):
        copy(src, src, at, shard=sh).wait_send()

    def y_peer(d):
        return z * SIDE + lax.rem(y + d, SIDE)

    def z_peer(d):
        return lax.rem(z + d, SIDE) * SIDE + y

    def z_from(d):
        return lax.rem(z + SIDE - d, SIDE)

    def y_from(d):
        return lax.rem(y + SIDE - d, SIDE)

    last = pl.ds(pl.multiple_of(lax.div(sh, SIDE) * CHUNK, CHUNK), CHUNK)
    for l in range(2):
        kv[l, last, :] = jnp.zeros((CHUNK, 384), bf16)
    def padded(ref, value):
        ref[0:32] = value[0:32]
        ref[32:PAD] = jnp.concatenate(
            [value[32:ROWS].astype(f32), jnp.zeros((PAD - ROWS, value.shape[1]), f32)], axis=0
        ).astype(bf16)

    @pl.when(core == 1)
    def _():
        row16 = lax.broadcasted_iota(jnp.int32, (16, ROWS), 0)
        gain16 = jnp.where(
            row16 == 0, ga_ref[...].astype(f32), jnp.where(row16 == 1, gf_ref[...].astype(f32), 0.0)
        ).astype(bf16)
        place = lax.broadcasted_iota(jnp.int32, (16, 64), 0) == lax.broadcasted_iota(jnp.int32, (16, 64), 1)
        gain_cols = dot_tn(gain16, jnp.where(place, 1.0, 0.0).astype(bf16))
        whole = jnp.concatenate(
            [wq_ref[0].astype(f32), wk_ref[0].astype(f32), wv_ref[0].astype(f32), gain_cols], axis=1
        ).astype(bf16)
        padded(stage_q.at[sec, y], whole)
        whole = jnp.concatenate([wo_ref[0].astype(f32), jnp.zeros((ROWS, OUT - D), f32)], axis=1).astype(bf16)
        padded(stage_o.at[sec, y], whole)
        w_d[sec, z, y] = wd_ref[0]

    for c in range(2):
        @pl.when((core == 0) & (sec == c))
        def _():
            padded(stage_gu.at[sec, y], (wg_ref, wu_ref)[c][0])
            padded(pack_gu, (wg_ref, wu_ref)[1 - c][0])

    cos1, sin1 = near_ref[:, 0:128], near_ref[:, 128:256]
    first = far_ref[sh]
    cos2, sin2 = first[0:1, 0:128], first[0:1, 128:256]
    low = lax.rem(lax.broadcasted_iota(jnp.int32, (TOK, 128), 1), HEAD_DIM) < HEAD_DIM // 2
    cos_ref[...] = cos1 * cos2 - sin1 * sin2
    sine = sin1 * cos2 + cos1 * sin2
    sin_ref[...] = jnp.where(low, -sine, sine)
    xs_[0] = x_ref[sec, 0].astype(f32).T

    barrier = pltpu.get_barrier_semaphore()

    def greet(d, c):
        pl.semaphore_signal(barrier, inc=1, device_id={"shard": lax.rem(sh + d, SHARDS)}, device_id_type=MESH)
        return c

    lax.fori_loop(1, SHARDS, greet, 0)
    pl.semaphore_signal(barrier, inc=1, device_id={"replica": sib}, device_id_type=MESH)
    pl.semaphore_signal(barrier, inc=1, device_id={"replica": far}, device_id_type=MESH)
    pl.semaphore_signal(barrier, inc=1, device_id={"section": 1 - sec}, device_id_type=MESH)
    pl.semaphore_signal(barrier, inc=1, device_id={"section": 1 - sec, "replica": far}, device_id_type=MESH)
    pl.semaphore_wait(barrier, SHARDS - 1 + 4)

    mine = pl.ds(pl.multiple_of(sec * FF, 128), FF)
    theirs = pl.ds(pl.multiple_of((1 - sec) * FF, 128), FF)

    class Gather:
        def __init__(self, owner, send, stage, w, cols, width):
            self.owner, self.send, self.stage, self.w, self.width = owner, send, stage, w, width
            self.cols = cols
            self.at_x = take(1)
            self.at_y = [take(3) for _ in range(2)]
            self.at_z = [take(3) for _ in range(2)]
            self.at_f = [take(4) for _ in range(2)]

        def band(self, l, j):
            return self.w.at[l, j, :, self.cols]

    kgu = Gather(0, pack_gu, stage_gu, w_gu, mine, FF)
    kq = Gather(1, stage_q.at[sec, y], stage_q, w_q, pl.ds(0, QKV), QKV)
    ko = Gather(1, stage_o.at[sec, y], stage_o, w_o, pl.ds(0, OUT), OUT)
    at_xd = take(1)
    at_dz = [take(3) for _ in range(2)]
    at_dy = [take(3) for _ in range(2)]
    at_df = [take(1) for _ in range(2)]
    at_swap = [take(4) for _ in range(2)]
    at_sf = [take(4) for _ in range(2)]

    def x_start(k):
        @pl.when(core == k.owner)
        def _():
            copy(k.send, k.stage.at[sec, y], k.at_x, section=1 - sec).start()

    def dx_start():
        @pl.when(core == 1)
        def _():
            copy(w_d.at[sec, z, y], w_d.at[sec, z, y], at_xd, section=1 - sec).start()

    def y_start(k, l):
        @pl.when(core == k.owner)
        def _():
            own = k.stage.at[l, y]

            @pl.when(sec != l)
            def _():
                arrived(own, k.at_x)

            for d in (2, 1, 3):
                copy(own, own, k.at_y[l] + d - 1, shard=y_peer(d)).start()

    def dz_start(l):
        @pl.when(core == 1)
        def _():
            own = w_d.at[l, z, y]

            @pl.when(sec != l)
            def _():
                arrived(own, at_xd)

            for d in (2, 1, 3):
                copy(own, own, at_dz[l] + d - 1, shard=z_peer(d)).start()

    def z_start(k, l):
        @pl.when(core == k.owner)
        def _():
            for d in range(1, SIDE):
                arrived(k.stage.at[l, y_from(d)], k.at_y[l] + d - 1)
            own = k.band(l, z)
            for at in range(0, k.width, 128):
                parts = [k.stage[l, j, :, at : at + 128][0:ROWS].astype(f32) for j in range(SIDE)]
                own[:, at : at + 128] = jnp.concatenate(parts, axis=0).astype(bf16)
            for d in (2, 1, 3):
                copy(own, own, k.at_z[l] + d - 1, shard=z_peer(d)).start()
            copy(own, own, k.at_f[l], replica=sib).start()

    def dy_start(l):
        @pl.when(core == 1)
        def _():
            for d in range(1, SIDE):
                arrived(w_d.at[l, z_from(d), y], at_dz[l] + d - 1)
            own = w_d.at[l, :, y]
            for d in (2, 1, 3):
                copy(own, own, at_dy[l] + d - 1, shard=y_peer(d)).start()

    def z_end(k, l):
        @pl.when(core == k.owner)
        def _():
            for d in (1, 3, 2):
                got = k.band(l, z_from(d))
                arrived(got, k.at_z[l] + d - 1)
                copy(got, got, k.at_f[l] + d, replica=sib).start()
            if k is kgu:
                for j in range(SIDE):
                    got = k.band(l, j)
                    copy(got, got, at_swap[l] + j, **swap_to(j)).start()

    def swap_to(j):
        return {"section": 1 - sec} if j < 2 else {"section": 1 - sec, "replica": far}

    def swap_end(l):
        @pl.when(core == 0)
        def _():
            for j in range(SIDE):
                got = w_gu.at[l, j, :, theirs]
                arrived(got, at_swap[l] + j)
                copy(got, got, at_sf[l] + j, replica=sib).start()

    def d_forward_on(l):
        @pl.when(core == 1)
        def _():
            for d in range(1, SIDE):
                arrived(w_d.at[l, :, y_from(d)], at_dy[l] + d - 1)
            copy(w_d.at[l], w_d.at[l], at_df[l], replica=sib).start()

    def gather_end(k, l):
        @pl.when(core != k.owner)
        def _():
            arrived(k.band(l, z), k.at_f[l])
            for d in range(1, SIDE):
                arrived(k.band(l, z_from(d)), k.at_f[l] + d)
            if k is kgu:
                for j in range(SIDE):
                    arrived(w_gu.at[l, j, :, theirs], at_sf[l] + j)

    def d_gather_end(l):
        @pl.when(core == 0)
        def _():
            arrived(w_d.at[l], at_df[l])

    def gather_sent():
        for l in range(2):
            for k in (kgu, kq, ko):
                @pl.when(core == k.owner)
                def _():
                    @pl.when(sec == l)
                    def _():
                        sent(k.send, k.at_x)

                    for d in range(1, SIDE):
                        sent(k.stage.at[l, y], k.at_y[l] + d - 1)
                        sent(k.band(l, z), k.at_z[l] + d - 1)
                        sent(k.band(l, z), k.at_f[l] + d)
                    sent(k.band(l, z), k.at_f[l])
                    if k is kgu:
                        for j in range(SIDE):
                            sent(k.band(l, j), at_swap[l] + j)
                            sent(k.band(l, j), at_sf[l] + j)

            @pl.when(core == 1)
            def _():
                @pl.when(sec == l)
                def _():
                    sent(w_d.at[0, z, y], at_xd)

                for d in range(1, SIDE):
                    sent(w_d.at[l, z, y], at_dz[l] + d - 1)
                    sent(w_d.at[l, :, y], at_dy[l] + d - 1)
                sent(w_d.at[l], at_df[l])

    at_kv = [take(SHARDS) for _ in range(2)]
    at_kvr = [take(4) for _ in range(2)]
    at_dkv = [take(SHARDS) for _ in range(2)]
    at_dky = [take(4) for _ in range(2)]
    tokens = pl.ds(pl.multiple_of(sh * TOK, TOK), TOK)
    twice = 2 * SIDE

    def block(l, j):
        return kv.at[l, pl.ds(pl.multiple_of(j * TOK, TOK), TOK)]

    def relayed(j):
        gap = lax.div(j, SIDE) - z
        return ((gap == 2) | (gap == -2)) & (lax.rem(j, SIDE) != y)

    def kv_start(l):
        own = kv.at[l, tokens]

        def go(d, c):
            @pl.when(jnp.logical_not(relayed(sh + d)))
            def _():
                copy(own, own, at_kv[l] + d, shard=sh + d).start()

            return c

        lax.fori_loop(1, SHARDS - sh, go, 0)

    def kv_wait(l):
        @pl.when(z >= 2)
        def _():
            passing = block(l, sh - twice)
            arrived(passing, at_kv[l] + twice)
            for e in range(1, SIDE):
                yt = lax.rem(y + e, SIDE)
                copy(passing, passing, at_kvr[l] + e, to=at_kv[l] + twice + yt - y, shard=y_peer(e)).start()

        def go(d, c):
            @pl.when(d != twice)
            def _():
                arrived(block(l, sh - d), at_kv[l] + d)

            return c

        lax.fori_loop(1, sh + 1, go, 0)

    def kv_sent(l):
        def go(d, c):
            @pl.when(jnp.logical_not(relayed(sh + d)))
            def _():
                sent(kv.at[l, tokens], at_kv[l] + d)

            return c

        lax.fori_loop(1, SHARDS - sh, go, 0)

        @pl.when(z >= 2)
        def _():
            for e in range(1, SIDE):
                sent(kv.at[l, tokens], at_kvr[l] + e)

    def dkv_start(l, j):
        away = relayed(j)

        @pl.when(away)
        def _():
            e = lax.rem(lax.rem(j, SIDE) - y + SIDE, SIDE)
            copy(
                block(l, j), dkv_r.at[l, twice - 1 + e], at_dkv[l] + sh - j,
                to=at_dky[l] + e, shard=z * SIDE + lax.rem(j, SIDE),
            ).start()

        @pl.when(jnp.logical_not(away) & (sh - j != twice))
        def _():
            copy(block(l, j), dkv_r.at[l, sh - j - 1], at_dkv[l] + sh - j, shard=j).start()

    def dkv_relay(l):
        @pl.when(z >= 2)
        def _():
            passing = block(l, sh - twice)
            for e in range(1, SIDE):
                arrived(dkv_r.at[l, twice - 1 + e], at_dky[l] + e)
            tot = passing[...].astype(f32)
            for e in range(1, SIDE):
                tot += dkv_r[l, twice - 1 + e].astype(f32)
            passing[...] = tot.astype(bf16)
            copy(passing, dkv_r.at[l, twice - 1], at_dkv[l] + twice, shard=sh - twice).start()

    def dkv_sent(l):
        def go(d, c):
            sent(kv.at[l, pl.ds(0, TOK)], at_dkv[l] + d)
            return c

        lax.fori_loop(1, sh + 1, go, 0)

    def gains(l):
        tile = w_q[l, :, :, 896:1024].reshape(D, 128)
        row = lax.broadcasted_iota(jnp.int32, (8, 128), 0)
        lane = lax.broadcasted_iota(jnp.int32, (8, 128), 1)
        pick = jnp.where(lane == row + 64, 1.0, 0.0).astype(bf16)
        both = dot_nt(pick, tile)
        return both[0:1], both[1:2]

    nfull = lax.div(sh, SIDE)

    def causal():
        row = lax.broadcasted_iota(jnp.int32, (GROUP, CHUNK), 0)
        col = lax.broadcasted_iota(jnp.int32, (GROUP, CHUNK), 1)
        return col <= lax.rem(sh, SIDE) * TOK + lax.rem(row, TOK)

    def keys_at(c):
        return pl.ds(pl.multiple_of(c * CHUNK, CHUNK), CHUNK)

    def tables():
        cos = jnp.concatenate([cos_ref[...]] * 6, axis=1)
        sin = jnp.concatenate([sin_ref[...]] * 6, axis=1)
        return cos, sin

    def project_in(l):
        x = xs_[l]
        gain, _ = gains(l)
        a = (x * factor_of(x) * gain).astype(bf16)
        a_[l] = a
        qkv = dot(a, w_q[l].reshape(D, QKV))
        cos, sin = tables()
        u = qkv[:, 0:768]
        turned = u * cos + half_swap(u) * sin
        for h in range(HEADS):
            head = turned[:, h * 64 : h * 64 + 64].astype(bf16)
            q8_[l, h] = (head.astype(f32) * score_scale).astype(bf16)
        block = jnp.concatenate([turned[:, 576:768], qkv[:, 768:960]], axis=1).astype(bf16)
        kv[l, tokens] = block

    def attend(l, g):
        if True:
            q = q8_[l, 3 * g : 3 * g + 3].reshape(GROUP, 64)

            def keep(c, s):
                scr[:, keys_at(c)] = s
                top = jnp.maximum(
                    jnp.maximum(s[:, 0:128], s[:, 128:256]), jnp.maximum(s[:, 256:384], s[:, 384:512])
                )
                mx[...] = jnp.maximum(mx[...], top)

            def scores(c):
                k = kv[l, keys_at(c), :][:, g * 64 : g * 64 + 64]
                return dot_nt(q, k)

            mx[...] = jnp.full_like(mx, -1e30)

            def first(c, carry):
                keep(c, scores(c))
                return carry

            lax.fori_loop(0, nfull, first, 0)
            keep(nfull, jnp.where(causal(), scores(nfull), -1e30))
            peak = jnp.max(mx[...], axis=1, keepdims=True)
            acc[...] = jnp.zeros_like(acc)

            def second(c, carry):
                p = jnp.exp(scr[:, keys_at(c)] - peak).astype(bf16)
                v = kv[l, keys_at(c), :][:, 192 + g * 64 : 256 + g * 64]
                v = jnp.concatenate([v, jnp.ones_like(v)], axis=1)
                acc[...] += dot(p, v)
                return carry

            lax.fori_loop(0, nfull + 1, second, 0)
            total = acc[:, 64:65]
            mixed = (acc[:, 0:64] / total).astype(bf16)
            lse_[l, g] = peak + jnp.log(total)
            o_[l, 3 * g : 3 * g + 3] = mixed.reshape(3, TOK, 64)

    def heads_in(ref):
        return jnp.concatenate([ref[h] for h in range(HEADS)], axis=1)

    def after_attention(l):
        o = heads_in(o_.at[l])
        mid = xs_[l] + dot(o, w_o[l, :, :, 0:D].reshape(D, D))
        mid_[l] = mid
        _, gain = gains(l)
        bn_[l] = (mid * factor_of(mid) * gain).astype(bf16)
        acc2[...] = mid

        def tile(t, c):
            gcols = pl.ds(pl.multiple_of(t * FBAND, 128), FBAND)
            ucols = pl.ds(pl.multiple_of(FF + t * FBAND, 128), FBAND)
            bn = bn_[l]
            gt = dot(bn, w_gu[l, :, :, gcols].reshape(D, FBAND))
            up = dot(bn, w_gu[l, :, :, ucols].reshape(D, FBAND))
            gu_[l, :, gcols] = gt
            gu_[l, :, ucols] = up
            hid = (gt * jax.nn.sigmoid(gt) * up).astype(bf16)
            acc2[...] += dot(hid, w_d[l, t].reshape(FBAND, D))
            return c

        lax.fori_loop(0, SIDE, tile, 0)
        return acc2[...]

    def ffn_back(l, dy):
        dyb_[...] = dy.astype(bf16)
        acc2[...] = jnp.zeros_like(acc2)

        def tile(t, c):
            gcols = pl.ds(pl.multiple_of(t * FBAND, 128), FBAND)
            ucols = pl.ds(pl.multiple_of(FF + t * FBAND, 128), FBAND)
            dyb = dyb_[...]
            bn = bn_[l]
            wd = w_d[l, t].reshape(FBAND, D)
            dhid = dot_nt(dyb, wd).astype(bf16).astype(f32)
            gt, up = gu_[l, :, gcols], gu_[l, :, ucols]
            s = jax.nn.sigmoid(gt)
            hid = (gt * s * up).astype(bf16)
            g_d[t] = dot_tn(hid, dyb).astype(bf16).reshape(SIDE, FROWS, D)
            dgt = (dhid * up * s * (1.0 + gt * (1.0 - s))).astype(bf16)
            dup = (dhid * gt * s).astype(bf16)
            g_gu[:, :, gcols] = dot_tn(bn, dgt).astype(bf16).reshape(SIDE, BAND, FBAND)
            g_gu[:, :, ucols] = dot_tn(bn, dup).astype(bf16).reshape(SIDE, BAND, FBAND)
            acc2[...] += dot_nt(dgt, w_gu[l, :, :, gcols].reshape(D, FBAND))
            acc2[...] += dot_nt(dup, w_gu[l, :, :, ucols].reshape(D, FBAND))
            return c

        lax.fori_loop(0, SIDE, tile, 0)
        dbn = acc2[...]
        mid = mid_[l]
        r = factor_of(mid)
        _, gain = gains(l)
        gain_term[...] = (dbn * mid * r).astype(bf16)
        return dy + norm_back(mid, r, gain, dbn)

    def out_back(l, dmid):
        dmb = dmid.astype(bf16)
        o = heads_in(o_.at[l])
        g_o[...] = jnp.concatenate(
            [dot_tn(o, dmb), jnp.zeros((D, 64), f32)], axis=1
        ).astype(bf16).reshape(SIDE, BAND, 640)
        dob = dot_nt(dmb, w_o[l, :, :, 0:D].reshape(D, D)).astype(bf16)
        for h in range(HEADS):
            do_h = dob[:, h * 64 : h * 64 + 64]
            dq_[h] = jnp.zeros((TOK, 64), f32)
            dob_[h] = do_h

    def attention_back(l, part):
        for g in range(KV_HEADS):
            do = dob_[3 * g : 3 * g + 3].reshape(GROUP, 64).astype(f32)
            og = o_[l, 3 * g : 3 * g + 3].reshape(GROUP, 64).astype(f32)
            delta_[g] = jnp.sum(do * og, axis=1, keepdims=True)

        def chunk(c, masked):
            kvb = kv[l, keys_at(c), :]
            dks, dvs = [], []
            for g in range(KV_HEADS):
                q = q8_[l, 3 * g : 3 * g + 3].reshape(GROUP, 64)
                do = dob_[3 * g : 3 * g + 3].reshape(GROUP, 64)
                k = kvb[:, g * 64 : g * 64 + 64]
                v = kvb[:, 192 + g * 64 : 256 + g * 64]
                s = dot_nt(q, k)
                if masked:
                    s = jnp.where(causal(), s, -1e30)
                p = jnp.exp(s - lse_[l, g])
                ds = (p * (dot_nt(do, v) - delta_[g])).astype(bf16)
                dq_[3 * g : 3 * g + 3] += dot(ds, k).reshape(3, TOK, 64)
                dks.append(dot_tn(ds, q))
                dvs.append(dot_tn(p.astype(bf16), do))
            kv[l, keys_at(c), :] = jnp.concatenate(dks + dvs, axis=1).astype(bf16)

        def full(c, carry):
            chunk(c, False)
            for i in range(SIDE):
                dkv_start(l, c * SIDE + i)
            return carry

        def rest(j, carry):
            dkv_start(l, j)
            return carry

        if part == 0:
            lax.fori_loop(0, nfull, full, 0)
        else:
            chunk(nfull, True)
            lax.fori_loop(nfull * SIDE, sh, rest, 0)

    def finish_back(l, dmid_at):
        dkv_acc[...] = kv[l, tokens, :].astype(f32)

        def add(d, c):
            @pl.when(jnp.logical_not(relayed(sh + d)))
            def _():
                arrived(dkv_r.at[l, d - 1], at_dkv[l] + d)
                dkv_acc[...] += dkv_r[l, d - 1].astype(f32)

            return c

        lax.fori_loop(1, SHARDS - sh, add, 0)
        dkv = dkv_acc[...]
        cos, sin = tables()
        dq = jnp.concatenate([dq_[h] for h in range(HEADS)], axis=1) * score_scale
        u = jnp.concatenate([dq, dkv[:, 0:192]], axis=1)
        back = u * cos - half_swap(u) * sin
        dqkv = jnp.concatenate([back, dkv[:, 192:384], jnp.zeros((TOK, 64), f32)], axis=1).astype(bf16)
        a = a_[l]
        gq = dot_tn(a, dqkv)
        da = dot_nt(dqkv, w_q[l].reshape(D, QKV))
        x = xs_[l]
        r = factor_of(x)
        gain, _ = gains(l)
        lane = lax.broadcasted_iota(jnp.int32, (TOK, 128), 1)
        e0 = jnp.where(lane == 64, 1.0, 0.0).astype(bf16)
        e1 = jnp.where(lane == 65, 1.0, 0.0).astype(bf16)
        cols = dot_tn((da * x * r).astype(bf16), e0) + dot_tn(gain_term[...], e1)
        g_q[:, :, 0:896] = gq[:, 0:896].astype(bf16).reshape(SIDE, BAND, 896)
        g_q[:, :, 896:1024] = (gq[:, 896:1024] + cols).astype(bf16).reshape(SIDE, BAND, 128)
        return dmid_at + norm_back(x, r, gain, da)

    class Sum:
        def __init__(self, name, owner, w, cols, g, zr, ys, yr, xs, xr, fs, fr, width):
            self.name, self.owner, self.w, self.cols, self.g = name, owner, w, cols, g
            self.zr, self.ys, self.yr, self.xs, self.xr, self.fs, self.fr = zr, ys, yr, xs, xr, fs, fr
            self.width = width
            self.at = [take(12) for _ in range(2)]
            self.free = credits(2)
            self.again_z, self.again_y = credits(1), credits(1)

            first_y = name == "d"
            self.i1, self.peer1 = (y, y_peer) if first_y else (z, z_peer)
            self.i2, self.peer2 = (z, z_peer) if first_y else (y, y_peer)

        def band(self, l, j):
            return self.w.at[l, :, j] if self.name == "d" else self.w.at[l, j, :, self.cols]

    granted = [0]

    def credits(n):
        at = granted[0]
        granted[0] += n
        return at

    sgu = Sum("gu", 0, w_gu, mine, g_gu, zr_gu, ys_gu, yr_gu, xs_gu, xr_gu, fs_gu, fr_gu, FF)
    sq = Sum("q", 1, w_q, pl.ds(0, QKV), g_q, zr_q, ys_q, yr_q, xs_q, xr_q, fs_q, fr_q, QKV)
    so = Sum("o", 1, w_o, pl.ds(0, OUT), g_o, zr_o, ys_o, yr_o, xs_o, xr_o, fs_o, fr_o, OUT)
    sd = Sum("d", 1, w_d, None, g_d, zr_d, ys_d, yr_d, xs_d, xr_d, fs_d, fr_d, D)
    at_rswap = [take(4) for _ in range(2)]
    swap_again = credits(1)

    def pair_start(k, l):
        pl.semaphore_signal(credit.at[k.free + l], inc=1, device_id={"replica": sib}, device_id_type=MESH)
        pl.semaphore_wait(credit.at[k.free + l], 1)

        @pl.when(core != k.owner)
        def _():
            copy(k.g, k.w.at[l], k.at[l], replica=sib).start()

    def pair_sent(k, l):
        @pl.when(core != k.owner)
        def _():
            sent(k.g, k.at[l])

    def add_into(dst, src, width):
        step = 256 if width % 256 == 0 else 128

        def add(t, c):
            cols = pl.ds(pl.multiple_of(t * step, 128), step)
            dst[:, cols] = (dst[:, cols].astype(f32) + src[:, cols].astype(f32)).astype(bf16)
            return c

        lax.fori_loop(0, width // step, add, 0)

    def rs_swap_start(l):
        @pl.when(core == 0)
        def _():
            arrived(w_gu.at[l], sgu.at[l])
            if l == 0:
                pl.semaphore_wait(credit.at[swap_again], 2)
            for j in (0, 2, 1, 3):
                src = w_gu.at[l, j, :, theirs]
                add_into(src, g_gu.at[j, :, theirs], FF)
                copy(src, xg.at[j], at_rswap[l] + j, **swap_to(j)).start()
            for j in range(SIDE):
                add_into(w_gu.at[l, j, :, mine], g_gu.at[j, :, mine], FF)

    def rs_z_start(k, l):
        @pl.when(core == k.owner)
        def _():
            if k is not sgu:
                arrived(k.w.at[l], k.at[l])
            if l == 0:
                pl.semaphore_wait(credit.at[k.again_z], 3)
            for d in (2, 1, 3, 0):
                zt = lax.rem(k.i1 + d, SIDE)
                part = k.band(l, zt)
                if k is sd:
                    part[...] = (part[...].astype(f32) + k.g[:, zt].astype(f32)).astype(bf16)
                elif k is sgu:
                    arrived(xg.at[zt], at_rswap[l] + zt)
                    add_into(part, xg.at[zt], FF)
                else:
                    add_into(part, k.g.at[zt], k.width)
                if d:
                    copy(part, k.zr.at[d - 1], k.at[l] + d, shard=k.peer1(d)).start()
            if k is sgu and l == 1:
                for j in (0, 2):
                    pl.semaphore_signal(
                        credit.at[swap_again], inc=1, device_id=swap_to(j), device_id_type=MESH
                    )

    def rs_y_start(k, l):
        @pl.when(core == k.owner)
        def _():
            for d in range(1, SIDE):
                arrived(k.zr.at[d - 1], k.at[l] + d)
            if l == 0:
                for d in range(1, SIDE):
                    sent(k.yr.at[0], k.at[1] + 3 + d)
            own = k.band(l, k.i1)
            if k is sd:
                tot = own[...].astype(f32)
                for d in range(3):
                    tot += k.zr[d].astype(f32)
                k.ys[...] = tot.astype(bf16)
            else:
                step = 256 if k.width % 256 == 0 else 128

                def add(t, c):
                    cols = pl.ds(pl.multiple_of(t * step, 128), step)
                    tot = own[:, cols].astype(f32)
                    for d in range(3):
                        tot += k.zr[d, :, cols].astype(f32)
                    for j in range(SIDE):
                        rows = tot[j * ROWS : j * ROWS + ROWS]
                        rows = jnp.concatenate([rows, jnp.zeros((PAD - ROWS, step), f32)], axis=0)
                        k.ys[j, :, cols] = rows.astype(bf16)
                    return c

                lax.fori_loop(0, k.width // step, add, 0)
            if l == 1:
                for d in range(1, SIDE):
                    pl.semaphore_signal(
                        credit.at[k.again_z], inc=1, device_id={"shard": k.peer1(d)}, device_id_type=MESH
                    )
            else:
                pl.semaphore_wait(credit.at[k.again_y], 3)
            for d in (2, 1, 3):
                yt = lax.rem(k.i2 + d, SIDE)
                copy(k.ys.at[yt], k.yr.at[d - 1], k.at[l] + 3 + d, shard=k.peer2(d)).start()

    def x_targets(l):
        for t in (1, 2, 3):
            other = 1 - sec if t >= 2 else sec
            where = {}
            if t >= 2:
                where["section"] = 1 - sec
            if t % 2:
                where["replica"] = far
            yield t, other == l, where

    def rs_x_start(k, l):
        @pl.when(core == k.owner)
        def _():
            for d in range(1, SIDE):
                arrived(k.yr.at[d - 1], k.at[l] + 3 + d)
            if l == 0:
                xs_sent(k, 1)
            tot = k.ys[k.i2].astype(f32)
            for d in range(3):
                tot += k.yr[d].astype(f32)
            k.xs[...] = tot.astype(bf16)
            if l == 1:
                for d in range(1, SIDE):
                    pl.semaphore_signal(
                        credit.at[k.again_y], inc=1, device_id={"shard": k.peer2(d)}, device_id_type=MESH
                    )
            for t, hit, where in x_targets(l):
                @pl.when(hit)
                def _():
                    copy(k.xs, k.xr.at[t - 1], k.at[l] + 6 + t, **where).start()

    def xs_sent(k, l):
        for t, hit, where in x_targets(l):
            @pl.when(hit)
            def _():
                sent(k.xs, k.at[l] + 6 + t)

    fins = {"gu": fin_gu, "q": fin_q, "o": fin_o, "d": fin_d}

    def rs_end_start(k, l):
        @pl.when((core == k.owner) & (sec == l))
        def _():
            for t in (1, 2, 3):
                arrived(k.xr.at[t - 1], k.at[l] + 6 + t)
            if k is sgu:
                own = k.xs[...].astype(f32) + k.xr[0].astype(f32)
                other = k.xr[1].astype(f32) + k.xr[2].astype(f32)
                k.fs[l] = own.astype(bf16)
                k.fs[1 - l] = other.astype(bf16)
                copy(k.fs, k.fr, k.at[l] + 10, replica=sib).start()
            else:
                tot = k.xs[...].astype(f32)
                for t in range(3):
                    tot += k.xr[t].astype(f32)
                k.fs[...] = tot.astype(bf16)
                copy(k.fs, k.fr, k.at[l] + 10, replica=sib).start()

    def rs_end(k, l):
        @pl.when((core != k.owner) & (sec == l))
        def _():
            arrived(k.fr, k.at[l] + 10)
            fins[k.name][...] = k.fr[...]

        @pl.when((core == k.owner) & (sec == l))
        def _():
            fins[k.name][...] = k.fs[...]

    def rs_sent():
        for k in (sgu, sd, so, sq):
            @pl.when(core == k.owner)
            def _():
                for l in (1, 0):
                    for d in range(1, SIDE):
                        sent(k.zr.at[0], k.at[l] + d)
                    if k is sgu:
                        for j in range(SIDE):
                            sent(xg.at[j], at_rswap[l] + j)

                    @pl.when(sec == l)
                    def _():
                        sent(k.fs, k.at[l] + 10)

                for d in range(1, SIDE):
                    sent(k.yr.at[0], k.at[0] + 3 + d)
                xs_sent(k, 0)

    at_o = [take(1) for _ in range(2)]
    at_d = [take(1) for _ in range(2)]

    def hand_over(l, value, own_ref, send, recv, at):
        value = value.T.astype(own_ref.dtype)

        @pl.when(sec == l)
        def _():
            own_ref[0, sec, 0] = value

        @pl.when(sec != l)
        def _():
            send[...] = value
            copy(send, recv, at[l], section=1 - sec).start()

    def hand_over_end(own_ref, send, recv, at):
        for l in range(2):
            @pl.when(sec == l)
            def _():
                arrived(recv, at[l])
                own_ref[0, 1 - sec, 0] = recv[...]

            @pl.when(sec != l)
            def _():
                sent(send, at[l])

    x_start(kq)
    x_start(kgu)
    x_start(ko)
    dx_start()
    y_start(kq, 0)
    y_start(kgu, 0)
    dz_start(0)
    y_start(ko, 0)
    z_start(kq, 0)
    z_start(kgu, 0)
    z_start(ko, 0)
    dy_start(0)
    y_start(kq, 1)
    y_start(kgu, 1)
    dz_start(1)
    y_start(ko, 1)
    z_end(kq, 0)
    gather_end(kq, 0)
    project_in(0)
    kv_start(0)
    z_end(kgu, 0)
    z_end(ko, 0)
    d_forward_on(0)
    z_start(kq, 1)
    kv_wait(0)
    attend(0, 0)
    swap_end(0)
    z_start(kgu, 1)
    z_start(ko, 1)
    dy_start(1)
    attend(0, 1)
    z_end(kq, 1)
    attend(0, 2)
    gather_end(ko, 0)
    gather_end(kgu, 0)
    d_gather_end(0)
    out = after_attention(0)
    xs_[1] = out.astype(bf16).astype(f32)
    hand_over(0, out, out_ref, osend, orecv, at_o)
    gather_end(kq, 1)
    project_in(1)
    kv_start(1)
    z_end(kgu, 1)
    z_end(ko, 1)
    d_forward_on(1)
    kv_wait(1)
    attend(1, 0)
    attend(1, 1)
    swap_end(1)
    attend(1, 2)
    gather_end(ko, 1)
    gather_end(kgu, 1)
    d_gather_end(1)
    out = after_attention(1)
    hand_over(1, out, out_ref, osend, orecv, at_o)
    kv_sent(0)
    kv_sent(1)
    gather_sent()

    dmid = ffn_back(1, dy_ref[sec, 0].astype(f32).T)
    mid_[1] = dmid
    pair_start(sgu, 1)
    pair_start(sd, 1)
    out_back(1, dmid)
    pair_start(so, 1)
    attention_back(1, 0)
    rs_swap_start(1)
    attention_back(1, 1)
    rs_z_start(sd, 1)
    dkv_relay(1)
    rs_z_start(so, 1)
    rs_z_start(sgu, 1)
    dx = finish_back(1, mid_[1])
    pair_start(sq, 1)
    hand_over(1, dx, dx_ref, dsend, drecv, at_d)
    dkv_sent(1)
    rs_y_start(sd, 1)
    pair_sent(sgu, 1)
    pair_sent(sd, 1)
    dmid = ffn_back(0, dx.astype(bf16).astype(f32))
    mid_[0] = dmid
    pair_start(sgu, 0)
    pair_start(sd, 0)
    rs_z_start(sq, 1)
    rs_y_start(so, 1)
    pair_sent(so, 1)
    out_back(0, mid_[0])
    pair_start(so, 0)
    rs_y_start(sgu, 1)
    attention_back(0, 0)
    rs_swap_start(0)
    attention_back(0, 1)
    rs_x_start(sd, 1)
    rs_z_start(sd, 0)
    dkv_relay(0)
    rs_z_start(so, 0)
    rs_z_start(sgu, 0)
    rs_y_start(sq, 1)
    rs_x_start(so, 1)
    rs_x_start(sgu, 1)
    pair_sent(sq, 1)
    dx = finish_back(0, mid_[0])
    pair_start(sq, 0)
    hand_over(0, dx, dx_ref, dsend, drecv, at_d)
    rs_y_start(sd, 0)
    rs_z_start(sq, 0)
    rs_y_start(so, 0)
    rs_x_start(sq, 1)
    rs_y_start(sgu, 0)
    for k in (sd, so, sgu, sq):
        rs_end_start(k, 1)
    rs_x_start(sd, 0)
    rs_x_start(so, 0)
    rs_y_start(sq, 0)
    rs_x_start(sgu, 0)
    for k in (sd, so, sgu, sq):
        rs_end(k, 1)
    rs_x_start(sq, 0)
    for k in (sd, so, sgu, sq):
        rs_end_start(k, 0)
    for k in (sd, so, sgu, sq):
        rs_end(k, 0)
    for k in (sd, so, sgu, sq):
        pair_sent(k, 0)
    dkv_sent(0)
    rs_sent()
    hand_over_end(out_ref, osend, orecv, at_o)
    hand_over_end(dx_ref, dsend, drecv, at_d)
    assert used[0] <= SEMS, used[0]


SEMS = 400


def scratch():
    v = lambda *shape: pltpu.VMEM(shape, bf16)
    w = lambda *shape: pltpu.VMEM(shape, f32)
    widths = (FF, QKV, OUT)
    return [
        *[v(2, SIDE, PAD, n) for n in widths],
        *[v(2, SIDE, BAND, n) for n in (GU, QKV, OUT)], v(2, SIDE, SIDE, FROWS, D),
        v(2, SHARDS * TOK, 384), v(2, SHARDS - 1, TOK, 384),
        w(GROUP, SHARDS * TOK), w(GROUP, 128), w(GROUP, 128),
        w(2, TOK, D), v(2, TOK, D), v(2, HEADS, TOK, 64), v(2, HEADS, TOK, 64),
        w(2, KV_HEADS, GROUP, 1), w(2, TOK, D), v(2, TOK, D), w(2, TOK, GU),
        v(TOK, D), v(HEADS, TOK, 64), w(KV_HEADS, GROUP, 1), w(HEADS, TOK, 64), w(TOK, 384),
        w(TOK, D), v(TOK, D),
        *[v(SIDE, BAND, n) for n in (GU, QKV, OUT)], v(SIDE, SIDE, FROWS, D), v(SIDE, BAND, FF),
        *[v(3, BAND, n) for n in widths], v(3, SIDE, FROWS, D),
        *[v(SIDE, PAD, n) for n in widths], v(SIDE, FROWS, D),
        *[v(3, PAD, n) for n in widths], v(3, FROWS, D),
        *[v(PAD, n) for n in widths], v(FROWS, D),
        *[v(3, PAD, n) for n in widths], v(3, FROWS, D),
        v(2, PAD, FF), v(PAD, QKV), v(PAD, OUT), v(FROWS, D),
        v(2, PAD, FF), v(PAD, QKV), v(PAD, OUT), v(FROWS, D),
        v(D, TOK), v(D, TOK), w(D, TOK), w(D, TOK),
        v(PAD, FF), w(TOK, 128), w(TOK, 128),
        pltpu.SemaphoreType.DMA((SEMS,)), pltpu.SemaphoreType.DMA((SEMS,)),
        pltpu.SemaphoreType.REGULAR((32,)),
    ]


def kernel(*refs):
    body(*refs)


def spread(
    out_in, dx_in, gu_in, q_in, o_in, d_in,
    out_ref, dx_ref, gq_ref, gk_ref, gv_ref, go_ref, gg_ref, gu_ref, gd_ref, ga_ref, gf_ref,
):
    out_ref[...] = out_in[...]
    dx_ref[...] = dx_in[...]
    q = q_in[...].astype(f32)
    gq_ref[:, 0, :] = q[0:ROWS, 0:576]
    gk_ref[:, 0, :] = q[0:ROWS, 576:768]
    gv_ref[:, 0, :] = q[0:ROWS, 768:960]
    go_ref[:, 0, :] = o_in[...].astype(f32)[0:ROWS, 0:D]
    gg_ref[:, 0, :] = gu_in[0].astype(f32)[0:ROWS]
    gu_ref[:, 0, :] = gu_in[1].astype(f32)[0:ROWS]
    gd_ref[0] = d_in[...].astype(f32)
    row = lax.broadcasted_iota(jnp.int32, (PAD, 128), 0)
    lane = lax.broadcasted_iota(jnp.int32, (PAD, 128), 1)
    rows = dot_tn(q_in[:, 896:1024], jnp.where(row == lane, 1.0, 0.0).astype(bf16))
    ga_ref[...] = rows[64:65, 0:ROWS]
    gf_ref[...] = rows[65:66, 0:ROWS]


def angle_tables():
    half = HEAD_DIM // 2
    inverse = np.float64(rope_base) ** (-(np.arange(half) * 2.0 / HEAD_DIM))

    def table(positions):
        angles = np.tile(positions[:, None] * inverse[None, :], (1, 4))
        return jnp.asarray(np.concatenate([np.cos(angles), np.sin(angles)], axis=1).astype(np.float32))

    firsts = np.repeat(np.arange(SHARDS) * TOK, 8)
    return table(np.arange(TOK)), table(firsts).reshape(SHARDS, 8, 256)


def local(
    inputs, out_grad, w_query, w_key, w_value, w_out, w_gate, w_up, w_down, gain_attn, gain_ffn
):
    near, far = angle_tables()
    whole = pl.BlockSpec(memory_space=pltpu.VMEM)
    turned = ((1, 2, 1, D, TOK), bf16), ((1, 2, 1, D, TOK), f32)
    shapes = turned + (((2, PAD, FF), bf16), ((PAD, QKV), bf16), ((PAD, OUT), bf16), ((FROWS, D), bf16))
    res = pl.pallas_call(
        kernel,
        out_shape=[jax.ShapeDtypeStruct(s, t) for s, t in shapes],
        in_specs=[whole] * 13,
        out_specs=[whole] * len(shapes),
        scratch_shapes=scratch(),
        compiler_params=pltpu.CompilerParams(
            collective_id=0, has_side_effects=True, vmem_limit_bytes=63 * 1024 * 1024
        ),
        name="two_layers",
    )(
        jnp.swapaxes(inputs, 2, 3), jnp.swapaxes(out_grad, 2, 3), w_query, w_key, w_value, w_out,
        w_gate, w_up, w_down, gain_attn, gain_ffn, near, far,
    )
    rows = lambda n: ((ROWS, 1, n), f32)
    shapes = turned + (
        rows(576), rows(192), rows(192), rows(D), rows(FF), rows(FF), ((1, FROWS, D), f32),
        ((1, ROWS), f32), ((1, ROWS), f32),
    )
    out, dx, *grads = pl.pallas_call(
        spread,
        out_shape=[jax.ShapeDtypeStruct(s, t) for s, t in shapes],
        in_specs=[whole] * 6,
        out_specs=[whole] * 11,
        name="spread",
    )(*res)
    grads[:6] = [jnp.swapaxes(g, 0, 1) for g in grads[:6]]
    return (jnp.swapaxes(out, 3, 4), jnp.swapaxes(dx, 3, 4), *grads)


def solution(mesh):
    return jax.shard_map(
        local,
        mesh=mesh,
        in_specs=(
            P(None, "replica", "shard", None),
            P(None, "replica", "shard", None),
            P("section", "shard", None),
            P("section", "shard", None),
            P("section", "shard", None),
            P("section", "shard", None),
            P("section", "shard", None),
            P("section", "shard", None),
            P("section", "shard", None),
            P("section", "shard"),
            P("section", "shard"),
        ),
        out_specs=(
            P("section", None, "replica", "shard", None),
            P("section", None, "replica", "shard", None),
            P("section", "shard", None),
            P("section", "shard", None),
            P("section", "shard", None),
            P("section", "shard", None),
            P("section", "shard", None),
            P("section", "shard", None),
            P("section", "shard", None),
            P("section", "shard"),
            P("section", "shard"),
        ),
        check_vma=False,
    )
```

```python
import functools

import jax
import jax.numpy as jnp
import numpy as np
from jax import lax
from jax.experimental import pallas as pl
from jax.experimental.pallas import tpu as pltpu
from jax.sharding import PartitionSpec as P

HEADS = 9
KV_HEADS = 3
HEAD_DIM = 64
D = 576
FF = 1536
TOK = 128
SHARDS = 16
SIDE = 4
ROWS = 36
PAD = 48
BAND = SIDE * ROWS
FROWS = 96
FBAND = SIDE * FROWS
PART = 2 * FBAND
GU = 2 * FF
QKV = 1024
OUT = 640
CHUNK = 512
HALVES = {1: pl.ds(0, 80), 3: pl.ds(80, BAND - 80)}
GROUP = 3 * TOK

bf16 = jnp.bfloat16
f32 = jnp.float32
MESH = pl.DeviceIdType.MESH
epsilon = 1e-05
rope_base = 100000.0
score_scale = 0.125


def dot(a, b):
    return lax.dot_general(a, b, (((1,), (0,)), ((), ())), preferred_element_type=f32)


def dot_nt(a, b):
    return lax.dot_general(a, b, (((1,), (1,)), ((), ())), preferred_element_type=f32)


def dot_tn(a, b):
    return lax.dot_general(a, b, (((0,), (0,)), ((), ())), preferred_element_type=f32)


def factor_of(v):
    return lax.rsqrt(jnp.mean(v * v, axis=-1, keepdims=True) + epsilon)


def norm_back(v, r, gain, up):
    scaled = gain * up
    return r * scaled - v * (r * r * r) * jnp.mean(scaled * v, axis=-1, keepdims=True)


def half_swap(u):
    width = u.shape[1]
    lane = lax.broadcasted_iota(jnp.int32, u.shape, 1)
    first = lax.rem(lane, HEAD_DIM) < HEAD_DIM // 2
    return jnp.where(first, pltpu.roll(u, width - 32, 1), pltpu.roll(u, 32, 1))


def body(
    x_ref, dy_ref, wq_ref, wk_ref, wv_ref, wo_ref, wg_ref, wu_ref, wd_ref, ga_ref, gf_ref, near_ref, far_ref,
    out_ref, dx_ref, fin_gu, fin_q, fin_o, fin_d,
    stage_gu, stage_q, stage_o, w_gu, w_q, w_o, w_d, kv, dkv_r, scr, mx, acc,
    xs_, a_, q8_, o_, lse_, mid_, bn_, gu_,
    dyb_, dob_, delta_, dq_, dkv_acc, acc2, gain_term,
    g_gu, g_q, g_o, g_d, xg,
    zr_gu, zr_q, zr_o, zr_d, ys_gu, ys_q, ys_o, ys_d, yr_gu, yr_q, yr_o, yr_d,
    xs_gu, xs_q, xs_o, xs_d, xr_gu, xr_q, xr_o, xr_d, fs_gu, fs_q, fs_o, fs_d, fr_gu, fr_q, fr_o, fr_d,
    osend, orecv, dsend, drecv, pack_gu, cos_ref, sin_ref,
    ssem, rsem, credit,
):
    sec = lax.axis_index("section")
    sh = lax.axis_index("shard")
    rep = lax.axis_index("replica")
    z, y = lax.div(sh, SIDE), lax.rem(sh, SIDE)
    core = lax.rem(rep, 2)
    sib = rep + 1 - 2 * core
    far = lax.rem(rep + 2, 4)
    used = [0]

    def take(n):
        at = used[0]
        used[0] += n
        return at

    def copy(src, dst, at, to=None, **dev):
        return pltpu.make_async_remote_copy(
            src_ref=src, dst_ref=dst, send_sem=ssem.at[at], recv_sem=rsem.at[at if to is None else to],
            device_id=dev, device_id_type=MESH,
        )

    def arrived(dst, at):
        copy(dst, dst, at, shard=sh).wait_recv()

    def sent(src, at):
        copy(src, src, at, shard=sh).wait_send()

    def y_peer(d):
        return z * SIDE + lax.rem(y + d, SIDE)

    def z_peer(d):
        return lax.rem(z + d, SIDE) * SIDE + y

    def z_from(d):
        return lax.rem(z + SIDE - d, SIDE)

    def y_from(d):
        return lax.rem(y + SIDE - d, SIDE)

    last = pl.ds(pl.multiple_of(lax.div(sh, SIDE) * CHUNK, CHUNK), CHUNK)
    for l in range(2):
        kv[l, last, :] = jnp.zeros((CHUNK, 384), bf16)
    def padded(ref, value):
        ref[0:32] = value[0:32]
        ref[32:PAD] = jnp.concatenate(
            [value[32:ROWS].astype(f32), jnp.zeros((PAD - ROWS, value.shape[1]), f32)], axis=0
        ).astype(bf16)

    @pl.when(core == 1)
    def _():
        row16 = lax.broadcasted_iota(jnp.int32, (16, ROWS), 0)
        gain16 = jnp.where(
            row16 == 0, ga_ref[...].astype(f32), jnp.where(row16 == 1, gf_ref[...].astype(f32), 0.0)
        ).astype(bf16)
        place = lax.broadcasted_iota(jnp.int32, (16, 64), 0) == lax.broadcasted_iota(jnp.int32, (16, 64), 1)
        gain_cols = dot_tn(gain16, jnp.where(place, 1.0, 0.0).astype(bf16))
        whole = jnp.concatenate(
            [wq_ref[0].astype(f32), wk_ref[0].astype(f32), wv_ref[0].astype(f32), gain_cols], axis=1
        ).astype(bf16)
        padded(stage_q.at[sec, y], whole)
        whole = jnp.concatenate([wo_ref[0].astype(f32), jnp.zeros((ROWS, OUT - D), f32)], axis=1).astype(bf16)
        padded(stage_o.at[sec, y], whole)
        w_d[sec, z, y] = wd_ref[0]

    for c in range(2):
        @pl.when((core == 0) & (sec == c))
        def _():
            padded(stage_gu.at[sec, y], (wg_ref, wu_ref)[c][0])
            padded(pack_gu, (wg_ref, wu_ref)[1 - c][0])

    cos1, sin1 = near_ref[:, 0:128], near_ref[:, 128:256]
    first = far_ref[sh]
    cos2, sin2 = first[0:1, 0:128], first[0:1, 128:256]
    low = lax.rem(lax.broadcasted_iota(jnp.int32, (TOK, 128), 1), HEAD_DIM) < HEAD_DIM // 2
    cos_ref[...] = cos1 * cos2 - sin1 * sin2
    sine = sin1 * cos2 + cos1 * sin2
    sin_ref[...] = jnp.where(low, -sine, sine)
    xs_[0] = x_ref[sec, 0].astype(f32).T

    barrier = pltpu.get_barrier_semaphore()

    def greet(d, c):
        pl.semaphore_signal(barrier, inc=1, device_id={"shard": lax.rem(sh + d, SHARDS)}, device_id_type=MESH)
        return c

    lax.fori_loop(1, SHARDS, greet, 0)
    pl.semaphore_signal(barrier, inc=1, device_id={"replica": sib}, device_id_type=MESH)
    pl.semaphore_signal(barrier, inc=1, device_id={"replica": far}, device_id_type=MESH)
    pl.semaphore_signal(barrier, inc=1, device_id={"section": 1 - sec}, device_id_type=MESH)
    pl.semaphore_signal(barrier, inc=1, device_id={"section": 1 - sec, "replica": far}, device_id_type=MESH)
    pl.semaphore_wait(barrier, SHARDS - 1 + 4)

    mine = pl.ds(pl.multiple_of(sec * FF, 128), FF)
    theirs = pl.ds(pl.multiple_of((1 - sec) * FF, 128), FF)

    class Gather:
        def __init__(self, owner, send, stage, w, cols, width):
            self.owner, self.send, self.stage, self.w, self.width = owner, send, stage, w, width
            self.cols = cols
            self.at_x = take(1)
            self.at_y = [take(3) for _ in range(2)]
            self.at_z = [take(4) for _ in range(2)]
            self.at_f = [take(4) for _ in range(2)]

        def band(self, l, j):
            return self.w.at[l, j, :, self.cols]

    kgu = Gather(0, pack_gu, stage_gu, w_gu, mine, FF)
    kq = Gather(1, stage_q.at[sec, y], stage_q, w_q, pl.ds(0, QKV), QKV)
    ko = Gather(1, stage_o.at[sec, y], stage_o, w_o, pl.ds(0, OUT), OUT)
    at_xd = take(1)
    at_dz = [take(3) for _ in range(2)]
    at_dy = [take(3) for _ in range(2)]
    at_df = [take(1) for _ in range(2)]
    at_swap = [take(4) for _ in range(2)]
    at_sf = [take(4) for _ in range(2)]

    def x_start(k):
        @pl.when(core == k.owner)
        def _():
            copy(k.send, k.stage.at[sec, y], k.at_x, section=1 - sec).start()

    def dx_start():
        @pl.when(core == 1)
        def _():
            copy(w_d.at[sec, z, y], w_d.at[sec, z, y], at_xd, section=1 - sec).start()

    def y_start(k, l):
        @pl.when(core == k.owner)
        def _():
            own = k.stage.at[l, y]

            @pl.when(sec != l)
            def _():
                arrived(own, k.at_x)

            for d in (2, 1, 3):
                copy(own, own, k.at_y[l] + d - 1, shard=y_peer(d)).start()

    def dz_start(l):
        @pl.when(core == 1)
        def _():
            own = w_d.at[l, z, y]

            @pl.when(sec != l)
            def _():
                arrived(own, at_xd)

            for d in (2, 1, 3):
                copy(own, own, at_dz[l] + d - 1, shard=z_peer(d)).start()

    def z_start(k, l):
        @pl.when(core == k.owner)
        def _():
            for d in range(1, SIDE):
                arrived(k.stage.at[l, y_from(d)], k.at_y[l] + d - 1)
            own = k.band(l, z)
            for at in range(0, k.width, 128):
                parts = [k.stage[l, j, :, at : at + 128][0:ROWS].astype(f32) for j in range(SIDE)]
                own[:, at : at + 128] = jnp.concatenate(parts, axis=0).astype(bf16)
            for d in (1, 3) if ring(k, l) else (2, 1, 3):
                copy(own, own, k.at_z[l] + d - 1, shard=z_peer(d)).start()
            pass_on(k, l, z, 0)

    def ring(k, l):
        return not (k is kq and l == 0)

    def pass_on(k, l, j, d):
        got = k.band(l, j)
        copy(got, got, k.at_f[l] + d, replica=sib).start()
        if k is kgu:
            copy(got, got, at_swap[l] + j, **swap_to(j)).start()

    def z_mid(k, l):
        @pl.when(core == k.owner)
        def _():
            for d in (1, 3):
                got = k.band(l, z_from(d))
                arrived(got, k.at_z[l] + d - 1)
                half = got.at[HALVES[d]]
                copy(half, half, k.at_z[l] + (1 if d == 1 else 3), shard=z_peer(d)).start()
                pass_on(k, l, z_from(d), d)

    def dy_start(l):
        @pl.when(core == 1)
        def _():
            for d in range(1, SIDE):
                arrived(w_d.at[l, z_from(d), y], at_dz[l] + d - 1)
            own = w_d.at[l, :, y]
            for d in (2, 1, 3):
                copy(own, own, at_dy[l] + d - 1, shard=y_peer(d)).start()

    def z_end(k, l):
        @pl.when(core == k.owner)
        def _():
            if ring(k, l):
                got = k.band(l, z_from(2))
                arrived(got.at[HALVES[1]], k.at_z[l] + 1)
                arrived(got.at[HALVES[3]], k.at_z[l] + 3)
                pass_on(k, l, z_from(2), 2)
            else:
                for d in (1, 3, 2):
                    arrived(k.band(l, z_from(d)), k.at_z[l] + d - 1)
                    pass_on(k, l, z_from(d), d)

    def swap_to(j):
        if isinstance(j, int):
            return {"section": 1 - sec} if j < 2 else {"section": 1 - sec, "replica": far}
        return {"section": 1 - sec, "replica": jnp.where(j < 2, rep, far)}

    def swap_end(l):
        @pl.when(core == 0)
        def _():
            for j in range(SIDE):
                got = w_gu.at[l, j, :, theirs]
                arrived(got, at_swap[l] + j)
                copy(got, got, at_sf[l] + j, replica=sib).start()

    def d_forward_on(l):
        @pl.when(core == 1)
        def _():
            for d in range(1, SIDE):
                arrived(w_d.at[l, :, y_from(d)], at_dy[l] + d - 1)
            copy(w_d.at[l], w_d.at[l], at_df[l], replica=sib).start()

    def gather_end(k, l):
        @pl.when(core != k.owner)
        def _():
            arrived(k.band(l, z), k.at_f[l])
            for d in range(1, SIDE):
                arrived(k.band(l, z_from(d)), k.at_f[l] + d)
            if k is kgu:
                for j in range(SIDE):
                    arrived(w_gu.at[l, j, :, theirs], at_sf[l] + j)

    def d_gather_end(l):
        @pl.when(core == 0)
        def _():
            arrived(w_d.at[l], at_df[l])

    def gather_sent():
        for l in range(2):
            for k in (kgu, kq, ko):
                @pl.when(core == k.owner)
                def _():
                    @pl.when(sec == l)
                    def _():
                        sent(k.send, k.at_x)

                    for d in range(1, SIDE):
                        sent(k.stage.at[l, y], k.at_y[l] + d - 1)
                        if not ring(k, l) or d != 2:
                            sent(k.band(l, z), k.at_z[l] + d - 1)
                        sent(k.band(l, z), k.at_f[l] + d)
                    if ring(k, l):
                        sent(k.band(l, z).at[HALVES[1]], k.at_z[l] + 1)
                        sent(k.band(l, z).at[HALVES[3]], k.at_z[l] + 3)
                    sent(k.band(l, z), k.at_f[l])
                    if k is kgu:
                        for j in range(SIDE):
                            sent(k.band(l, j), at_swap[l] + j)
                            sent(k.band(l, j), at_sf[l] + j)

            @pl.when(core == 1)
            def _():
                @pl.when(sec == l)
                def _():
                    sent(w_d.at[0, z, y], at_xd)

                for d in range(1, SIDE):
                    sent(w_d.at[l, z, y], at_dz[l] + d - 1)
                    sent(w_d.at[l, :, y], at_dy[l] + d - 1)
                sent(w_d.at[l], at_df[l])

    at_kv = [take(SHARDS) for _ in range(2)]
    at_kvr = [take(4) for _ in range(2)]
    at_dkv = [take(SHARDS) for _ in range(2)]
    at_dky = [take(4) for _ in range(2)]
    tokens = pl.ds(pl.multiple_of(sh * TOK, TOK), TOK)
    twice = 2 * SIDE

    def block(l, j):
        return kv.at[l, pl.ds(pl.multiple_of(j * TOK, TOK), TOK)]

    def relayed(j):
        gap = lax.div(j, SIDE) - z
        return ((gap == 2) | (gap == -2)) & (lax.rem(j, SIDE) != y)

    def kv_start(l):
        own = kv.at[l, tokens]

        def go(d, c):
            @pl.when(jnp.logical_not(relayed(sh + d)))
            def _():
                copy(own, own, at_kv[l] + d, shard=sh + d).start()

            return c

        lax.fori_loop(1, SHARDS - sh, go, 0)

    def kv_wait(l):
        @pl.when(z >= 2)
        def _():
            passing = block(l, sh - twice)
            arrived(passing, at_kv[l] + twice)
            for e in range(1, SIDE):
                yt = lax.rem(y + e, SIDE)
                copy(passing, passing, at_kvr[l] + e, to=at_kv[l] + twice + yt - y, shard=y_peer(e)).start()

        def go(d, c):
            @pl.when(d != twice)
            def _():
                arrived(block(l, sh - d), at_kv[l] + d)

            return c

        lax.fori_loop(1, sh + 1, go, 0)

    def kv_sent(l):
        def go(d, c):
            @pl.when(jnp.logical_not(relayed(sh + d)))
            def _():
                sent(kv.at[l, tokens], at_kv[l] + d)

            return c

        lax.fori_loop(1, SHARDS - sh, go, 0)

        @pl.when(z >= 2)
        def _():
            for e in range(1, SIDE):
                sent(kv.at[l, tokens], at_kvr[l] + e)

    def dkv_start(l, j):
        away = relayed(j)

        @pl.when(away)
        def _():
            e = lax.rem(lax.rem(j, SIDE) - y + SIDE, SIDE)
            copy(
                block(l, j), dkv_r.at[l, twice - 1 + e], at_dkv[l] + sh - j,
                to=at_dky[l] + e, shard=z * SIDE + lax.rem(j, SIDE),
            ).start()

        @pl.when(jnp.logical_not(away) & (sh - j != twice))
        def _():
            copy(block(l, j), dkv_r.at[l, sh - j - 1], at_dkv[l] + sh - j, shard=j).start()

    def dkv_relay(l):
        @pl.when(z >= 2)
        def _():
            passing = block(l, sh - twice)
            for e in range(1, SIDE):
                arrived(dkv_r.at[l, twice - 1 + e], at_dky[l] + e)
            tot = passing[...].astype(f32)
            for e in range(1, SIDE):
                tot += dkv_r[l, twice - 1 + e].astype(f32)
            passing[...] = tot.astype(bf16)
            copy(passing, dkv_r.at[l, twice - 1], at_dkv[l] + twice, shard=sh - twice).start()

    def dkv_sent(l):
        def go(d, c):
            sent(kv.at[l, pl.ds(0, TOK)], at_dkv[l] + d)
            return c

        lax.fori_loop(1, sh + 1, go, 0)

    def gains(l):
        tile = w_q[l, :, :, 896:1024].reshape(D, 128)
        row = lax.broadcasted_iota(jnp.int32, (8, 128), 0)
        lane = lax.broadcasted_iota(jnp.int32, (8, 128), 1)
        pick = jnp.where(lane == row + 64, 1.0, 0.0).astype(bf16)
        both = dot_nt(pick, tile)
        return both[0:1], both[1:2]

    nfull = lax.div(sh, SIDE)

    def causal():
        row = lax.broadcasted_iota(jnp.int32, (GROUP, CHUNK), 0)
        col = lax.broadcasted_iota(jnp.int32, (GROUP, CHUNK), 1)
        return col <= lax.rem(sh, SIDE) * TOK + lax.rem(row, TOK)

    def keys_at(c):
        return pl.ds(pl.multiple_of(c * CHUNK, CHUNK), CHUNK)

    def tables():
        cos = jnp.concatenate([cos_ref[...]] * 6, axis=1)
        sin = jnp.concatenate([sin_ref[...]] * 6, axis=1)
        return cos, sin

    def project_in(l):
        x = xs_[l]
        gain, _ = gains(l)
        a = (x * factor_of(x) * gain).astype(bf16)
        a_[l] = a
        qkv = dot(a, w_q[l].reshape(D, QKV))
        cos, sin = tables()
        u = qkv[:, 0:768]
        turned = u * cos + half_swap(u) * sin
        for h in range(HEADS):
            head = turned[:, h * 64 : h * 64 + 64].astype(bf16)
            q8_[l, h] = (head.astype(f32) * score_scale).astype(bf16)
        block = jnp.concatenate([turned[:, 576:768], qkv[:, 768:960]], axis=1).astype(bf16)
        kv[l, tokens] = block

    def attend(l, g):
        if True:
            q = q8_[l, 3 * g : 3 * g + 3].reshape(GROUP, 64)

            def keep(c, s):
                scr[:, keys_at(c)] = s
                top = jnp.maximum(
                    jnp.maximum(s[:, 0:128], s[:, 128:256]), jnp.maximum(s[:, 256:384], s[:, 384:512])
                )
                mx[...] = jnp.maximum(mx[...], top)

            def scores(c):
                k = kv[l, keys_at(c), :][:, g * 64 : g * 64 + 64]
                return dot_nt(q, k)

            mx[...] = jnp.full_like(mx, -1e30)

            def first(c, carry):
                keep(c, scores(c))
                return carry

            lax.fori_loop(0, nfull, first, 0)
            keep(nfull, jnp.where(causal(), scores(nfull), -1e30))
            peak = jnp.max(mx[...], axis=1, keepdims=True)
            acc[...] = jnp.zeros_like(acc)

            def second(c, carry):
                p = jnp.exp(scr[:, keys_at(c)] - peak).astype(bf16)
                v = kv[l, keys_at(c), :][:, 192 + g * 64 : 256 + g * 64]
                v = jnp.concatenate([v, jnp.ones_like(v)], axis=1)
                acc[...] += dot(p, v)
                return carry

            lax.fori_loop(0, nfull + 1, second, 0)
            total = acc[:, 64:65]
            mixed = (acc[:, 0:64] / total).astype(bf16)
            lse_[l, g] = peak + jnp.log(total)
            o_[l, 3 * g : 3 * g + 3] = mixed.reshape(3, TOK, 64)

    def heads_in(ref):
        return jnp.concatenate([ref[h] for h in range(HEADS)], axis=1)

    def after_attention(l):
        o = heads_in(o_.at[l])
        mid = xs_[l] + dot(o, w_o[l, :, :, 0:D].reshape(D, D))
        mid_[l] = mid
        _, gain = gains(l)
        bn_[l] = (mid * factor_of(mid) * gain).astype(bf16)
        acc2[...] = mid

        def tile(t, c):
            gcols = pl.ds(pl.multiple_of(t * PART, 128), PART)
            ucols = pl.ds(pl.multiple_of(FF + t * PART, 128), PART)
            bn = bn_[l]
            gt = dot(bn, w_gu[l, :, :, gcols].reshape(D, PART))
            up = dot(bn, w_gu[l, :, :, ucols].reshape(D, PART))
            gu_[l, :, gcols] = gt
            gu_[l, :, ucols] = up
            hid = (gt * jax.nn.sigmoid(gt) * up).astype(bf16)
            acc2[...] += dot(hid, w_d[l, pl.ds(2 * t, 2)].reshape(PART, D))
            return c

        lax.fori_loop(0, FF // PART, tile, 0)
        return acc2[...]

    def ffn_back(l, dy):
        dyb_[...] = dy.astype(bf16)
        acc2[...] = jnp.zeros_like(acc2)

        def tile(t, c):
            gcols = pl.ds(pl.multiple_of(t * PART, 128), PART)
            ucols = pl.ds(pl.multiple_of(FF + t * PART, 128), PART)
            dyb = dyb_[...]
            bn = bn_[l]
            wd = w_d[l, pl.ds(2 * t, 2)].reshape(PART, D)
            dhid = dot_nt(dyb, wd).astype(bf16).astype(f32)
            gt, up = gu_[l, :, gcols], gu_[l, :, ucols]
            s = jax.nn.sigmoid(gt)
            hid = (gt * s * up).astype(bf16)
            g_d[pl.ds(2 * t, 2)] = dot_tn(hid, dyb).astype(bf16).reshape(2, SIDE, FROWS, D)
            dgt = (dhid * up * s * (1.0 + gt * (1.0 - s))).astype(bf16)
            dup = (dhid * gt * s).astype(bf16)
            g_gu[:, :, gcols] = dot_tn(bn, dgt).astype(bf16).reshape(SIDE, BAND, PART)
            g_gu[:, :, ucols] = dot_tn(bn, dup).astype(bf16).reshape(SIDE, BAND, PART)
            acc2[...] += dot_nt(dgt, w_gu[l, :, :, gcols].reshape(D, PART))
            acc2[...] += dot_nt(dup, w_gu[l, :, :, ucols].reshape(D, PART))
            return c

        lax.fori_loop(0, FF // PART, tile, 0)
        dbn = acc2[...]
        mid = mid_[l]
        r = factor_of(mid)
        _, gain = gains(l)
        gain_term[...] = (dbn * mid * r).astype(bf16)
        return dy + norm_back(mid, r, gain, dbn)

    def out_back(l, dmid):
        dmb = dmid.astype(bf16)
        o = heads_in(o_.at[l])
        g_o[...] = jnp.concatenate(
            [dot_tn(o, dmb), jnp.zeros((D, 64), f32)], axis=1
        ).astype(bf16).reshape(SIDE, BAND, 640)
        dob = dot_nt(dmb, w_o[l, :, :, 0:D].reshape(D, D)).astype(bf16)
        for h in range(HEADS):
            do_h = dob[:, h * 64 : h * 64 + 64]
            dq_[h] = jnp.zeros((TOK, 64), f32)
            dob_[h] = do_h

    def attention_back(l, part):
        for g in range(KV_HEADS):
            do = dob_[3 * g : 3 * g + 3].reshape(GROUP, 64).astype(f32)
            og = o_[l, 3 * g : 3 * g + 3].reshape(GROUP, 64).astype(f32)
            if part == 0:
                delta_[g] = jnp.sum(do * og, axis=1, keepdims=True)

        def chunk(c, masked):
            kvb = kv[l, keys_at(c), :]
            dks, dvs = [], []
            for g in range(KV_HEADS):
                q = q8_[l, 3 * g : 3 * g + 3].reshape(GROUP, 64)
                do = dob_[3 * g : 3 * g + 3].reshape(GROUP, 64)
                k = kvb[:, g * 64 : g * 64 + 64]
                v = kvb[:, 192 + g * 64 : 256 + g * 64]
                s = dot_nt(q, k)
                if masked:
                    s = jnp.where(causal(), s, -1e30)
                p = jnp.exp(s - lse_[l, g])
                ds = (p * (dot_nt(do, v) - delta_[g])).astype(bf16)
                dq_[3 * g : 3 * g + 3] += dot(ds, k).reshape(3, TOK, 64)
                dks.append(dot_tn(ds, q))
                dvs.append(dot_tn(p.astype(bf16), do))
            kv[l, keys_at(c), :] = jnp.concatenate(dks + dvs, axis=1).astype(bf16)

        def full(c, carry):
            chunk(c, False)
            for i in range(SIDE):
                dkv_start(l, c * SIDE + i)
            return carry

        def rest(j, carry):
            dkv_start(l, j)
            return carry

        if part == 0:
            lax.fori_loop(0, nfull, full, 0)
        else:
            chunk(nfull, True)
            lax.fori_loop(nfull * SIDE, sh, rest, 0)

    def finish_back(l, dmid_at):
        dkv_acc[...] = kv[l, tokens, :].astype(f32)

        def add(d, c):
            @pl.when(jnp.logical_not(relayed(sh + d)))
            def _():
                arrived(dkv_r.at[l, d - 1], at_dkv[l] + d)
                dkv_acc[...] += dkv_r[l, d - 1].astype(f32)

            return c

        lax.fori_loop(1, SHARDS - sh, add, 0)
        dkv = dkv_acc[...]
        cos, sin = tables()
        dq = jnp.concatenate([dq_[h] for h in range(HEADS)], axis=1) * score_scale
        u = jnp.concatenate([dq, dkv[:, 0:192]], axis=1)
        back = u * cos - half_swap(u) * sin
        dqkv = jnp.concatenate([back, dkv[:, 192:384], jnp.zeros((TOK, 64), f32)], axis=1).astype(bf16)
        a = a_[l]
        gq = dot_tn(a, dqkv)
        da = dot_nt(dqkv, w_q[l].reshape(D, QKV))
        x = xs_[l]
        r = factor_of(x)
        gain, _ = gains(l)
        lane = lax.broadcasted_iota(jnp.int32, (TOK, 128), 1)
        e0 = jnp.where(lane == 64, 1.0, 0.0).astype(bf16)
        e1 = jnp.where(lane == 65, 1.0, 0.0).astype(bf16)
        cols = dot_tn((da * x * r).astype(bf16), e0) + dot_tn(gain_term[...], e1)
        g_q[:, :, 0:896] = gq[:, 0:896].astype(bf16).reshape(SIDE, BAND, 896)
        g_q[:, :, 896:1024] = (gq[:, 896:1024] + cols).astype(bf16).reshape(SIDE, BAND, 128)
        return dmid_at + norm_back(x, r, gain, da)

    class Sum:
        def __init__(self, name, owner, w, cols, g, zr, ys, yr, xs, xr, fs, fr, width):
            self.name, self.owner, self.w, self.cols, self.g = name, owner, w, cols, g
            self.zr, self.ys, self.yr, self.xs, self.xr, self.fs, self.fr = zr, ys, yr, xs, xr, fs, fr
            self.width = width
            self.at = [take(12) for _ in range(2)]
            self.free = credits(2)
            self.again_z, self.again_y = credits(1), credits(1)

            first_y = name == "d"
            self.i1, self.peer1 = (y, y_peer) if first_y else (z, z_peer)
            self.i2, self.peer2 = (z, z_peer) if first_y else (y, y_peer)

        def band(self, l, j):
            return self.w.at[l, :, j] if self.name == "d" else self.w.at[l, j, :, self.cols]

    granted = [0]

    def credits(n):
        at = granted[0]
        granted[0] += n
        return at

    sgu = Sum("gu", 0, w_gu, mine, g_gu, zr_gu, ys_gu, yr_gu, xs_gu, xr_gu, fs_gu, fr_gu, FF)
    sq = Sum("q", 1, w_q, pl.ds(0, QKV), g_q, zr_q, ys_q, yr_q, xs_q, xr_q, fs_q, fr_q, QKV)
    so = Sum("o", 1, w_o, pl.ds(0, OUT), g_o, zr_o, ys_o, yr_o, xs_o, xr_o, fs_o, fr_o, OUT)
    sd = Sum("d", 1, w_d, None, g_d, zr_d, ys_d, yr_d, xs_d, xr_d, fs_d, fr_d, D)
    at_rswap = [take(4) for _ in range(2)]
    swap_again = credits(1)

    def pair_start(k, l):
        pl.semaphore_signal(credit.at[k.free + l], inc=1, device_id={"replica": sib}, device_id_type=MESH)
        pl.semaphore_wait(credit.at[k.free + l], 1)

        @pl.when(core != k.owner)
        def _():
            copy(k.g, k.w.at[l], k.at[l], replica=sib).start()

    def pair_sent(k, l):
        @pl.when(core != k.owner)
        def _():
            sent(k.g, k.at[l])

    def add_into(dst, src, width):
        step = 256 if width % 256 == 0 else 128

        def add(t, c):
            cols = pl.ds(pl.multiple_of(t * step, 128), step)
            dst[:, cols] = (dst[:, cols].astype(f32) + src[:, cols].astype(f32)).astype(bf16)
            return c

        lax.fori_loop(0, width // step, add, 0)

    def rs_swap_start(l):
        @pl.when(core == 0)
        def _():
            arrived(w_gu.at[l], sgu.at[l])
            if l == 0:
                pl.semaphore_wait(credit.at[swap_again], 2)
            for j in (0, 2, 1, 3):
                src = w_gu.at[l, j, :, theirs]
                add_into(src, g_gu.at[j, :, theirs], FF)
                copy(src, xg.at[j], at_rswap[l] + j, **swap_to(j)).start()
            for j in range(SIDE):
                add_into(w_gu.at[l, j, :, mine], g_gu.at[j, :, mine], FF)

    def rs_z_start(k, l):
        @pl.when(core == k.owner)
        def _():
            if k is not sgu:
                arrived(k.w.at[l], k.at[l])
            if l == 0:
                pl.semaphore_wait(credit.at[k.again_z], 3)
            for d in (2, 1, 3, 0):
                zt = lax.rem(k.i1 + d, SIDE)
                part = k.band(l, zt)
                if k is sd:
                    part[...] = (part[...].astype(f32) + k.g[:, zt].astype(f32)).astype(bf16)
                elif k is sgu:
                    arrived(xg.at[zt], at_rswap[l] + zt)
                    add_into(part, xg.at[zt], FF)
                else:
                    add_into(part, k.g.at[zt], k.width)
                if d:
                    copy(part, k.zr.at[d - 1], k.at[l] + d, shard=k.peer1(d)).start()
            if k is sgu and l == 1:
                for j in (0, 2):
                    pl.semaphore_signal(
                        credit.at[swap_again], inc=1, device_id=swap_to(j), device_id_type=MESH
                    )

    def rs_y_start(k, l):
        @pl.when(core == k.owner)
        def _():
            for d in range(1, SIDE):
                arrived(k.zr.at[d - 1], k.at[l] + d)
            if l == 0:
                for d in range(1, SIDE):
                    sent(k.yr.at[0], k.at[1] + 3 + d)
            own = k.band(l, k.i1)
            if k is sd:
                tot = own[...].astype(f32)
                for d in range(3):
                    tot += k.zr[d].astype(f32)
                k.ys[...] = tot.astype(bf16)
            else:
                step = 256 if k.width % 256 == 0 else 128

                def add(t, c):
                    cols = pl.ds(pl.multiple_of(t * step, 128), step)
                    tot = own[:, cols].astype(f32)
                    for d in range(3):
                        tot += k.zr[d, :, cols].astype(f32)
                    for j in range(SIDE):
                        rows = tot[j * ROWS : j * ROWS + ROWS]
                        rows = jnp.concatenate([rows, jnp.zeros((PAD - ROWS, step), f32)], axis=0)
                        k.ys[j, :, cols] = rows.astype(bf16)
                    return c

                lax.fori_loop(0, k.width // step, add, 0)
            if l == 1:
                for d in range(1, SIDE):
                    pl.semaphore_signal(
                        credit.at[k.again_z], inc=1, device_id={"shard": k.peer1(d)}, device_id_type=MESH
                    )
            else:
                pl.semaphore_wait(credit.at[k.again_y], 3)
            for d in (2, 1, 3):
                yt = lax.rem(k.i2 + d, SIDE)
                copy(k.ys.at[yt], k.yr.at[d - 1], k.at[l] + 3 + d, shard=k.peer2(d)).start()

    def x_targets(l):
        for t in (1, 2, 3):
            other = 1 - sec if t >= 2 else sec
            where = {}
            if t >= 2:
                where["section"] = 1 - sec
            if t % 2:
                where["replica"] = far
            yield t, other == l, where

    def rs_x_start(k, l):
        @pl.when(core == k.owner)
        def _():
            for d in range(1, SIDE):
                arrived(k.yr.at[d - 1], k.at[l] + 3 + d)
            if l == 0:
                xs_sent(k, 1)
            tot = k.ys[k.i2].astype(f32)
            for d in range(3):
                tot += k.yr[d].astype(f32)
            k.xs[...] = tot.astype(bf16)
            if l == 1:
                for d in range(1, SIDE):
                    pl.semaphore_signal(
                        credit.at[k.again_y], inc=1, device_id={"shard": k.peer2(d)}, device_id_type=MESH
                    )
            for t, hit, where in x_targets(l):
                @pl.when(hit)
                def _():
                    copy(k.xs, k.xr.at[t - 1], k.at[l] + 6 + t, **where).start()

    def xs_sent(k, l):
        for t, hit, where in x_targets(l):
            @pl.when(hit)
            def _():
                sent(k.xs, k.at[l] + 6 + t)

    fins = {"gu": fin_gu, "q": fin_q, "o": fin_o, "d": fin_d}

    def rs_end_start(k, l):
        @pl.when((core == k.owner) & (sec == l))
        def _():
            for t in (1, 2, 3):
                arrived(k.xr.at[t - 1], k.at[l] + 6 + t)
            if k is sgu:
                own = k.xs[...].astype(f32) + k.xr[0].astype(f32)
                other = k.xr[1].astype(f32) + k.xr[2].astype(f32)
                k.fs[l] = own.astype(bf16)
                k.fs[1 - l] = other.astype(bf16)
                copy(k.fs, k.fr, k.at[l] + 10, replica=sib).start()
            else:
                tot = k.xs[...].astype(f32)
                for t in range(3):
                    tot += k.xr[t].astype(f32)
                k.fs[...] = tot.astype(bf16)
                copy(k.fs, k.fr, k.at[l] + 10, replica=sib).start()

    def rs_end(k, l):
        @pl.when((core != k.owner) & (sec == l))
        def _():
            arrived(k.fr, k.at[l] + 10)
            fins[k.name][...] = k.fr[...]

        @pl.when((core == k.owner) & (sec == l))
        def _():
            fins[k.name][...] = k.fs[...]

    def rs_sent():
        for k in (sgu, sd, so, sq):
            @pl.when(core == k.owner)
            def _():
                for l in (1, 0):
                    for d in range(1, SIDE):
                        sent(k.zr.at[0], k.at[l] + d)
                    if k is sgu:
                        for j in range(SIDE):
                            sent(xg.at[j], at_rswap[l] + j)

                    @pl.when(sec == l)
                    def _():
                        sent(k.fs, k.at[l] + 10)

                for d in range(1, SIDE):
                    sent(k.yr.at[0], k.at[0] + 3 + d)
                xs_sent(k, 0)

    at_o = [take(1) for _ in range(2)]
    at_d = [take(1) for _ in range(2)]

    def hand_over(l, value, own_ref, send, recv, at):
        value = value.T.astype(own_ref.dtype)

        @pl.when(sec == l)
        def _():
            own_ref[0, sec, 0] = value

        @pl.when(sec != l)
        def _():
            send[...] = value
            copy(send, recv, at[l], section=1 - sec).start()

    def hand_over_end(own_ref, send, recv, at):
        for l in range(2):
            @pl.when(sec == l)
            def _():
                arrived(recv, at[l])
                own_ref[0, 1 - sec, 0] = recv[...]

            @pl.when(sec != l)
            def _():
                sent(send, at[l])

    x_start(kq)
    x_start(kgu)
    x_start(ko)
    dx_start()
    y_start(kq, 0)
    y_start(kgu, 0)
    dz_start(0)
    y_start(ko, 0)
    z_start(kq, 0)
    z_start(kgu, 0)
    z_start(ko, 0)
    dy_start(0)
    y_start(kq, 1)
    y_start(kgu, 1)
    dz_start(1)
    y_start(ko, 1)
    z_end(kq, 0)
    gather_end(kq, 0)
    project_in(0)
    kv_start(0)
    z_mid(kgu, 0)
    z_mid(ko, 0)
    d_forward_on(0)
    z_start(kq, 1)
    kv_wait(0)
    z_end(kgu, 0)
    z_end(ko, 0)
    attend(0, 0)
    z_start(kgu, 1)
    z_start(ko, 1)
    dy_start(1)
    z_mid(kq, 1)
    attend(0, 1)
    swap_end(0)
    attend(0, 2)
    z_end(kq, 1)
    gather_end(ko, 0)
    gather_end(kgu, 0)
    d_gather_end(0)
    out = after_attention(0)
    xs_[1] = out.astype(bf16).astype(f32)
    hand_over(0, out, out_ref, osend, orecv, at_o)
    gather_end(kq, 1)
    project_in(1)
    kv_start(1)
    z_mid(kgu, 1)
    z_mid(ko, 1)
    d_forward_on(1)
    kv_wait(1)
    z_end(kgu, 1)
    z_end(ko, 1)
    attend(1, 0)
    attend(1, 1)
    swap_end(1)
    attend(1, 2)
    gather_end(ko, 1)
    gather_end(kgu, 1)
    d_gather_end(1)
    out = after_attention(1)
    hand_over(1, out, out_ref, osend, orecv, at_o)
    kv_sent(0)
    kv_sent(1)
    gather_sent()

    dmid = ffn_back(1, dy_ref[sec, 0].astype(f32).T)
    mid_[1] = dmid
    pair_start(sgu, 1)
    pair_start(sd, 1)
    out_back(1, dmid)
    pair_start(so, 1)
    attention_back(1, 0)
    rs_swap_start(1)
    attention_back(1, 1)
    rs_z_start(sd, 1)
    dkv_relay(1)
    rs_z_start(so, 1)
    rs_z_start(sgu, 1)
    dx = finish_back(1, mid_[1])
    pair_start(sq, 1)
    hand_over(1, dx, dx_ref, dsend, drecv, at_d)
    dkv_sent(1)
    rs_y_start(sd, 1)
    pair_sent(sgu, 1)
    pair_sent(sd, 1)
    dmid = ffn_back(0, dx.astype(bf16).astype(f32))
    mid_[0] = dmid
    pair_start(sgu, 0)
    pair_start(sd, 0)
    rs_z_start(sq, 1)
    rs_y_start(so, 1)
    pair_sent(so, 1)
    out_back(0, mid_[0])
    pair_start(so, 0)
    rs_y_start(sgu, 1)
    attention_back(0, 0)
    rs_swap_start(0)
    attention_back(0, 1)
    rs_x_start(sd, 1)
    rs_z_start(sd, 0)
    dkv_relay(0)
    rs_z_start(so, 0)
    rs_z_start(sgu, 0)
    rs_y_start(sq, 1)
    rs_x_start(so, 1)
    rs_x_start(sgu, 1)
    pair_sent(sq, 1)
    dx = finish_back(0, mid_[0])
    pair_start(sq, 0)
    hand_over(0, dx, dx_ref, dsend, drecv, at_d)
    rs_y_start(sd, 0)
    rs_z_start(sq, 0)
    rs_y_start(so, 0)
    rs_x_start(sq, 1)
    rs_y_start(sgu, 0)
    for k in (sd, so, sgu, sq):
        rs_end_start(k, 1)
    rs_x_start(sd, 0)
    rs_x_start(so, 0)
    rs_y_start(sq, 0)
    rs_x_start(sgu, 0)
    for k in (sd, so, sgu, sq):
        rs_end(k, 1)
    rs_x_start(sq, 0)
    for k in (sd, so, sgu, sq):
        rs_end_start(k, 0)
    for k in (sd, so, sgu, sq):
        rs_end(k, 0)
    for k in (sd, so, sgu, sq):
        pair_sent(k, 0)
    dkv_sent(0)
    rs_sent()
    hand_over_end(out_ref, osend, orecv, at_o)
    hand_over_end(dx_ref, dsend, drecv, at_d)
    assert used[0] <= SEMS, used[0]


SEMS = 400


def scratch():
    v = lambda *shape: pltpu.VMEM(shape, bf16)
    w = lambda *shape: pltpu.VMEM(shape, f32)
    widths = (FF, QKV, OUT)
    return [
        *[v(2, SIDE, PAD, n) for n in widths],
        *[v(2, SIDE, BAND, n) for n in (GU, QKV, OUT)], v(2, SIDE, SIDE, FROWS, D),
        v(2, SHARDS * TOK, 384), v(2, SHARDS - 1, TOK, 384),
        w(GROUP, SHARDS * TOK), w(GROUP, 128), w(GROUP, 128),
        w(2, TOK, D), v(2, TOK, D), v(2, HEADS, TOK, 64), v(2, HEADS, TOK, 64),
        w(2, KV_HEADS, GROUP, 1), w(2, TOK, D), v(2, TOK, D), w(2, TOK, GU),
        v(TOK, D), v(HEADS, TOK, 64), w(KV_HEADS, GROUP, 1), w(HEADS, TOK, 64), w(TOK, 384),
        w(TOK, D), v(TOK, D),
        *[v(SIDE, BAND, n) for n in (GU, QKV, OUT)], v(SIDE, SIDE, FROWS, D), v(SIDE, BAND, FF),
        *[v(3, BAND, n) for n in widths], v(3, SIDE, FROWS, D),
        *[v(SIDE, PAD, n) for n in widths], v(SIDE, FROWS, D),
        *[v(3, PAD, n) for n in widths], v(3, FROWS, D),
        *[v(PAD, n) for n in widths], v(FROWS, D),
        *[v(3, PAD, n) for n in widths], v(3, FROWS, D),
        v(2, PAD, FF), v(PAD, QKV), v(PAD, OUT), v(FROWS, D),
        v(2, PAD, FF), v(PAD, QKV), v(PAD, OUT), v(FROWS, D),
        v(D, TOK), v(D, TOK), w(D, TOK), w(D, TOK),
        v(PAD, FF), w(TOK, 128), w(TOK, 128),
        pltpu.SemaphoreType.DMA((SEMS,)), pltpu.SemaphoreType.DMA((SEMS,)),
        pltpu.SemaphoreType.REGULAR((32,)),
    ]


def kernel(*refs):
    body(*refs)


def spread(
    out_in, dx_in, gu_in, q_in, o_in, d_in,
    out_ref, dx_ref, gq_ref, gk_ref, gv_ref, go_ref, gg_ref, gu_ref, gd_ref, ga_ref, gf_ref,
):
    out_ref[...] = out_in[...]
    dx_ref[...] = dx_in[...]
    q = q_in[...].astype(f32)
    gq_ref[:, 0, :] = q[0:ROWS, 0:576]
    gk_ref[:, 0, :] = q[0:ROWS, 576:768]
    gv_ref[:, 0, :] = q[0:ROWS, 768:960]
    go_ref[:, 0, :] = o_in[...].astype(f32)[0:ROWS, 0:D]
    gg_ref[:, 0, :] = gu_in[0].astype(f32)[0:ROWS]
    gu_ref[:, 0, :] = gu_in[1].astype(f32)[0:ROWS]
    gd_ref[0] = d_in[...].astype(f32)
    row = lax.broadcasted_iota(jnp.int32, (PAD, 128), 0)
    lane = lax.broadcasted_iota(jnp.int32, (PAD, 128), 1)
    rows = dot_tn(q_in[:, 896:1024], jnp.where(row == lane, 1.0, 0.0).astype(bf16))
    ga_ref[...] = rows[64:65, 0:ROWS]
    gf_ref[...] = rows[65:66, 0:ROWS]


def angle_tables():
    half = HEAD_DIM // 2
    inverse = np.float64(rope_base) ** (-(np.arange(half) * 2.0 / HEAD_DIM))

    def table(positions):
        angles = np.tile(positions[:, None] * inverse[None, :], (1, 4))
        return jnp.asarray(np.concatenate([np.cos(angles), np.sin(angles)], axis=1).astype(np.float32))

    firsts = np.repeat(np.arange(SHARDS) * TOK, 8)
    return table(np.arange(TOK)), table(firsts).reshape(SHARDS, 8, 256)


def local(
    inputs, out_grad, w_query, w_key, w_value, w_out, w_gate, w_up, w_down, gain_attn, gain_ffn
):
    near, far = angle_tables()
    whole = pl.BlockSpec(memory_space=pltpu.VMEM)
    turned = ((1, 2, 1, D, TOK), bf16), ((1, 2, 1, D, TOK), f32)
    shapes = turned + (((2, PAD, FF), bf16), ((PAD, QKV), bf16), ((PAD, OUT), bf16), ((FROWS, D), bf16))
    res = pl.pallas_call(
        kernel,
        out_shape=[jax.ShapeDtypeStruct(s, t) for s, t in shapes],
        in_specs=[whole] * 13,
        out_specs=[whole] * len(shapes),
        scratch_shapes=scratch(),
        compiler_params=pltpu.CompilerParams(
            collective_id=0, has_side_effects=True, vmem_limit_bytes=63 * 1024 * 1024
        ),
        name="two_layers",
    )(
        jnp.swapaxes(inputs, 2, 3), jnp.swapaxes(out_grad, 2, 3), w_query, w_key, w_value, w_out,
        w_gate, w_up, w_down, gain_attn, gain_ffn, near, far,
    )
    rows = lambda n: ((ROWS, 1, n), f32)
    shapes = turned + (
        rows(576), rows(192), rows(192), rows(D), rows(FF), rows(FF), ((1, FROWS, D), f32),
        ((1, ROWS), f32), ((1, ROWS), f32),
    )
    out, dx, *grads = pl.pallas_call(
        spread,
        out_shape=[jax.ShapeDtypeStruct(s, t) for s, t in shapes],
        in_specs=[whole] * 6,
        out_specs=[whole] * 11,
        name="spread",
    )(*res)
    grads[:6] = [jnp.swapaxes(g, 0, 1) for g in grads[:6]]
    return (jnp.swapaxes(out, 3, 4), jnp.swapaxes(dx, 3, 4), *grads)


def solution(mesh):
    return jax.shard_map(
        local,
        mesh=mesh,
        in_specs=(
            P(None, "replica", "shard", None),
            P(None, "replica", "shard", None),
            P("section", "shard", None),
            P("section", "shard", None),
            P("section", "shard", None),
            P("section", "shard", None),
            P("section", "shard", None),
            P("section", "shard", None),
            P("section", "shard", None),
            P("section", "shard"),
            P("section", "shard"),
        ),
        out_specs=(
            P("section", None, "replica", "shard", None),
            P("section", None, "replica", "shard", None),
            P("section", "shard", None),
            P("section", "shard", None),
            P("section", "shard", None),
            P("section", "shard", None),
            P("section", "shard", None),
            P("section", "shard", None),
            P("section", "shard", None),
            P("section", "shard"),
            P("section", "shard"),
        ),
        check_vma=False,
    )
```

```python
import functools

import jax
import jax.numpy as jnp
import numpy as np
from jax import lax
from jax.experimental import pallas as pl
from jax.experimental.pallas import tpu as pltpu
from jax.sharding import PartitionSpec as P

HEADS = 9
KV_HEADS = 3
HEAD_DIM = 64
D = 576
FF = 1536
TOK = 128
SHARDS = 16
SIDE = 4
ROWS = 36
PAD = 48
BAND = SIDE * ROWS
FROWS = 96
FBAND = SIDE * FROWS
PART = 2 * FBAND
GU = 2 * FF
QKV = 1024
OUT = 640
CHUNK = 512
HALVES = {1: pl.ds(0, 80), 3: pl.ds(80, BAND - 80)}
GROUP = 3 * TOK

bf16 = jnp.bfloat16
f32 = jnp.float32
MESH = pl.DeviceIdType.MESH
epsilon = 1e-05
rope_base = 100000.0
score_scale = 0.125


def dot(a, b):
    return lax.dot_general(a, b, (((1,), (0,)), ((), ())), preferred_element_type=f32)


def dot_nt(a, b):
    return lax.dot_general(a, b, (((1,), (1,)), ((), ())), preferred_element_type=f32)


def dot_tn(a, b):
    return lax.dot_general(a, b, (((0,), (0,)), ((), ())), preferred_element_type=f32)


def factor_of(v):
    return lax.rsqrt(jnp.mean(v * v, axis=-1, keepdims=True) + epsilon)


def norm_back(v, r, gain, up):
    scaled = gain * up
    return r * scaled - v * (r * r * r) * jnp.mean(scaled * v, axis=-1, keepdims=True)


def half_swap(u):
    width = u.shape[1]
    lane = lax.broadcasted_iota(jnp.int32, u.shape, 1)
    first = lax.rem(lane, HEAD_DIM) < HEAD_DIM // 2
    return jnp.where(first, pltpu.roll(u, width - 32, 1), pltpu.roll(u, 32, 1))


def body(
    x_ref, dy_ref, wq_ref, wk_ref, wv_ref, wo_ref, wg_ref, wu_ref, wd_ref, ga_ref, gf_ref, near_ref, far_ref,
    out_ref, dx_ref, fin_gu, fin_q, fin_o, fin_d,
    stage_gu, stage_q, stage_o, w_gu, w_q, w_o, w_d, kv, dkv_r, scr, mx, acc,
    xs_, a_, q8_, o_, lse_, mid_, bn_, gu_,
    dyb_, dob_, delta_, dq_, dkv_acc, acc2, gain_term,
    g_gu, g_q, g_o, g_d, xg,
    zr_gu, zr_q, zr_o, zr_d, ys_gu, ys_q, ys_o, ys_d, yr_gu, yr_q, yr_o, yr_d,
    xs_gu, xs_q, xs_o, xs_d, xr_gu, xr_q, xr_o, xr_d, fs_gu, fs_q, fs_o, fs_d, fr_gu, fr_q, fr_o, fr_d,
    osend, orecv, dsend, drecv, pack_gu, cos_ref, sin_ref,
    ssem, rsem, credit,
):
    sec = lax.axis_index("section")
    sh = lax.axis_index("shard")
    rep = lax.axis_index("replica")
    z, y = lax.div(sh, SIDE), lax.rem(sh, SIDE)
    core = lax.rem(rep, 2)
    sib = rep + 1 - 2 * core
    far = lax.rem(rep + 2, 4)
    used = [0]

    def take(n):
        at = used[0]
        used[0] += n
        return at

    def copy(src, dst, at, to=None, **dev):
        return pltpu.make_async_remote_copy(
            src_ref=src, dst_ref=dst, send_sem=ssem.at[at], recv_sem=rsem.at[at if to is None else to],
            device_id=dev, device_id_type=MESH,
        )

    def arrived(dst, at):
        copy(dst, dst, at, shard=sh).wait_recv()

    def sent(src, at):
        copy(src, src, at, shard=sh).wait_send()

    def y_peer(d):
        return z * SIDE + lax.rem(y + d, SIDE)

    def z_peer(d):
        return lax.rem(z + d, SIDE) * SIDE + y

    def z_from(d):
        return lax.rem(z + SIDE - d, SIDE)

    def y_from(d):
        return lax.rem(y + SIDE - d, SIDE)

    last = pl.ds(pl.multiple_of(lax.div(sh, SIDE) * CHUNK, CHUNK), CHUNK)
    for l in range(2):
        kv[l, last, :] = jnp.zeros((CHUNK, 384), bf16)
    def padded(ref, value):
        ref[0:32] = value[0:32]
        ref[32:PAD] = jnp.concatenate(
            [value[32:ROWS].astype(f32), jnp.zeros((PAD - ROWS, value.shape[1]), f32)], axis=0
        ).astype(bf16)

    @pl.when(core == 1)
    def _():
        row16 = lax.broadcasted_iota(jnp.int32, (16, ROWS), 0)
        gain16 = jnp.where(
            row16 == 0, ga_ref[...].astype(f32), jnp.where(row16 == 1, gf_ref[...].astype(f32), 0.0)
        ).astype(bf16)
        place = lax.broadcasted_iota(jnp.int32, (16, 64), 0) == lax.broadcasted_iota(jnp.int32, (16, 64), 1)
        gain_cols = dot_tn(gain16, jnp.where(place, 1.0, 0.0).astype(bf16))
        whole = jnp.concatenate(
            [wq_ref[0].astype(f32), wk_ref[0].astype(f32), wv_ref[0].astype(f32), gain_cols], axis=1
        ).astype(bf16)
        padded(stage_q.at[sec, y], whole)
        whole = jnp.concatenate([wo_ref[0].astype(f32), jnp.zeros((ROWS, OUT - D), f32)], axis=1).astype(bf16)
        padded(stage_o.at[sec, y], whole)
        w_d[sec, z, y] = wd_ref[0]

    for c in range(2):
        @pl.when((core == 0) & (sec == c))
        def _():
            padded(stage_gu.at[sec, y], (wg_ref, wu_ref)[c][0])
            padded(pack_gu, (wg_ref, wu_ref)[1 - c][0])

    cos1, sin1 = near_ref[:, 0:128], near_ref[:, 128:256]
    first = far_ref[sh]
    cos2, sin2 = first[0:1, 0:128], first[0:1, 128:256]
    low = lax.rem(lax.broadcasted_iota(jnp.int32, (TOK, 128), 1), HEAD_DIM) < HEAD_DIM // 2
    cos_ref[...] = cos1 * cos2 - sin1 * sin2
    sine = sin1 * cos2 + cos1 * sin2
    sin_ref[...] = jnp.where(low, -sine, sine)
    xs_[0] = x_ref[sec, 0].astype(f32).T

    barrier = pltpu.get_barrier_semaphore()

    def greet(d, c):
        pl.semaphore_signal(barrier, inc=1, device_id={"shard": lax.rem(sh + d, SHARDS)}, device_id_type=MESH)
        return c

    lax.fori_loop(1, SHARDS, greet, 0)
    pl.semaphore_signal(barrier, inc=1, device_id={"replica": sib}, device_id_type=MESH)
    pl.semaphore_signal(barrier, inc=1, device_id={"replica": far}, device_id_type=MESH)
    pl.semaphore_signal(barrier, inc=1, device_id={"section": 1 - sec}, device_id_type=MESH)
    pl.semaphore_signal(barrier, inc=1, device_id={"section": 1 - sec, "replica": far}, device_id_type=MESH)
    pl.semaphore_wait(barrier, SHARDS - 1 + 4)

    mine = pl.ds(pl.multiple_of(sec * FF, 128), FF)
    theirs = pl.ds(pl.multiple_of((1 - sec) * FF, 128), FF)

    class Gather:
        def __init__(self, owner, send, stage, w, cols, width):
            self.owner, self.send, self.stage, self.w, self.width = owner, send, stage, w, width
            self.cols = cols
            self.at_x = take(1)
            self.at_y = [take(3) for _ in range(2)]
            self.at_z = [take(4) for _ in range(2)]
            self.at_f = [take(4) for _ in range(2)]

        def band(self, l, j):
            return self.w.at[l, j, :, self.cols]

    kgu = Gather(0, pack_gu, stage_gu, w_gu, mine, FF)
    kq = Gather(1, stage_q.at[sec, y], stage_q, w_q, pl.ds(0, QKV), QKV)
    ko = Gather(1, stage_o.at[sec, y], stage_o, w_o, pl.ds(0, OUT), OUT)
    at_xd = take(1)
    at_dz = [take(3) for _ in range(2)]
    at_dy = [take(3) for _ in range(2)]
    at_df = [take(1) for _ in range(2)]
    at_swap = [take(4) for _ in range(2)]
    at_sf = [take(4) for _ in range(2)]

    def x_start(k):
        @pl.when(core == k.owner)
        def _():
            copy(k.send, k.stage.at[sec, y], k.at_x, section=1 - sec).start()

    def dx_start():
        @pl.when(core == 1)
        def _():
            copy(w_d.at[sec, z, y], w_d.at[sec, z, y], at_xd, section=1 - sec).start()

    def y_start(k, l):
        @pl.when(core == k.owner)
        def _():
            own = k.stage.at[l, y]

            @pl.when(sec != l)
            def _():
                arrived(own, k.at_x)

            for d in (2, 1, 3):
                copy(own, own, k.at_y[l] + d - 1, shard=y_peer(d)).start()

    def dz_start(l):
        @pl.when(core == 1)
        def _():
            own = w_d.at[l, z, y]

            @pl.when(sec != l)
            def _():
                arrived(own, at_xd)

            for d in (2, 1, 3):
                copy(own, own, at_dz[l] + d - 1, shard=z_peer(d)).start()

    def z_start(k, l):
        @pl.when(core == k.owner)
        def _():
            for d in range(1, SIDE):
                arrived(k.stage.at[l, y_from(d)], k.at_y[l] + d - 1)
            own = k.band(l, z)
            for at in range(0, k.width, 128):
                parts = [k.stage[l, j, :, at : at + 128][0:ROWS].astype(f32) for j in range(SIDE)]
                own[:, at : at + 128] = jnp.concatenate(parts, axis=0).astype(bf16)
            for d in (1, 3) if ring(k, l) else (2, 1, 3):
                copy(own, own, k.at_z[l] + d - 1, shard=z_peer(d)).start()
            pass_on(k, l, z, 0)

    def ring(k, l):
        return not (k is kq and l == 0)

    def pass_on(k, l, j, d):
        got = k.band(l, j)
        copy(got, got, k.at_f[l] + d, replica=sib).start()
        if k is kgu:
            copy(got, got, at_swap[l] + j, **swap_to(j)).start()

    def z_mid(k, l):
        @pl.when(core == k.owner)
        def _():
            for d in (1, 3):
                got = k.band(l, z_from(d))
                arrived(got, k.at_z[l] + d - 1)
                half = got.at[HALVES[d]]
                copy(half, half, k.at_z[l] + (1 if d == 1 else 3), shard=z_peer(d)).start()
                pass_on(k, l, z_from(d), d)

    def dy_start(l):
        @pl.when(core == 1)
        def _():
            for d in range(1, SIDE):
                arrived(w_d.at[l, z_from(d), y], at_dz[l] + d - 1)
            own = w_d.at[l, :, y]
            for d in (2, 1, 3):
                copy(own, own, at_dy[l] + d - 1, shard=y_peer(d)).start()

    def z_end(k, l):
        @pl.when(core == k.owner)
        def _():
            if ring(k, l):
                got = k.band(l, z_from(2))
                arrived(got.at[HALVES[1]], k.at_z[l] + 1)
                arrived(got.at[HALVES[3]], k.at_z[l] + 3)
                pass_on(k, l, z_from(2), 2)
            else:
                for d in (1, 3, 2):
                    arrived(k.band(l, z_from(d)), k.at_z[l] + d - 1)
                    pass_on(k, l, z_from(d), d)

    def swap_to(j):
        if isinstance(j, int):
            return {"section": 1 - sec} if j < 2 else {"section": 1 - sec, "replica": far}
        return {"section": 1 - sec, "replica": jnp.where(j < 2, rep, far)}

    def swap_end(l):
        @pl.when(core == 0)
        def _():
            for j in range(SIDE):
                got = w_gu.at[l, j, :, theirs]
                arrived(got, at_swap[l] + j)
                copy(got, got, at_sf[l] + j, replica=sib).start()

    def d_forward_on(l):
        @pl.when(core == 1)
        def _():
            for d in range(1, SIDE):
                arrived(w_d.at[l, :, y_from(d)], at_dy[l] + d - 1)
            copy(w_d.at[l], w_d.at[l], at_df[l], replica=sib).start()

    def gather_end(k, l):
        @pl.when(core != k.owner)
        def _():
            arrived(k.band(l, z), k.at_f[l])
            for d in range(1, SIDE):
                arrived(k.band(l, z_from(d)), k.at_f[l] + d)
            if k is kgu:
                for j in range(SIDE):
                    arrived(w_gu.at[l, j, :, theirs], at_sf[l] + j)

    def d_gather_end(l):
        @pl.when(core == 0)
        def _():
            arrived(w_d.at[l], at_df[l])

    def gather_sent():
        for l in range(2):
            for k in (kgu, kq, ko):
                @pl.when(core == k.owner)
                def _():
                    @pl.when(sec == l)
                    def _():
                        sent(k.send, k.at_x)

                    for d in range(1, SIDE):
                        sent(k.stage.at[l, y], k.at_y[l] + d - 1)
                        if not ring(k, l) or d != 2:
                            sent(k.band(l, z), k.at_z[l] + d - 1)
                        sent(k.band(l, z), k.at_f[l] + d)
                    if ring(k, l):
                        sent(k.band(l, z).at[HALVES[1]], k.at_z[l] + 1)
                        sent(k.band(l, z).at[HALVES[3]], k.at_z[l] + 3)
                    sent(k.band(l, z), k.at_f[l])
                    if k is kgu:
                        for j in range(SIDE):
                            sent(k.band(l, j), at_swap[l] + j)
                            sent(k.band(l, j), at_sf[l] + j)

            @pl.when(core == 1)
            def _():
                @pl.when(sec == l)
                def _():
                    sent(w_d.at[0, z, y], at_xd)

                for d in range(1, SIDE):
                    sent(w_d.at[l, z, y], at_dz[l] + d - 1)
                    sent(w_d.at[l, :, y], at_dy[l] + d - 1)
                sent(w_d.at[l], at_df[l])

    at_kv = [take(SHARDS) for _ in range(2)]
    at_kvr = [take(4) for _ in range(2)]
    at_dkv = [take(SHARDS) for _ in range(2)]
    at_dky = [take(4) for _ in range(2)]
    tokens = pl.ds(pl.multiple_of(sh * TOK, TOK), TOK)
    twice = 2 * SIDE

    def block(l, j):
        return kv.at[l, pl.ds(pl.multiple_of(j * TOK, TOK), TOK)]

    def relayed(j):
        gap = lax.div(j, SIDE) - z
        return ((gap == 2) | (gap == -2)) & (lax.rem(j, SIDE) != y)

    def kv_start(l):
        own = kv.at[l, tokens]

        def go(d, c):
            @pl.when(jnp.logical_not(relayed(sh + d)))
            def _():
                copy(own, own, at_kv[l] + d, shard=sh + d).start()

            return c

        lax.fori_loop(1, SHARDS - sh, go, 0)

    def kv_wait(l):
        @pl.when(z >= 2)
        def _():
            passing = block(l, sh - twice)
            arrived(passing, at_kv[l] + twice)
            for e in range(1, SIDE):
                yt = lax.rem(y + e, SIDE)
                copy(passing, passing, at_kvr[l] + e, to=at_kv[l] + twice + yt - y, shard=y_peer(e)).start()

        def go(d, c):
            @pl.when(d != twice)
            def _():
                arrived(block(l, sh - d), at_kv[l] + d)

            return c

        lax.fori_loop(1, sh + 1, go, 0)

    def kv_sent(l):
        def go(d, c):
            @pl.when(jnp.logical_not(relayed(sh + d)))
            def _():
                sent(kv.at[l, tokens], at_kv[l] + d)

            return c

        lax.fori_loop(1, SHARDS - sh, go, 0)

        @pl.when(z >= 2)
        def _():
            for e in range(1, SIDE):
                sent(kv.at[l, tokens], at_kvr[l] + e)

    def dkv_start(l, j):
        away = relayed(j)

        @pl.when(away)
        def _():
            e = lax.rem(lax.rem(j, SIDE) - y + SIDE, SIDE)
            copy(
                block(l, j), dkv_r.at[l, twice - 1 + e], at_dkv[l] + sh - j,
                to=at_dky[l] + e, shard=z * SIDE + lax.rem(j, SIDE),
            ).start()

        @pl.when(jnp.logical_not(away) & (sh - j != twice))
        def _():
            copy(block(l, j), dkv_r.at[l, sh - j - 1], at_dkv[l] + sh - j, shard=j).start()

    def dkv_relay(l):
        @pl.when(z >= 2)
        def _():
            passing = block(l, sh - twice)
            for e in range(1, SIDE):
                arrived(dkv_r.at[l, twice - 1 + e], at_dky[l] + e)
            tot = passing[...].astype(f32)
            for e in range(1, SIDE):
                tot += dkv_r[l, twice - 1 + e].astype(f32)
            passing[...] = tot.astype(bf16)
            copy(passing, dkv_r.at[l, twice - 1], at_dkv[l] + twice, shard=sh - twice).start()

    def dkv_sent(l):
        def go(d, c):
            sent(kv.at[l, pl.ds(0, TOK)], at_dkv[l] + d)
            return c

        lax.fori_loop(1, sh + 1, go, 0)

    def gains(l):
        tile = w_q[l, :, :, 896:1024].reshape(D, 128)
        row = lax.broadcasted_iota(jnp.int32, (8, 128), 0)
        lane = lax.broadcasted_iota(jnp.int32, (8, 128), 1)
        pick = jnp.where(lane == row + 64, 1.0, 0.0).astype(bf16)
        both = dot_nt(pick, tile)
        return both[0:1], both[1:2]

    nfull = lax.div(sh, SIDE)

    def causal():
        row = lax.broadcasted_iota(jnp.int32, (GROUP, CHUNK), 0)
        col = lax.broadcasted_iota(jnp.int32, (GROUP, CHUNK), 1)
        return col <= lax.rem(sh, SIDE) * TOK + lax.rem(row, TOK)

    def keys_at(c):
        return pl.ds(pl.multiple_of(c * CHUNK, CHUNK), CHUNK)

    def tables():
        cos = jnp.concatenate([cos_ref[...]] * 6, axis=1)
        sin = jnp.concatenate([sin_ref[...]] * 6, axis=1)
        return cos, sin

    def project_in(l):
        x = xs_[l]
        gain, _ = gains(l)
        a = (x * factor_of(x) * gain).astype(bf16)
        a_[l] = a
        qkv = dot(a, w_q[l].reshape(D, QKV))
        cos, sin = tables()
        u = qkv[:, 0:768]
        turned = u * cos + half_swap(u) * sin
        for h in range(HEADS):
            head = turned[:, h * 64 : h * 64 + 64].astype(bf16)
            q8_[l, h] = (head.astype(f32) * score_scale).astype(bf16)
        block = jnp.concatenate([turned[:, 576:768], qkv[:, 768:960]], axis=1).astype(bf16)
        kv[l, tokens] = block

    def attend(l, g):
        if True:
            q = q8_[l, 3 * g : 3 * g + 3].reshape(GROUP, 64)

            def keep(c, s):
                scr[:, keys_at(c)] = s
                top = jnp.maximum(
                    jnp.maximum(s[:, 0:128], s[:, 128:256]), jnp.maximum(s[:, 256:384], s[:, 384:512])
                )
                mx[...] = jnp.maximum(mx[...], top)

            def scores(c):
                k = kv[l, keys_at(c), :][:, g * 64 : g * 64 + 64]
                return dot_nt(q, k)

            mx[...] = jnp.full_like(mx, -1e30)

            def first(c, carry):
                keep(c, scores(c))
                return carry

            lax.fori_loop(0, nfull, first, 0)
            keep(nfull, jnp.where(causal(), scores(nfull), -1e30))
            peak = jnp.max(mx[...], axis=1, keepdims=True)
            acc[...] = jnp.zeros_like(acc)

            def second(c, carry):
                p = jnp.exp(scr[:, keys_at(c)] - peak).astype(bf16)
                v = kv[l, keys_at(c), :][:, 192 + g * 64 : 256 + g * 64]
                v = jnp.concatenate([v, jnp.ones_like(v)], axis=1)
                acc[...] += dot(p, v)
                return carry

            lax.fori_loop(0, nfull + 1, second, 0)
            total = acc[:, 64:65]
            mixed = (acc[:, 0:64] / total).astype(bf16)
            lse_[l, g] = peak + jnp.log(total)
            o_[l, 3 * g : 3 * g + 3] = mixed.reshape(3, TOK, 64)

    def heads_in(ref):
        return jnp.concatenate([ref[h] for h in range(HEADS)], axis=1)

    def after_attention(l):
        o = heads_in(o_.at[l])
        mid = xs_[l] + dot(o, w_o[l, :, :, 0:D].reshape(D, D))
        mid_[l] = mid
        _, gain = gains(l)
        bn_[l] = (mid * factor_of(mid) * gain).astype(bf16)
        acc2[...] = mid

        def tile(t, c):
            gcols = pl.ds(pl.multiple_of(t * PART, 128), PART)
            ucols = pl.ds(pl.multiple_of(FF + t * PART, 128), PART)
            bn = bn_[l]
            gt = dot(bn, w_gu[l, :, :, gcols].reshape(D, PART))
            up = dot(bn, w_gu[l, :, :, ucols].reshape(D, PART))
            gu_[l, :, gcols] = gt
            gu_[l, :, ucols] = up
            hid = (gt * jax.nn.sigmoid(gt) * up).astype(bf16)
            acc2[...] += dot(hid, w_d[l, pl.ds(2 * t, 2)].reshape(PART, D))
            return c

        lax.fori_loop(0, FF // PART, tile, 0)
        return acc2[...]

    def ffn_back(l, dy):
        dyb_[...] = dy.astype(bf16)
        acc2[...] = jnp.zeros_like(acc2)

        def tile(t, c):
            gcols = pl.ds(pl.multiple_of(t * PART, 128), PART)
            ucols = pl.ds(pl.multiple_of(FF + t * PART, 128), PART)
            dyb = dyb_[...]
            bn = bn_[l]
            wd = w_d[l, pl.ds(2 * t, 2)].reshape(PART, D)
            dhid = dot_nt(dyb, wd).astype(bf16).astype(f32)
            gt, up = gu_[l, :, gcols], gu_[l, :, ucols]
            s = jax.nn.sigmoid(gt)
            hid = (gt * s * up).astype(bf16)
            g_d[pl.ds(2 * t, 2)] = dot_tn(hid, dyb).astype(bf16).reshape(2, SIDE, FROWS, D)
            dgt = (dhid * up * s * (1.0 + gt * (1.0 - s))).astype(bf16)
            dup = (dhid * gt * s).astype(bf16)
            g_gu[:, :, gcols] = dot_tn(bn, dgt).astype(bf16).reshape(SIDE, BAND, PART)
            g_gu[:, :, ucols] = dot_tn(bn, dup).astype(bf16).reshape(SIDE, BAND, PART)
            acc2[...] += dot_nt(dgt, w_gu[l, :, :, gcols].reshape(D, PART))
            acc2[...] += dot_nt(dup, w_gu[l, :, :, ucols].reshape(D, PART))
            return c

        lax.fori_loop(0, FF // PART, tile, 0)
        dbn = acc2[...]
        mid = mid_[l]
        r = factor_of(mid)
        _, gain = gains(l)
        gain_term[...] = (dbn * mid * r).astype(bf16)
        return dy + norm_back(mid, r, gain, dbn)

    def out_back(l, dmid):
        dmb = dmid.astype(bf16)
        o = heads_in(o_.at[l])
        g_o[...] = jnp.concatenate(
            [dot_tn(o, dmb), jnp.zeros((D, 64), f32)], axis=1
        ).astype(bf16).reshape(SIDE, BAND, 640)
        dob = dot_nt(dmb, w_o[l, :, :, 0:D].reshape(D, D)).astype(bf16)
        for h in range(HEADS):
            do_h = dob[:, h * 64 : h * 64 + 64]
            dq_[h] = jnp.zeros((TOK, 64), f32)
            dob_[h] = do_h

    def attention_back(l, part):
        for g in range(KV_HEADS):
            do = dob_[3 * g : 3 * g + 3].reshape(GROUP, 64).astype(f32)
            og = o_[l, 3 * g : 3 * g + 3].reshape(GROUP, 64).astype(f32)
            if part == 0:
                delta_[g] = jnp.sum(do * og, axis=1, keepdims=True)

        def chunk(c, masked):
            kvb = kv[l, keys_at(c), :]
            dks, dvs = [], []
            for g in range(KV_HEADS):
                q = q8_[l, 3 * g : 3 * g + 3].reshape(GROUP, 64)
                do = dob_[3 * g : 3 * g + 3].reshape(GROUP, 64)
                k = kvb[:, g * 64 : g * 64 + 64]
                v = kvb[:, 192 + g * 64 : 256 + g * 64]
                s = dot_nt(q, k)
                if masked:
                    s = jnp.where(causal(), s, -1e30)
                p = jnp.exp(s - lse_[l, g])
                ds = (p * (dot_nt(do, v) - delta_[g])).astype(bf16)
                dq_[3 * g : 3 * g + 3] += dot(ds, k).reshape(3, TOK, 64)
                dks.append(dot_tn(ds, q))
                dvs.append(dot_tn(p.astype(bf16), do))
            kv[l, keys_at(c), :] = jnp.concatenate(dks + dvs, axis=1).astype(bf16)

        def full(c, carry):
            chunk(c, False)
            for i in range(SIDE):
                dkv_start(l, c * SIDE + i)
            return carry

        def rest(j, carry):
            dkv_start(l, j)
            return carry

        if part == 0:
            lax.fori_loop(0, nfull, full, 0)
        else:
            chunk(nfull, True)
            lax.fori_loop(nfull * SIDE, sh, rest, 0)

    def finish_back(l, dmid_at):
        dkv_acc[...] = kv[l, tokens, :].astype(f32)

        def add(d, c):
            @pl.when(jnp.logical_not(relayed(sh + d)))
            def _():
                arrived(dkv_r.at[l, d - 1], at_dkv[l] + d)
                dkv_acc[...] += dkv_r[l, d - 1].astype(f32)

            return c

        lax.fori_loop(1, SHARDS - sh, add, 0)
        dkv = dkv_acc[...]
        cos, sin = tables()
        dq = jnp.concatenate([dq_[h] for h in range(HEADS)], axis=1) * score_scale
        u = jnp.concatenate([dq, dkv[:, 0:192]], axis=1)
        back = u * cos - half_swap(u) * sin
        dqkv = jnp.concatenate([back, dkv[:, 192:384], jnp.zeros((TOK, 64), f32)], axis=1).astype(bf16)
        a = a_[l]
        gq = dot_tn(a, dqkv)
        da = dot_nt(dqkv, w_q[l].reshape(D, QKV))
        x = xs_[l]
        r = factor_of(x)
        gain, _ = gains(l)
        lane = lax.broadcasted_iota(jnp.int32, (TOK, 128), 1)
        e0 = jnp.where(lane == 64, 1.0, 0.0).astype(bf16)
        e1 = jnp.where(lane == 65, 1.0, 0.0).astype(bf16)
        cols = dot_tn((da * x * r).astype(bf16), e0) + dot_tn(gain_term[...], e1)
        g_q[:, :, 0:896] = gq[:, 0:896].astype(bf16).reshape(SIDE, BAND, 896)
        g_q[:, :, 896:1024] = (gq[:, 896:1024] + cols).astype(bf16).reshape(SIDE, BAND, 128)
        return dmid_at + norm_back(x, r, gain, da)

    class Sum:
        def __init__(self, name, owner, w, cols, g, zr, ys, yr, xs, xr, fs, fr, width):
            self.name, self.owner, self.w, self.cols, self.g = name, owner, w, cols, g
            self.zr, self.ys, self.yr, self.xs, self.xr, self.fs, self.fr = zr, ys, yr, xs, xr, fs, fr
            self.width = width
            self.at = [take(12) for _ in range(2)]
            self.free = credits(2)
            self.again_z, self.again_y = credits(1), credits(1)

            first_y = name == "d"
            self.i1, self.peer1 = (y, y_peer) if first_y else (z, z_peer)
            self.i2, self.peer2 = (z, z_peer) if first_y else (y, y_peer)

        def band(self, l, j):
            return self.w.at[l, :, j] if self.name == "d" else self.w.at[l, j, :, self.cols]

    granted = [0]

    def credits(n):
        at = granted[0]
        granted[0] += n
        return at

    sgu = Sum("gu", 0, w_gu, mine, g_gu, zr_gu, ys_gu, yr_gu, xs_gu, xr_gu, fs_gu, fr_gu, FF)
    sq = Sum("q", 1, w_q, pl.ds(0, QKV), g_q, zr_q, ys_q, yr_q, xs_q, xr_q, fs_q, fr_q, QKV)
    so = Sum("o", 1, w_o, pl.ds(0, OUT), g_o, zr_o, ys_o, yr_o, xs_o, xr_o, fs_o, fr_o, OUT)
    sd = Sum("d", 1, w_d, None, g_d, zr_d, ys_d, yr_d, xs_d, xr_d, fs_d, fr_d, D)
    at_rswap = [take(4) for _ in range(2)]
    swap_again = credits(1)

    def pair_start(k, l):
        pl.semaphore_signal(credit.at[k.free + l], inc=1, device_id={"replica": sib}, device_id_type=MESH)
        pl.semaphore_wait(credit.at[k.free + l], 1)

        @pl.when(core != k.owner)
        def _():
            copy(k.g, k.w.at[l], k.at[l], replica=sib).start()

    def pair_sent(k, l):
        @pl.when(core != k.owner)
        def _():
            sent(k.g, k.at[l])

    def add_into(dst, src, width):
        step = 256 if width % 256 == 0 else 128

        def add(t, c):
            cols = pl.ds(pl.multiple_of(t * step, 128), step)
            dst[:, cols] = (dst[:, cols].astype(f32) + src[:, cols].astype(f32)).astype(bf16)
            return c

        lax.fori_loop(0, width // step, add, 0)

    def rs_swap_start(l):
        @pl.when(core == 0)
        def _():
            arrived(w_gu.at[l], sgu.at[l])
            if l == 0:
                pl.semaphore_wait(credit.at[swap_again], 2)
            for j in (0, 2, 1, 3):
                src = w_gu.at[l, j, :, theirs]
                add_into(src, g_gu.at[j, :, theirs], FF)
                copy(src, xg.at[j], at_rswap[l] + j, **swap_to(j)).start()
            for j in range(SIDE):
                add_into(w_gu.at[l, j, :, mine], g_gu.at[j, :, mine], FF)

    def rs_z_start(k, l):
        @pl.when(core == k.owner)
        def _():
            if k is not sgu:
                arrived(k.w.at[l], k.at[l])
            if l == 0:
                pl.semaphore_wait(credit.at[k.again_z], 3)
            for d in (2, 1, 3, 0):
                zt = lax.rem(k.i1 + d, SIDE)
                part = k.band(l, zt)
                if k is sd:
                    part[...] = (part[...].astype(f32) + k.g[:, zt].astype(f32)).astype(bf16)
                elif k is sgu:
                    arrived(xg.at[zt], at_rswap[l] + zt)
                    add_into(part, xg.at[zt], FF)
                else:
                    add_into(part, k.g.at[zt], k.width)
                if d:
                    copy(part, k.zr.at[d - 1], k.at[l] + d, shard=k.peer1(d)).start()
            if k is sgu and l == 1:
                for j in (0, 2):
                    pl.semaphore_signal(
                        credit.at[swap_again], inc=1, device_id=swap_to(j), device_id_type=MESH
                    )

    def rs_y_start(k, l):
        @pl.when(core == k.owner)
        def _():
            for d in range(1, SIDE):
                arrived(k.zr.at[d - 1], k.at[l] + d)
            if l == 0:
                for d in range(1, SIDE):
                    sent(k.yr.at[0], k.at[1] + 3 + d)
            own = k.band(l, k.i1)
            if k is sd:
                tot = own[...].astype(f32)
                for d in range(3):
                    tot += k.zr[d].astype(f32)
                k.ys[...] = tot.astype(bf16)
            else:
                step = 256 if k.width % 256 == 0 else 128

                def add(t, c):
                    cols = pl.ds(pl.multiple_of(t * step, 128), step)
                    tot = own[:, cols].astype(f32)
                    for d in range(3):
                        tot += k.zr[d, :, cols].astype(f32)
                    for j in range(SIDE):
                        rows = tot[j * ROWS : j * ROWS + ROWS]
                        rows = jnp.concatenate([rows, jnp.zeros((PAD - ROWS, step), f32)], axis=0)
                        k.ys[j, :, cols] = rows.astype(bf16)
                    return c

                lax.fori_loop(0, k.width // step, add, 0)
            if l == 1:
                for d in range(1, SIDE):
                    pl.semaphore_signal(
                        credit.at[k.again_z], inc=1, device_id={"shard": k.peer1(d)}, device_id_type=MESH
                    )
            else:
                pl.semaphore_wait(credit.at[k.again_y], 3)
            for d in (2, 1, 3):
                yt = lax.rem(k.i2 + d, SIDE)
                copy(k.ys.at[yt], k.yr.at[d - 1], k.at[l] + 3 + d, shard=k.peer2(d)).start()

    def x_targets(l):
        for t in (1, 2, 3):
            other = 1 - sec if t >= 2 else sec
            where = {}
            if t >= 2:
                where["section"] = 1 - sec
            if t % 2:
                where["replica"] = far
            yield t, other == l, where

    def rs_x_start(k, l):
        @pl.when(core == k.owner)
        def _():
            for d in range(1, SIDE):
                arrived(k.yr.at[d - 1], k.at[l] + 3 + d)
            if l == 0:
                xs_sent(k, 1)
            tot = k.ys[k.i2].astype(f32)
            for d in range(3):
                tot += k.yr[d].astype(f32)
            k.xs[...] = tot.astype(bf16)
            if l == 1:
                for d in range(1, SIDE):
                    pl.semaphore_signal(
                        credit.at[k.again_y], inc=1, device_id={"shard": k.peer2(d)}, device_id_type=MESH
                    )
            for t, hit, where in x_targets(l):
                @pl.when(hit)
                def _():
                    copy(k.xs, k.xr.at[t - 1], k.at[l] + 6 + t, **where).start()

    def xs_sent(k, l):
        for t, hit, where in x_targets(l):
            @pl.when(hit)
            def _():
                sent(k.xs, k.at[l] + 6 + t)

    fins = {"gu": fin_gu, "q": fin_q, "o": fin_o, "d": fin_d}

    def rs_end_start(k, l):
        @pl.when((core == k.owner) & (sec == l))
        def _():
            for t in (1, 2, 3):
                arrived(k.xr.at[t - 1], k.at[l] + 6 + t)
            if k is sgu:
                own = k.xs[...].astype(f32) + k.xr[0].astype(f32)
                other = k.xr[1].astype(f32) + k.xr[2].astype(f32)
                k.fs[l] = own.astype(bf16)
                k.fs[1 - l] = other.astype(bf16)
                copy(k.fs, k.fr, k.at[l] + 10, replica=sib).start()
            else:
                tot = k.xs[...].astype(f32)
                for t in range(3):
                    tot += k.xr[t].astype(f32)
                k.fs[...] = tot.astype(bf16)
                copy(k.fs, k.fr, k.at[l] + 10, replica=sib).start()

    def rs_end(k, l):
        @pl.when((core != k.owner) & (sec == l))
        def _():
            arrived(k.fr, k.at[l] + 10)
            fins[k.name][...] = k.fr[...]

        @pl.when((core == k.owner) & (sec == l))
        def _():
            fins[k.name][...] = k.fs[...]

    def rs_sent():
        for k in (sgu, sd, so, sq):
            @pl.when(core == k.owner)
            def _():
                for l in (1, 0):
                    for d in range(1, SIDE):
                        sent(k.zr.at[0], k.at[l] + d)
                    if k is sgu:
                        for j in range(SIDE):
                            sent(xg.at[j], at_rswap[l] + j)

                    @pl.when(sec == l)
                    def _():
                        sent(k.fs, k.at[l] + 10)

                for d in range(1, SIDE):
                    sent(k.yr.at[0], k.at[0] + 3 + d)
                xs_sent(k, 0)

    at_o = [take(1) for _ in range(2)]
    at_d = [take(1) for _ in range(2)]

    def hand_over(l, value, own_ref, send, recv, at):
        value = value.T.astype(own_ref.dtype)

        @pl.when(sec == l)
        def _():
            own_ref[0, sec, 0] = value

        @pl.when(sec != l)
        def _():
            send[...] = value
            copy(send, recv, at[l], section=1 - sec).start()

    def hand_over_end(own_ref, send, recv, at):
        for l in range(2):
            @pl.when(sec == l)
            def _():
                arrived(recv, at[l])
                own_ref[0, 1 - sec, 0] = recv[...]

            @pl.when(sec != l)
            def _():
                sent(send, at[l])

    x_start(kq)
    x_start(kgu)
    x_start(ko)
    dx_start()
    y_start(kq, 0)
    y_start(kgu, 0)
    dz_start(0)
    y_start(ko, 0)
    z_start(kq, 0)
    z_start(kgu, 0)
    z_start(ko, 0)
    dy_start(0)
    y_start(kq, 1)
    y_start(kgu, 1)
    dz_start(1)
    y_start(ko, 1)
    z_end(kq, 0)
    gather_end(kq, 0)
    project_in(0)
    kv_start(0)
    z_mid(kgu, 0)
    z_mid(ko, 0)
    d_forward_on(0)
    z_start(kq, 1)
    kv_wait(0)
    z_end(kgu, 0)
    z_end(ko, 0)
    attend(0, 0)
    z_start(kgu, 1)
    z_start(ko, 1)
    dy_start(1)
    z_mid(kq, 1)
    attend(0, 1)
    swap_end(0)
    attend(0, 2)
    z_end(kq, 1)
    gather_end(ko, 0)
    gather_end(kgu, 0)
    d_gather_end(0)
    out = after_attention(0)
    xs_[1] = out.astype(bf16).astype(f32)
    hand_over(0, out, out_ref, osend, orecv, at_o)
    gather_end(kq, 1)
    project_in(1)
    kv_start(1)
    z_mid(kgu, 1)
    z_mid(ko, 1)
    d_forward_on(1)
    kv_wait(1)
    z_end(kgu, 1)
    z_end(ko, 1)
    attend(1, 0)
    attend(1, 1)
    swap_end(1)
    attend(1, 2)
    gather_end(ko, 1)
    gather_end(kgu, 1)
    d_gather_end(1)
    out = after_attention(1)
    hand_over(1, out, out_ref, osend, orecv, at_o)
    kv_sent(0)
    kv_sent(1)
    gather_sent()

    dmid = ffn_back(1, dy_ref[sec, 0].astype(f32).T)
    mid_[1] = dmid
    pair_start(sgu, 1)
    pair_start(sd, 1)
    out_back(1, dmid)
    pair_start(so, 1)
    attention_back(1, 0)
    rs_swap_start(1)
    attention_back(1, 1)
    rs_z_start(sd, 1)
    dkv_relay(1)
    rs_z_start(so, 1)
    rs_z_start(sgu, 1)
    dx = finish_back(1, mid_[1])
    pair_start(sq, 1)
    hand_over(1, dx, dx_ref, dsend, drecv, at_d)
    dkv_sent(1)
    rs_y_start(sd, 1)
    pair_sent(sgu, 1)
    pair_sent(sd, 1)
    dmid = ffn_back(0, dx.astype(bf16).astype(f32))
    mid_[0] = dmid
    pair_start(sgu, 0)
    pair_start(sd, 0)
    rs_z_start(sq, 1)
    rs_y_start(so, 1)
    pair_sent(so, 1)
    out_back(0, mid_[0])
    pair_start(so, 0)
    rs_y_start(sgu, 1)
    rs_swap_start(0)
    attention_back(0, 0)
    attention_back(0, 1)
    rs_x_start(sd, 1)
    rs_z_start(sd, 0)
    dkv_relay(0)
    rs_z_start(so, 0)
    rs_z_start(sgu, 0)
    pair_sent(sq, 1)
    dx = finish_back(0, mid_[0])
    pair_start(sq, 0)
    hand_over(0, dx, dx_ref, dsend, drecv, at_d)
    rs_y_start(sq, 1)
    rs_x_start(so, 1)
    rs_x_start(sgu, 1)
    rs_y_start(sd, 0)
    rs_z_start(sq, 0)
    rs_y_start(so, 0)
    rs_x_start(sq, 1)
    rs_y_start(sgu, 0)
    for k in (sd, so, sgu, sq):
        rs_end_start(k, 1)
    rs_x_start(sd, 0)
    rs_x_start(so, 0)
    rs_y_start(sq, 0)
    rs_x_start(sgu, 0)
    for k in (sd, so, sgu, sq):
        rs_end(k, 1)
    rs_x_start(sq, 0)
    for k in (sd, so, sgu, sq):
        rs_end_start(k, 0)
    for k in (sd, so, sgu, sq):
        rs_end(k, 0)
    for k in (sd, so, sgu, sq):
        pair_sent(k, 0)
    dkv_sent(0)
    rs_sent()
    hand_over_end(out_ref, osend, orecv, at_o)
    hand_over_end(dx_ref, dsend, drecv, at_d)
    assert used[0] <= SEMS, used[0]


SEMS = 400


def scratch():
    v = lambda *shape: pltpu.VMEM(shape, bf16)
    w = lambda *shape: pltpu.VMEM(shape, f32)
    widths = (FF, QKV, OUT)
    return [
        *[v(2, SIDE, PAD, n) for n in widths],
        *[v(2, SIDE, BAND, n) for n in (GU, QKV, OUT)], v(2, SIDE, SIDE, FROWS, D),
        v(2, SHARDS * TOK, 384), v(2, SHARDS - 1, TOK, 384),
        w(GROUP, SHARDS * TOK), w(GROUP, 128), w(GROUP, 128),
        w(2, TOK, D), v(2, TOK, D), v(2, HEADS, TOK, 64), v(2, HEADS, TOK, 64),
        w(2, KV_HEADS, GROUP, 1), w(2, TOK, D), v(2, TOK, D), w(2, TOK, GU),
        v(TOK, D), v(HEADS, TOK, 64), w(KV_HEADS, GROUP, 1), w(HEADS, TOK, 64), w(TOK, 384),
        w(TOK, D), v(TOK, D),
        *[v(SIDE, BAND, n) for n in (GU, QKV, OUT)], v(SIDE, SIDE, FROWS, D), v(SIDE, BAND, FF),
        *[v(3, BAND, n) for n in widths], v(3, SIDE, FROWS, D),
        *[v(SIDE, PAD, n) for n in widths], v(SIDE, FROWS, D),
        *[v(3, PAD, n) for n in widths], v(3, FROWS, D),
        *[v(PAD, n) for n in widths], v(FROWS, D),
        *[v(3, PAD, n) for n in widths], v(3, FROWS, D),
        v(2, PAD, FF), v(PAD, QKV), v(PAD, OUT), v(FROWS, D),
        v(2, PAD, FF), v(PAD, QKV), v(PAD, OUT), v(FROWS, D),
        v(D, TOK), v(D, TOK), w(D, TOK), w(D, TOK),
        v(PAD, FF), w(TOK, 128), w(TOK, 128),
        pltpu.SemaphoreType.DMA((SEMS,)), pltpu.SemaphoreType.DMA((SEMS,)),
        pltpu.SemaphoreType.REGULAR((32,)),
    ]


def kernel(*refs):
    body(*refs)


def spread(
    out_in, dx_in, gu_in, q_in, o_in, d_in,
    out_ref, dx_ref, gq_ref, gk_ref, gv_ref, go_ref, gg_ref, gu_ref, gd_ref, ga_ref, gf_ref,
):
    out_ref[...] = out_in[...]
    dx_ref[...] = dx_in[...]
    q = q_in[...].astype(f32)
    gq_ref[:, 0, :] = q[0:ROWS, 0:576]
    gk_ref[:, 0, :] = q[0:ROWS, 576:768]
    gv_ref[:, 0, :] = q[0:ROWS, 768:960]
    go_ref[:, 0, :] = o_in[...].astype(f32)[0:ROWS, 0:D]
    gg_ref[:, 0, :] = gu_in[0].astype(f32)[0:ROWS]
    gu_ref[:, 0, :] = gu_in[1].astype(f32)[0:ROWS]
    gd_ref[0] = d_in[...].astype(f32)
    row = lax.broadcasted_iota(jnp.int32, (PAD, 128), 0)
    lane = lax.broadcasted_iota(jnp.int32, (PAD, 128), 1)
    rows = dot_tn(q_in[:, 896:1024], jnp.where(row == lane, 1.0, 0.0).astype(bf16))
    ga_ref[...] = rows[64:65, 0:ROWS]
    gf_ref[...] = rows[65:66, 0:ROWS]


def angle_tables():
    half = HEAD_DIM // 2
    inverse = np.float64(rope_base) ** (-(np.arange(half) * 2.0 / HEAD_DIM))

    def table(positions):
        angles = np.tile(positions[:, None] * inverse[None, :], (1, 4))
        return jnp.asarray(np.concatenate([np.cos(angles), np.sin(angles)], axis=1).astype(np.float32))

    firsts = np.repeat(np.arange(SHARDS) * TOK, 8)
    return table(np.arange(TOK)), table(firsts).reshape(SHARDS, 8, 256)


def local(
    inputs, out_grad, w_query, w_key, w_value, w_out, w_gate, w_up, w_down, gain_attn, gain_ffn
):
    near, far = angle_tables()
    whole = pl.BlockSpec(memory_space=pltpu.VMEM)
    turned = ((1, 2, 1, D, TOK), bf16), ((1, 2, 1, D, TOK), f32)
    shapes = turned + (((2, PAD, FF), bf16), ((PAD, QKV), bf16), ((PAD, OUT), bf16), ((FROWS, D), bf16))
    res = pl.pallas_call(
        kernel,
        out_shape=[jax.ShapeDtypeStruct(s, t) for s, t in shapes],
        in_specs=[whole] * 13,
        out_specs=[whole] * len(shapes),
        scratch_shapes=scratch(),
        compiler_params=pltpu.CompilerParams(
            collective_id=0, has_side_effects=True, vmem_limit_bytes=63 * 1024 * 1024
        ),
        name="two_layers",
    )(
        jnp.swapaxes(inputs, 2, 3), jnp.swapaxes(out_grad, 2, 3), w_query, w_key, w_value, w_out,
        w_gate, w_up, w_down, gain_attn, gain_ffn, near, far,
    )
    rows = lambda n: ((ROWS, 1, n), f32)
    shapes = turned + (
        rows(576), rows(192), rows(192), rows(D), rows(FF), rows(FF), ((1, FROWS, D), f32),
        ((1, ROWS), f32), ((1, ROWS), f32),
    )
    out, dx, *grads = pl.pallas_call(
        spread,
        out_shape=[jax.ShapeDtypeStruct(s, t) for s, t in shapes],
        in_specs=[whole] * 6,
        out_specs=[whole] * 11,
        name="spread",
    )(*res)
    grads[:6] = [jnp.swapaxes(g, 0, 1) for g in grads[:6]]
    return (jnp.swapaxes(out, 3, 4), jnp.swapaxes(dx, 3, 4), *grads)


def solution(mesh):
    return jax.shard_map(
        local,
        mesh=mesh,
        in_specs=(
            P(None, "replica", "shard", None),
            P(None, "replica", "shard", None),
            P("section", "shard", None),
            P("section", "shard", None),
            P("section", "shard", None),
            P("section", "shard", None),
            P("section", "shard", None),
            P("section", "shard", None),
            P("section", "shard", None),
            P("section", "shard"),
            P("section", "shard"),
        ),
        out_specs=(
            P("section", None, "replica", "shard", None),
            P("section", None, "replica", "shard", None),
            P("section", "shard", None),
            P("section", "shard", None),
            P("section", "shard", None),
            P("section", "shard", None),
            P("section", "shard", None),
            P("section", "shard", None),
            P("section", "shard", None),
            P("section", "shard"),
            P("section", "shard"),
        ),
        check_vma=False,
    )
```
